32 devices in a mesh: dom: 8 (over z, y), sub: 4 (over x, core).
Axes of the slice: x: 2, y: 2, z: 4, core: 2. Of those that a mesh axis runs over, the one named last changes fastest.
Arguments:
- fields: float32 [6, 20, 32768], P(None, None, ('dom', 'sub')), may hold values from -6 to 6
- geometry: float32 [9, 32768], P(None, ('dom', 'sub')), may hold values from -4 to 4
- normals: float32 [3, 4, 32768], P(None, None, ('dom', 'sub')), may hold values from -3 to 3
- face_scale: float32 [4, 32768], P(None, ('dom', 'sub')), may hold values from 0.5 to 3
- derivatives: float32 [3, 20, 20], replicated, may hold values from -1.25 to 1.25
- lift_matrix: float32 [20, 40], replicated, may hold values from -1 to 1
- face_nbr: int32 [4, 32768], P(None, ('dom', 'sub')), may hold values from 0 to 4607, as said below
- send_rows: int32 [16384], P(('dom', 'sub')), may hold values from 64 to 1024, as said below
- fine_slots: int32 [4096], P(('dom', 'sub')), may hold values from 0 to 511, as said below
- export_rows: int32 [2, 512], P(None, ('dom', 'sub')), may hold values from 0 to 127, as said below
- fine_nbr: int32 [4, 4096], P(None, ('dom', 'sub')), may hold values from 0 to 640
Outputs:
- fields_out: float32 [6, 20, 32768], P(None, None, ('dom', 'sub'))
The draws below stay inside these ranges and needn't reach their ends.
Inputs may be any that keep to these rules, and one draw needn't show every extreme that they name: `face_nbr`: A wall face holds its own number 4 (e - p * 1024) + f. Codes from 4096 up occur only on the first 64 and the last 64 elements of a device: the first 64 use 4 * 1024 to 4351, the last 64 use 4 * 1024 + 4 * 64 and above. `send_rows`: entry p * 512 + j * 64 + c is the row within device p of the c-th element that p hands to the device of dom index j and p's sub index; 1024 marks an empty slot, and filled slots come first in each group of 64. Each group holds 0, 32 or 64 elements; in each sub index half of the dom indices hand 2 * 128 elements each, each of them 64 to some device, the others hand none. Handed rows are distinct and lie in 64 to 959. `fine_slots`: the 128 entries of a device are the filled slots j * 64 + c addressed to it (j the sender's dom index), each exactly once, in some order. `export_rows`: each row of a device holds 16 distinct positions among its 128 fine elements.
All inputs are finite; a program needn't handle non-finite values.
Results may differ from the reference program's by a relative error of at most 0.0001.
Values sent between devices are 32-bit elements; how exact they have to be, the bound alone decides.
A program may use at most 128 MiB of HBM per device.

```python
import math
import jax
import jax.numpy as jnp
import numpy as np
from jax import lax

NP = 20
NFP = 10
CE = 1024
FINE_DEV = 128
SUBSTEPS = 4
NB = 64
PB = 16
CAP = 64
SLOTS = 512
ELEMENTS = 32768
FINE_TOT = 4096
N_DOM = 8
N_SUB = 4
DEVICES = 32


def column_routing(column_key):
    subkeys = jax.random.split(column_key, 4)
    owner_order = jax.random.permutation(subkeys[0], N_DOM)
    receiver_order = jax.random.permutation(subkeys[1], N_DOM)
    half_dom = N_DOM // 2
    is_owner = owner_order < half_dom
    sign_one = jnp.where(owner_order < N_DOM // 4, 1, -1)
    sign_two = jnp.where((owner_order < N_DOM // 8) | (owner_order >= N_DOM // 4) & (owner_order < 3 * N_DOM // 8), 1, -1)
    recv_one = jnp.where(receiver_order < half_dom, 1, -1)
    recv_two = jnp.where((receiver_order < N_DOM // 4) | (receiver_order >= half_dom) & (receiver_order < 3 * N_DOM // 4), 1, -1)
    counts = CAP // 2 * (1 + (sign_one[:, None] * recv_one[None, :] + sign_two[:, None] * recv_two[None, :]) // 2)
    counts = jnp.where(is_owner[:, None], counts, 0)
    row_keys = jax.random.split(subkeys[2], N_DOM)

    def owner_pick(row_key):
        return jax.random.permutation(row_key, CE - 2 * NB)[:2 * FINE_DEV] + NB
    owner_rows = jax.vmap(owner_pick)(row_keys)
    starts = jnp.cumsum(counts, axis=1) - counts
    places = jnp.arange(CAP)
    filled = places[None, None, :] < counts[:, :, None]
    rank_index = jnp.minimum(starts[:, :, None] + places[None, None, :], 2 * FINE_DEV - 1)
    chosen_rows = owner_rows[jnp.arange(N_DOM)[:, None, None], rank_index]
    send_table = jnp.where(filled, chosen_rows, CE).reshape(N_DOM, SLOTS)
    slot_flags = filled.transpose(1, 0, 2).reshape(N_DOM, SLOTS)
    slot_keys = jax.random.split(subkeys[3], N_DOM)

    def receiver_slots(slot_key, flags_row):
        scores = jax.random.permutation(slot_key, SLOTS)
        return jnp.argsort(jnp.where(flags_row, scores, scores + SLOTS), stable=True)[:FINE_DEV]
    slot_table = jax.vmap(receiver_slots)(slot_keys, slot_flags)
    return (send_table, slot_table)


def fine_routing(key):
    sends, slot_table = jax.vmap(column_routing)(jax.random.split(key, N_SUB))
    sends = sends.transpose(1, 0, 2).reshape(DEVICES * SLOTS)
    slot_table = slot_table.transpose(1, 0, 2).reshape(DEVICES * FINE_DEV)
    return (sends.astype(jnp.int32), slot_table.astype(jnp.int32))


def draw_send_rows(key, part):
    shared = fine_routing(key)
    return shared[0]


def draw_fine_slots(key, part):
    shared = fine_routing(key)
    return shared[1]


def draw_face_nbr(key, part):
    key = jax.random.fold_in(key, 11)
    subkeys = jax.random.split(key, 4)
    grid_shape = (4, ELEMENTS)
    element = jnp.arange(ELEMENTS)[None, :] + jnp.zeros((4, 1), jnp.int32)
    facets = jnp.arange(4)[:, None] + jnp.zeros((1, ELEMENTS), jnp.int32)
    own_row = element % CE
    category = jax.random.randint(subkeys[0], grid_shape, 0, 10)
    any_row = jax.random.randint(subkeys[1], grid_shape, 0, CE)
    any_face = jax.random.randint(subkeys[2], grid_shape, 0, 4)
    rim_row = jax.random.randint(subkeys[3], grid_shape, 0, NB)
    inside = 4 * any_row + any_face
    lower_face = 4 * CE + 4 * rim_row + any_face
    upper_face = 4 * CE + 4 * NB + 4 * rim_row + any_face
    self_face = 4 * own_row + facets
    result = jnp.where(category == 0, self_face, jnp.where((category <= 3) & (own_row < NB), lower_face, jnp.where((category <= 3) & (own_row >= CE - NB), upper_face, inside)))
    return result.astype(jnp.int32)


def draw_export_rows(key, part):
    key = jax.random.fold_in(key, 5)

    def one_device(device_key):
        pair_keys = jax.random.split(device_key)
        return jnp.stack([jax.random.permutation(pair_keys[0], FINE_DEV)[:PB], jax.random.permutation(pair_keys[1], FINE_DEV)[:PB]])
    export_lists = jax.vmap(one_device)(jax.random.split(key, DEVICES))
    return export_lists.transpose(1, 0, 2).reshape(2, DEVICES * PB).astype(jnp.int32)


def draw_fine_nbr(key, part):
    key = jax.random.fold_in(key, 7)
    subkeys = jax.random.split(key, 3)
    grid_shape = (4, FINE_DEV * DEVICES)
    category = jax.random.randint(subkeys[0], grid_shape, 0, 10)
    nearby = jax.random.randint(subkeys[1], grid_shape, 0, 4 * FINE_DEV)
    remote = jax.random.randint(subkeys[2], grid_shape, 0, 4 * PB)
    result = jnp.where(category < 6, nearby, jnp.where(category == 6, 4 * FINE_DEV + remote, jnp.where(category == 7, 4 * FINE_DEV + 4 * PB + remote, 4 * FINE_DEV + 8 * PB)))
    return result.astype(jnp.int32)


def block_levels(own_key, dims, shards, smallest, largest):
    level, own = 1.0, jax.random.fold_in(own_key, 6)
    for dim, blocks in shards:
        heights = jnp.exp(jax.random.uniform(jax.random.fold_in(own, dim), (blocks,), jnp.float32, smallest / len(shards), largest / len(shards)))
        level = level * jnp.repeat(heights, dims[dim] // blocks).reshape([-1 if axis == dim else 1 for axis in range(len(dims))])
    return level


def normal_values(own_key, dims, deviation, bound, cuts=(), held_as=jnp.bfloat16):
    entries = deviation * jax.random.normal(own_key, dims, jnp.float32)
    if cuts:
        entries = entries * block_levels(own_key, dims, cuts, -0.22, 0.18)
    return jnp.clip(entries, -bound, bound).astype(held_as)


def setup_inputs(seed: int = 0) -> dict:
    streams_of = jax.random.split(jax.random.key(seed), 12)
    return {
        "fields": normal_values(streams_of[0], (6, NP, ELEMENTS), 1.0, 6.0, ((2, 32),), jnp.float32),
        "geometry": normal_values(streams_of[1], (9, ELEMENTS), 0.8, 4.0, ((1, 32),), jnp.float32),
        "normals": normal_values(streams_of[2], (3, 4, ELEMENTS), 0.6, 3.0, ((2, 32),), jnp.float32),
        "face_scale": jnp.clip(jnp.exp(math.log(3.0) - 1.7917595 * jax.random.uniform(streams_of[3], (4, ELEMENTS), jnp.float32) ** block_levels(streams_of[3], (4, ELEMENTS), ((1, 32),), -0.2, 0.2)), 0.5, 3.0),
        "derivatives": normal_values(streams_of[4], (3, NP, NP), NP ** -0.5, 1.25, (), jnp.float32),
        "lift_matrix": normal_values(streams_of[5], (NP, 4 * NFP), (4 * NFP) ** -0.5, 1.0, (), jnp.float32),
        "face_nbr": draw_face_nbr(jax.random.fold_in(streams_of[11], 71), 0),
        "send_rows": draw_send_rows(jax.random.fold_in(streams_of[11], 71), 0),
        "fine_slots": draw_fine_slots(jax.random.fold_in(streams_of[11], 71), 0),
        "export_rows": draw_export_rows(jax.random.fold_in(streams_of[11], 71), 0),
        "fine_nbr": draw_fine_nbr(jax.random.fold_in(streams_of[11], 71), 0),
    }


coarse_step = 0.2
highest = lax.Precision.HIGHEST


def face_table():
    places = [(along_r, along_s, along_t) for along_t in range(4) for along_s in range(4 - along_t) for along_r in range(4 - along_t - along_s)]
    bottom_face = [number for number, location in enumerate(places) if location[2] == 0]
    front_face = [number for number, location in enumerate(places) if location[1] == 0]
    slanted = [number for number, location in enumerate(places) if location[0] + location[1] + location[2] == 3]
    beside = [number for number, location in enumerate(places) if location[0] == 0]
    return np.array([bottom_face, front_face, slanted, beside], dtype=np.int32).T


def traces_of(vector_field, face_nodes):
    return vector_field[:, face_nodes, :]


def curl_of(vector_field, geometry, derivatives):
    local_grad = jnp.einsum('apq,cqe->acpe', derivatives, vector_field, precision=highest)
    factors = geometry.reshape(3, 3, geometry.shape[-1])

    def derivative(axis_out, component):
        return factors[axis_out, 0] * local_grad[0, component] + factors[axis_out, 1] * local_grad[1, component] + factors[axis_out, 2] * local_grad[2, component]

    return jnp.stack([derivative(1, 2) - derivative(2, 1), derivative(2, 0) - derivative(0, 2), derivative(0, 1) - derivative(1, 0)])


def cross_product(normals, jump_values):
    return jnp.stack([normals[1] * jump_values[2] - normals[2] * jump_values[1], normals[2] * jump_values[0] - normals[0] * jump_values[2], normals[0] * jump_values[1] - normals[1] * jump_values[0]])


def lift_of(lift_matrix, face_scale, flux_values):
    scaled = flux_values * face_scale
    shaped = lift_matrix.reshape(lift_matrix.shape[0], 4, lift_matrix.shape[1] // 4)
    return 0.5 * jnp.einsum('pfn,cnfe->cpe', shaped, scaled, precision=highest)


def magnetic_rate(curl_e, efield, outside, normals, face_scale, lift_matrix, face_nodes):
    jump_values = outside - traces_of(efield, face_nodes)
    return -curl_e - lift_of(lift_matrix, face_scale, cross_product(normals, jump_values))


def electric_rate(curl_h, hfield, outside, normals, face_scale, lift_matrix, face_nodes):
    jump_values = outside - traces_of(hfield, face_nodes)
    return curl_h + lift_of(lift_matrix, face_scale, cross_product(normals, jump_values))


def global_faces(face_nbr):
    element = jnp.arange(ELEMENTS, dtype=jnp.int32)[None, :]
    device = element // CE
    quarter = face_nbr // 4
    target = jnp.where(face_nbr < 4 * CE, device * CE + quarter,
                       jnp.where(face_nbr < 4 * CE + 4 * NB, ((device - 1) % DEVICES) * CE + CE - NB + quarter - CE,
                                 ((device + 1) % DEVICES) * CE + quarter - CE - NB))
    wall = face_nbr == 4 * (element % CE) + jnp.arange(4, dtype=jnp.int32)[:, None]
    return (face_nbr % 4) * ELEMENTS + target, wall


def exterior_global(vector_field, flat_index, wall, mirror_sign, face_nodes):
    interior = traces_of(vector_field, face_nodes)
    flat_traces = interior.reshape(vector_field.shape[0], interior.shape[1], 4 * vector_field.shape[2])
    return jnp.where(wall, mirror_sign * interior, flat_traces[:, :, flat_index])


def reference(fields, geometry, normals, face_scale, derivatives, lift_matrix, face_nbr, send_rows, fine_slots, export_rows, fine_nbr):
    face_nodes = face_table()
    flat_index, wall = global_faces(face_nbr)
    fine_index = jnp.arange(FINE_TOT, dtype=jnp.int32)
    receiver = fine_index // FINE_DEV
    source = (fine_slots // CAP) * N_SUB + receiver % N_SUB
    source_row = send_rows[source * SLOTS + (receiver // N_SUB) * CAP + fine_slots % CAP]
    fine_elements = source * CE + source_row
    held_e = exterior_global(fields[:3], flat_index, wall, -1.0, face_nodes)[..., fine_elements]
    held_h = exterior_global(fields[3:], flat_index, wall, 1.0, face_nodes)[..., fine_elements]

    local_end = 4 * FINE_DEV
    remote_span = 4 * PB
    below_dev = ((receiver - 1) % DEVICES)[None, :]
    above_dev = ((receiver + 1) % DEVICES)[None, :]
    first_part = jnp.clip(fine_nbr - local_end, 0, remote_span - 1)
    second_part = jnp.clip(fine_nbr - local_end - remote_span, 0, remote_span - 1)
    below_row = export_rows[1][below_dev * PB + first_part // 4]
    above_row = export_rows[0][above_dev * PB + second_part // 4]
    nearby_face = fine_nbr < local_end
    lower_side = fine_nbr < local_end + remote_span
    target = jnp.where(nearby_face, receiver[None, :] * FINE_DEV + fine_nbr // 4,
                       jnp.where(lower_side, below_dev * FINE_DEV + below_row, above_dev * FINE_DEV + above_row))
    target_face = jnp.where(nearby_face, fine_nbr % 4, jnp.where(lower_side, first_part % 4, second_part % 4))
    fine_flat_index = target_face * FINE_TOT + target
    frozen = fine_nbr == local_end + 2 * remote_span

    def fine_outside(vector_field, held_part):
        flat_traces = traces_of(vector_field, face_nodes).reshape(3, NFP, 4 * FINE_TOT)
        return jnp.where(frozen, held_part, flat_traces[:, :, fine_flat_index])

    geometry_fine = geometry[:, fine_elements]
    normals_fine = normals[:, :, fine_elements]
    scale_fine = face_scale[:, fine_elements]
    efield = fields[:3][:, :, fine_elements]
    hfield = fields[3:][:, :, fine_elements]
    fine_step = coarse_step / SUBSTEPS
    for substep in range(SUBSTEPS):
        outside = fine_outside(efield, held_e)
        hfield = hfield + fine_step * magnetic_rate(curl_of(efield, geometry_fine, derivatives), efield, outside, normals_fine, scale_fine, lift_matrix, face_nodes)
        outside = fine_outside(hfield, held_h)
        efield = efield + fine_step * electric_rate(curl_of(hfield, geometry_fine, derivatives), hfield, outside, normals_fine, scale_fine, lift_matrix, face_nodes)
    merged = fields.at[:, :, fine_elements].set(jnp.concatenate([efield, hfield]))

    efield = merged[:3]
    hfield = merged[3:]
    outside = exterior_global(efield, flat_index, wall, -1.0, face_nodes)
    hfield = hfield + coarse_step * magnetic_rate(curl_of(efield, geometry, derivatives), efield, outside, normals, face_scale, lift_matrix, face_nodes)
    outside = exterior_global(hfield, flat_index, wall, 1.0, face_nodes)
    efield = efield + coarse_step * electric_rate(curl_of(hfield, geometry, derivatives), hfield, outside, normals, face_scale, lift_matrix, face_nodes)
    return jnp.concatenate([efield, hfield])
```

```python
import functools

import jax
import jax.numpy as jnp
import numpy as np
from jax import lax
from jax.experimental import pallas as pl
from jax.experimental.pallas import tpu as pltpu
from jax.sharding import PartitionSpec as P

SUBSTEPS = 4
coarse_step = 0.2

PADC = 24
FR = 80
FN = 16
TR = 192
PK = 384
RK = 128
GEO, NS, CODE = 0, 9, 24
CHUNK = 256

bf16 = jnp.bfloat16
f32 = jnp.float32
MESH = pl.DeviceIdType.MESH


def face_table():
    places = [
        (along_r, along_s, along_t)
        for along_t in range(4)
        for along_s in range(4 - along_t)
        for along_r in range(4 - along_t - along_s)
    ]
    bottom_face = [number for number, location in enumerate(places) if location[2] == 0]
    front_face = [number for number, location in enumerate(places) if location[1] == 0]
    slanted = [number for number, location in enumerate(places) if sum(location) == 3]
    beside = [number for number, location in enumerate(places) if location[0] == 0]
    return np.array([bottom_face, front_face, slanted, beside], dtype=np.int32).T


def tables():
    nodes = face_table()
    sel = np.zeros((TR, 2 * FR), np.float32)
    pack = np.zeros((368, 4 * FR + 4 * TR), np.float32)
    unpack = np.zeros((2 * FR + 2 * TR, 2 * PK), np.float32)
    ret = np.zeros((RK, 4 * FR), np.float32)
    back = np.zeros((2 * FR, 2 * RK), np.float32)
    for c in range(3):
        for p in range(20):
            for field in range(2):
                packed = (field * 3 + c) * 20 + p
                for s in range(2):
                    at = field * 2 * FR + s * FR + c * PADC + p
                    pack[packed, at] = 1
                    ret[packed, at] = 1
                    unpack[field * FR + c * PADC + p, s * PK + packed] = 1
                    back[field * FR + c * PADC + p, s * RK + packed] = 1
        for f in range(4):
            for n in range(10):
                row = f * 3 * FN + c * FN + n
                for s in range(2):
                    sel[row, s * FR + c * PADC + nodes[n, f]] = 1
                for field in range(2):
                    packed = 120 + field * 120 + (f * 3 + c) * 10 + n
                    for s in range(2):
                        pack[packed, 4 * FR + field * 2 * TR + s * TR + row] = 1
                        unpack[2 * FR + field * TR + row, s * PK + packed] = 1
    d_rows = np.zeros((3, 224, 20), np.float32)
    d_hi = np.zeros((20, 3 * FR), np.float32)
    d_lo = np.zeros((20, 3 * FR), np.float32)
    d_mask = np.zeros((224, 3 * FR), np.float32)
    l_rows = np.zeros((FR, 20), np.float32)
    l_hi = np.zeros((40, 3 * TR), np.float32)
    l_lo = np.zeros((40, 3 * TR), np.float32)
    l_mask = np.zeros((FR, 3 * TR), np.float32)
    for c in range(3):
        for p in range(20):
            l_rows[c * PADC + p, p] = 1
            for a in range(3):
                d_rows[a, (a * 3 + c) * PADC + p, p] = 1
            d_hi[p, c * PADC + p] = 1
            d_hi[p, FR + c * PADC + p] = 1
            d_lo[p, 2 * FR + c * PADC + p] = 1
        for s in range(3):
            for a in range(3):
                at = (a * 3 + c) * PADC
                d_mask[at : at + 20, s * FR + c * PADC : s * FR + c * PADC + 20] = 1
            for f in range(4):
                col = s * TR + f * 3 * FN + c * FN
                l_mask[c * PADC : c * PADC + 20, col : col + 10] = 0.5
                for n in range(10):
                    (l_lo if s == 2 else l_hi)[f * 10 + n, col + n] = 1
    out = [sel, pack, unpack, ret, back, d_rows, d_hi, d_lo, l_rows, l_hi, l_lo]
    return [x.astype(jnp.bfloat16) for x in out] + [d_mask, l_mask]


def split(x):
    hi = x.astype(bf16).astype(f32)
    return hi, x - hi


def split2(x):
    hi, lo = split(x)
    return jnp.concatenate([hi, lo], axis=0).astype(bf16)


def split3(x):
    hi, lo = split(x)
    return jnp.concatenate([hi, lo, hi], axis=0).astype(bf16)


def dot(a, b):
    return jnp.dot(a, b, preferred_element_type=f32)


def dot_t(a, b):
    return lax.dot_general(a, b, (((1,), (1,)), ((), ())), preferred_element_type=f32)


def one_hot(count, row):
    at = lax.broadcasted_iota(jnp.int32, (count, row.shape[1]), 0)
    return jnp.where(at == row, 1.0, 0.0).astype(bf16)


def curl(grad, geo):
    def partial(m, c):
        total = None
        for a in range(3):
            at = (a * 3 + c) * PADC
            term = geo[3 * m + a : 3 * m + a + 1] * grad[at : at + PADC]
            total = term if total is None else total + term
        return total

    parts = [
        partial(1, 2) - partial(2, 1),
        partial(2, 0) - partial(0, 2),
        partial(0, 1) - partial(1, 0),
    ]
    pad = jnp.zeros((FR - 3 * PADC, grad.shape[1]), f32)
    return jnp.concatenate([*parts, pad], axis=0)


def pick_face(traces, face):
    total = traces[: 3 * FN]
    for g in range(1, 4):
        total = jnp.where(face == g, traces[g * 3 * FN : (g + 1) * 3 * FN], total)
    return total


def flux(jump, ns, f):
    n = [ns[c * 4 + f : c * 4 + f + 1] for c in range(3)]
    j = [jump[c * FN : (c + 1) * FN] for c in range(3)]
    return [
        n[1] * j[2] - n[2] * j[1],
        n[2] * j[0] - n[0] * j[2],
        n[0] * j[1] - n[1] * j[0],
    ]


def kernel(
    n_dom,
    n_sub,
    width,
    fields,
    geometry,
    normals,
    face_scale,
    derivatives,
    lift_matrix,
    face_nbr,
    send_rows,
    fine_slots,
    export_row,
    fine_nbr,
    sel,
    pack,
    unpack,
    ret,
    back,
    d_rows,
    d_hi,
    d_lo,
    l_rows,
    l_hi,
    l_lo,
    d_mask,
    l_mask,
    out,
    own_e,
    own_h,
    pool_e,
    pool_h,
    stat,
    send_hot,
    fine_own,
    fine_halo,
    dmat,
    lmat,
    hand_out,
    hand_in,
    back_out,
    back_in,
    fine_out,
    fine_in,
    halo_out,
    halo_in,
    hand_send,
    hand_recv,
    back_send,
    back_recv,
    fine_send,
    fine_recv,
    halo_send,
    halo_recv,
):
    count = fields.shape[2]
    fine = fine_slots.shape[1]
    cap = hand_out.shape[1]
    slots = n_dom * cap
    dom, sub = lax.axis_index("dom"), lax.axis_index("sub")
    me = dom * n_sub + sub
    total = n_dom * n_sub
    after, before = lax.rem(me + 1, total), lax.rem(me + total - 1, total)
    after_id = (after // n_sub, lax.rem(after, n_sub))
    before_id = (before // n_sub, lax.rem(before, n_sub))

    barrier = pltpu.get_barrier_semaphore()
    for target in (after_id, before_id):
        pl.semaphore_signal(barrier, inc=1, device_id=target, device_id_type=MESH)

    @pl.loop(1, n_dom)
    def _(i):
        pl.semaphore_signal(
            barrier, inc=1, device_id=(lax.rem(dom + i, n_dom), sub), device_id_type=MESH
        )

    for ref, first in ((own_e, 0), (own_h, 3)):
        ref[...] = jnp.zeros(ref.shape, f32)
        for c in range(3):
            ref[c * PADC : c * PADC + 20, :] = fields[first + c]
    pool_e[:, :count] = split2(own_e[...])
    pool_h[:, :count] = split2(own_h[...])
    stat[...] = jnp.zeros(stat.shape, f32)
    stat[GEO : GEO + 9, :] = geometry[...]
    for c in range(3):
        stat[NS + 4 * c : NS + 4 * c + 4, :] = normals[c] * face_scale[...]
    stat[CODE : CODE + 4, :] = face_nbr[...].astype(f32)

    halo_out[0, 0] = own_e[:, count - 128 :]
    halo_out[0, 1] = own_e[:, :128]

    rows = send_rows[...]
    hot = one_hot(count, rows)
    send_hot[...] = hot
    picked_e = dot(pool_e[:, :count], hot).astype(bf16)
    picked_h = dot(pool_h[:, :count], hot).astype(bf16)
    picked_stat = dot(split2(stat[...]), hot)
    picked_stat = picked_stat[:32] + picked_stat[32:]
    traces_e = dot(sel[...], picked_e)
    traces_h = dot(sel[...], picked_h)
    held_e, held_h = [], []
    for f in range(4):
        code = picked_stat[CODE + f : CODE + f + 1].astype(jnp.int32)
        near = one_hot(count, code >> 2)
        face = code & 3
        wall = code == 4 * rows + f
        e = pick_face(dot(sel[...], dot(pool_e[:, :count], near).astype(bf16)), face)
        h = pick_face(dot(sel[...], dot(pool_h[:, :count], near).astype(bf16)), face)
        at = f * 3 * FN
        held_e.append(jnp.where(wall, -traces_e[at : at + 3 * FN], e))
        held_h.append(jnp.where(wall, traces_h[at : at + 3 * FN], h))
    everything = jnp.concatenate(
        [
            picked_e,
            picked_h,
            split2(jnp.concatenate(held_e, axis=0)),
            split2(jnp.concatenate(held_h, axis=0)),
        ],
        axis=0,
    )
    packed = jnp.concatenate([dot(pack[...], everything)[:360], picked_stat[:24]], axis=0)
    hand_out[...] = packed.T.reshape(n_dom, cap, PK)

    pl.semaphore_wait(barrier, n_dom + 1)

    def exchange(src, dst, send, recv):
        def copy(i):
            target = lax.rem(dom + i, n_dom)
            return pltpu.make_async_remote_copy(
                src_ref=src.at[target],
                dst_ref=dst.at[dom],
                send_sem=send.at[i],
                recv_sem=recv.at[i],
                device_id=(target, sub),
                device_id_type=MESH,
            )

        @pl.loop(1, n_dom)
        def _(i):
            copy(i).start()

        dst[pl.ds(dom, 1)] = src[pl.ds(dom, 1)]
        return copy

    def finish(copy):
        @pl.loop(1, n_dom)
        def _(i):
            copy(i).wait()

    def to_neighbours(src_up, src_down, dst, send, recv):
        copies = []
        for side, (src, target) in enumerate(((src_up, after_id), (src_down, before_id))):
            copy = pltpu.make_async_remote_copy(
                src_ref=src,
                dst_ref=dst.at[side],
                send_sem=send.at[side],
                recv_sem=recv.at[side],
                device_id=target,
                device_id_type=MESH,
            )
            copy.start()
            copies.append(copy)
        return copies

    handed = exchange(hand_out, hand_in, hand_send, hand_recv)
    halo_e = to_neighbours(
        halo_out.at[0, 0], halo_out.at[0, 1], halo_in.at[0], halo_send.at[0], halo_recv.at[0]
    )

    rows_hi = rows_lo = None
    for a in range(3):
        hi, lo = split(derivatives[a])
        hi = dot(d_rows[a], hi.astype(bf16))
        lo = dot(d_rows[a], lo.astype(bf16))
        rows_hi = hi if a == 0 else rows_hi + hi
        rows_lo = lo if a == 0 else rows_lo + lo
    wide = dot(rows_hi.astype(bf16), d_hi[...]) + dot(rows_lo.astype(bf16), d_lo[...])
    dmat[...] = (wide * d_mask[...]).astype(bf16)
    hi, lo = split(lift_matrix[...])
    hi = dot(l_rows[...], hi.astype(bf16))
    lo = dot(l_rows[...], lo.astype(bf16))
    wide = dot(hi.astype(bf16), l_hi[...]) + dot(lo.astype(bf16), l_lo[...])
    lmat[...] = (wide * l_mask[...]).astype(bf16)

    codes = [fine_nbr[f : f + 1, :] for f in range(4)]
    code_row = jnp.concatenate(codes, axis=1) >> 2
    fine_own[...] = one_hot(fine, code_row)
    fine_halo[...] = one_hot(128, code_row - fine)
    export_hot = one_hot(fine, export_row[...])
    slot_hot = one_hot(slots, fine_slots[...])

    finish(handed)
    received = hand_in[...].reshape(slots, PK).T
    received = dot(split2(received), slot_hot)
    fine_stat = received[360:384] + received[PK + 360 : PK + 384]
    state = dot(unpack[...], received.astype(bf16))
    efield, hfield = state[:FR], state[FR : 2 * FR]
    fine_held = (state[2 * FR : 2 * FR + TR], state[2 * FR + TR :])
    fine_geo, fine_ns = fine_stat[GEO : GEO + 9], fine_stat[NS : NS + 12]
    lane = lax.broadcasted_iota(jnp.int32, (FR, 128), 1)
    frozen_code = 4 * fine + 8 * width

    def fine_rate(field, held, turn):
        parts = split2(field)
        export = dot(parts, export_hot)
        fine_out[turn] = export[:FR] + export[FR:]
        copies = to_neighbours(
            fine_out.at[turn], fine_out.at[turn], fine_in.at[turn], fine_send.at[turn], fine_recv.at[turn]
        )
        near = dot(parts, fine_own[...])
        own = dot(sel[...], parts)
        spin = curl(dot(dmat[...], split3(field)), fine_geo)
        for copy in copies:
            copy.wait()
        halo = jnp.where(lane < width, fine_in[turn, 0], fine_in[turn, 1])
        near = near + dot(split2(halo), fine_halo[...])
        traces = dot(sel[...], near.astype(bf16))
        fluxes = []
        for f in range(4):
            at = f * 3 * FN
            outside = pick_face(traces[:, f * fine : (f + 1) * fine], codes[f] & 3)
            outside = jnp.where(codes[f] == frozen_code, held[at : at + 3 * FN], outside)
            fluxes += flux(outside - own[at : at + 3 * FN], fine_ns, f)
        return spin + dot(lmat[...], split3(jnp.concatenate(fluxes, axis=0)))

    fine_step = coarse_step / SUBSTEPS
    for substep in range(SUBSTEPS):
        hfield = hfield - fine_step * fine_rate(efield, fine_held[0], 2 * substep)
        efield = efield + fine_step * fine_rate(hfield, fine_held[1], 2 * substep + 1)

    result = jnp.concatenate([split2(efield), split2(hfield)], axis=0)
    result = split2(dot(ret[...], result))
    result = dot_t(slot_hot, result)
    result = result[:, :RK] + result[:, RK:]
    back_out[...] = result.reshape(n_dom, cap, RK)
    returned = exchange(back_out, back_in, back_send, back_recv)
    is_fine = dot_t(jnp.ones((16, slots), bf16), send_hot[...])[:1] > 0.5
    finish(returned)
    came = back_in[...].reshape(slots, RK).T
    came = dot_t(split2(came), send_hot[...]).astype(bf16)
    came = dot(back[...], came)
    merged_e = jnp.where(is_fine, came[:FR], own_e[...])
    merged_h = jnp.where(is_fine, came[FR:], own_h[...])
    own_e[...] = merged_e
    own_h[...] = merged_h
    pool_e[:, :count] = split2(merged_e)

    halo_lane = lax.broadcasted_iota(jnp.int32, (FR, 128), 1)
    place = lax.broadcasted_iota(jnp.int32, (1, CHUNK), 1)

    def coarse_rate(start, source, pool, reach, mirror):
        window = pl.ds(start, CHUNK)
        field = source[:, window]
        table = stat[:, window]
        spin = curl(dot(dmat[...], split3(field)), table[GEO : GEO + 9])
        own = dot(sel[...], split2(field))
        ns = table[NS : NS + 12]
        fluxes = []
        for f in range(4):
            code = face_nbr[f : f + 1, window]
            near = dot(pool[:, :reach], one_hot(reach, code >> 2)).astype(bf16)
            outside = pick_face(dot(sel[...], near), code & 3)
            mine = own[f * 3 * FN : (f + 1) * 3 * FN]
            wall = code == 4 * (start + place) + f
            outside = jnp.where(wall, mirror * mine, outside)
            fluxes += flux(outside - mine, ns, f)
        return spin + dot(lmat[...], split3(jnp.concatenate(fluxes, axis=0)))

    def set_halo(pool, turn, copies):
        for copy in copies:
            copy.wait()
        tile = jnp.where(halo_lane < 64, halo_in[turn, 1], halo_in[turn, 0])
        pool[:, count:] = split2(pltpu.roll(tile, 64, 1))

    def update(start, source, pool, target, first, scale, reach, mirror):
        start = pl.multiple_of(start, CHUNK)
        window = pl.ds(start, CHUNK)
        new = target[:, window] + scale * coarse_rate(start, source, pool, reach, mirror)
        target[:, window] = new
        for c in range(3):
            out[first + c, :, window] = new[c * PADC : c * PADC + 20]
        if first == 3:
            pool_h[:, window] = split2(new)

    last = count - CHUNK
    full = count + 128
    set_halo(pool_e, 0, halo_e)

    @pl.loop(0, 2)
    def _(i):
        update(i * last, own_e, pool_e, own_h, 3, -coarse_step, full, -1.0)

    halo_out[1, 0] = own_h[:, count - 128 :]
    halo_out[1, 1] = own_h[:, :128]
    halo_h = to_neighbours(
        halo_out.at[1, 0], halo_out.at[1, 1], halo_in.at[1], halo_send.at[1], halo_recv.at[1]
    )

    @pl.loop(1, count // CHUNK - 1)
    def _(i):
        update(i * CHUNK, own_e, pool_e, own_h, 3, -coarse_step, count, -1.0)

    @pl.loop(1, count // CHUNK - 1)
    def _(i):
        update(i * CHUNK, own_h, pool_h, own_e, 0, coarse_step, count, 1.0)

    set_halo(pool_h, 1, halo_h)

    @pl.loop(0, 2)
    def _(i):
        update(i * last, own_h, pool_h, own_e, 0, coarse_step, full, 1.0)


def per_device(
    n_dom,
    n_sub,
    fields,
    geometry,
    normals,
    face_scale,
    derivatives,
    lift_matrix,
    face_nbr,
    send_rows,
    fine_slots,
    export_rows,
    fine_nbr,
):
    count = fields.shape[2]
    fine = fine_slots.shape[0]
    width = export_rows.shape[1]
    group = send_rows.shape[0] // n_dom
    cap = -(-group // 8) * 8
    slots = n_dom * cap
    turns = 2 * SUBSTEPS
    if cap != group:
        send_rows = jnp.pad(
            send_rows.reshape(n_dom, group),
            ((0, 0), (0, cap - group)),
            constant_values=count,
        ).reshape(-1)
        fine_slots = fine_slots // group * cap + fine_slots % group
    export_row = jnp.concatenate(
        [export_rows[1], export_rows[0], jnp.full((128 - 2 * width,), -1, jnp.int32)]
    )
    operands = [
        fields,
        geometry,
        normals,
        face_scale,
        derivatives,
        lift_matrix,
        face_nbr,
        send_rows[None],
        fine_slots[None],
        export_row[None],
        fine_nbr,
        *[jnp.asarray(x) for x in tables()],
    ]
    vmem = pl.BlockSpec(memory_space=pltpu.VMEM)
    dma = pltpu.SemaphoreType.DMA
    return pl.pallas_call(
        functools.partial(kernel, n_dom, n_sub, width),
        out_shape=jax.ShapeDtypeStruct(fields.shape, f32),
        in_specs=[vmem] * len(operands),
        out_specs=vmem,
        scratch_shapes=[
            pltpu.VMEM((FR, count), f32),
            pltpu.VMEM((FR, count), f32),
            pltpu.VMEM((2 * FR, count + 128), bf16),
            pltpu.VMEM((2 * FR, count + 128), bf16),
            pltpu.VMEM((32, count), f32),
            pltpu.VMEM((count, slots), bf16),
            pltpu.VMEM((fine, 4 * fine), bf16),
            pltpu.VMEM((128, 4 * fine), bf16),
            pltpu.VMEM((224, 3 * FR), bf16),
            pltpu.VMEM((FR, 3 * TR), bf16),
            pltpu.VMEM((n_dom, cap, PK), f32),
            pltpu.VMEM((n_dom, cap, PK), f32),
            pltpu.VMEM((n_dom, cap, RK), f32),
            pltpu.VMEM((n_dom, cap, RK), f32),
            pltpu.VMEM((turns, FR, 128), f32),
            pltpu.VMEM((turns, 2, FR, 128), f32),
            pltpu.VMEM((2, 2, FR, 128), f32),
            pltpu.VMEM((2, 2, FR, 128), f32),
            dma((n_dom,)),
            dma((n_dom,)),
            dma((n_dom,)),
            dma((n_dom,)),
            dma((turns, 2)),
            dma((turns, 2)),
            dma((2, 2)),
            dma((2, 2)),
        ],
        compiler_params=pltpu.CompilerParams(
            collective_id=0, has_side_effects=True, vmem_limit_bytes=56 * 1024 * 1024
        ),
    )(*operands)


def solution(mesh):
    return jax.shard_map(
        functools.partial(per_device, mesh.shape["dom"], mesh.shape["sub"]),
        mesh=mesh,
        in_specs=(
            P(None, None, ("dom", "sub")),
            P(None, ("dom", "sub")),
            P(None, None, ("dom", "sub")),
            P(None, ("dom", "sub")),
            P(),
            P(),
            P(None, ("dom", "sub")),
            P(("dom", "sub")),
            P(("dom", "sub")),
            P(None, ("dom", "sub")),
            P(None, ("dom", "sub")),
        ),
        out_specs=P(None, None, ("dom", "sub")),
        check_vma=False,
    )
```

```python
import functools

import jax
import jax.numpy as jnp
import numpy as np
from jax import lax
from jax.experimental import pallas as pl
from jax.experimental.pallas import tpu as pltpu
from jax.sharding import PartitionSpec as P

SUBSTEPS = 4
coarse_step = 0.2

PADC = 24
FR = 80
FN = 16
TR = 192
RK = 128
GEO, NS, CODE = 0, 9, 24
CHUNK = 256

bf16 = jnp.bfloat16
f32 = jnp.float32
MESH = pl.DeviceIdType.MESH


def face_table():
    places = [
        (along_r, along_s, along_t)
        for along_t in range(4)
        for along_s in range(4 - along_t)
        for along_r in range(4 - along_t - along_s)
    ]
    bottom_face = [number for number, location in enumerate(places) if location[2] == 0]
    front_face = [number for number, location in enumerate(places) if location[1] == 0]
    slanted = [number for number, location in enumerate(places) if sum(location) == 3]
    beside = [number for number, location in enumerate(places) if location[0] == 0]
    return np.array([bottom_face, front_face, slanted, beside], dtype=np.int32).T


def tables():
    nodes = face_table()
    sel = np.zeros((TR, 2 * FR), np.float32)
    pack = np.zeros((RK, 4 * FR), np.float32)
    unpack = np.zeros((2 * FR, 2 * RK), np.float32)
    for c in range(3):
        for p in range(20):
            for field in range(2):
                packed = (field * 3 + c) * 20 + p
                for s in range(2):
                    pack[packed, field * 2 * FR + s * FR + c * PADC + p] = 1
                    unpack[field * FR + c * PADC + p, s * RK + packed] = 1
        for f in range(4):
            for n in range(10):
                for s in range(2):
                    sel[f * 3 * FN + c * FN + n, s * FR + c * PADC + nodes[n, f]] = 1
    d_rows = np.zeros((3, 224, 20), np.float32)
    d_hi = np.zeros((20, 3 * FR), np.float32)
    d_lo = np.zeros((20, 3 * FR), np.float32)
    d_mask = np.zeros((224, 3 * FR), np.float32)
    l_rows = np.zeros((FR, 20), np.float32)
    l_hi = np.zeros((40, 3 * TR), np.float32)
    l_lo = np.zeros((40, 3 * TR), np.float32)
    l_mask = np.zeros((FR, 3 * TR), np.float32)
    for c in range(3):
        for p in range(20):
            l_rows[c * PADC + p, p] = 1
            for a in range(3):
                d_rows[a, (a * 3 + c) * PADC + p, p] = 1
            d_hi[p, c * PADC + p] = 1
            d_hi[p, FR + c * PADC + p] = 1
            d_lo[p, 2 * FR + c * PADC + p] = 1
        for s in range(3):
            for a in range(3):
                at = (a * 3 + c) * PADC
                d_mask[at : at + 20, s * FR + c * PADC : s * FR + c * PADC + 20] = 1
            for f in range(4):
                col = s * TR + f * 3 * FN + c * FN
                l_mask[c * PADC : c * PADC + 20, col : col + 10] = 0.5
                for n in range(10):
                    (l_lo if s == 2 else l_hi)[f * 10 + n, col + n] = 1
    out = [sel, pack, unpack, d_rows, d_hi, d_lo, l_rows, l_hi, l_lo]
    return [x.astype(jnp.bfloat16) for x in out] + [d_mask, l_mask]


def split(x):
    hi = x.astype(bf16).astype(f32)
    return hi, x - hi


def split2(x):
    hi, lo = split(x)
    return jnp.concatenate([hi, lo], axis=0).astype(bf16)


def split3(x):
    hi, lo = split(x)
    return jnp.concatenate([hi, lo, hi], axis=0).astype(bf16)


def dot(a, b):
    return jnp.dot(a, b, preferred_element_type=f32)


def dot_t(a, b):
    return lax.dot_general(a, b, (((1,), (1,)), ((), ())), preferred_element_type=f32)


def one_hot(count, row):
    at = lax.broadcasted_iota(jnp.int32, (count, row.shape[1]), 0)
    return jnp.where(at == row, 1.0, 0.0).astype(bf16)


def curl(grad, geo):
    def partial(m, c):
        total = None
        for a in range(3):
            at = (a * 3 + c) * PADC
            term = geo[3 * m + a : 3 * m + a + 1] * grad[at : at + PADC]
            total = term if total is None else total + term
        return total

    parts = [
        partial(1, 2) - partial(2, 1),
        partial(2, 0) - partial(0, 2),
        partial(0, 1) - partial(1, 0),
    ]
    pad = jnp.zeros((FR - 3 * PADC, grad.shape[1]), f32)
    return jnp.concatenate([*parts, pad], axis=0)


def pick_face(traces, face):
    total = traces[: 3 * FN]
    for g in range(1, 4):
        total = jnp.where(face == g, traces[g * 3 * FN : (g + 1) * 3 * FN], total)
    return total


def flux(jump, ns, f):
    n = [ns[c * 4 + f : c * 4 + f + 1] for c in range(3)]
    j = [jump[c * FN : (c + 1) * FN] for c in range(3)]
    return [
        n[1] * j[2] - n[2] * j[1],
        n[2] * j[0] - n[0] * j[2],
        n[0] * j[1] - n[1] * j[0],
    ]


def kernel(
    n_dom,
    n_sub,
    width,
    fields,
    geometry,
    normals,
    face_scale,
    derivatives,
    lift_matrix,
    face_nbr,
    send_rows,
    fine_slots,
    export_rows,
    fine_nbr,
    sel,
    pack,
    unpack,
    d_rows,
    d_hi,
    d_lo,
    l_rows,
    l_hi,
    l_lo,
    d_mask,
    l_mask,
    out,
    own_e,
    own_h,
    pool,
    stat,
    frozen,
    send_hot,
    coarse_hot,
    fine_own,
    fine_halo,
    dmat,
    lmat,
    mask_out,
    mask_in,
    extra_out,
    extra_in,
    hand_out,
    hand_in,
    back_out,
    back_in,
    fine_out,
    fine_in,
    halo_out,
    halo_in,
    mask_send,
    mask_recv,
    extra_send,
    extra_recv,
    hand_send,
    hand_recv,
    back_send,
    back_recv,
    fine_send,
    fine_recv,
    halo_send,
    halo_recv,
):
    count = fields.shape[2]
    fine = fine_slots.shape[1]
    cap = hand_out.shape[2]
    slots = n_dom * cap
    full = count + 128
    dom, sub = lax.axis_index("dom"), lax.axis_index("sub")
    me = dom * n_sub + sub
    total = n_dom * n_sub
    after, before = lax.rem(me + 1, total), lax.rem(me + total - 1, total)
    after_id = (after // n_sub, lax.rem(after, n_sub))
    before_id = (before // n_sub, lax.rem(before, n_sub))

    barrier = pltpu.get_barrier_semaphore()
    for target in (after_id, before_id):
        pl.semaphore_signal(barrier, inc=1, device_id=target, device_id_type=MESH)

    @pl.loop(1, n_dom)
    def _(i):
        pl.semaphore_signal(
            barrier, inc=1, device_id=(lax.rem(dom + i, n_dom), sub), device_id_type=MESH
        )

    def exchange(src, dst, send, recv):
        def copy(i):
            target = lax.rem(dom + i, n_dom)
            return pltpu.make_async_remote_copy(
                src_ref=src.at[target],
                dst_ref=dst.at[dom],
                send_sem=send.at[i],
                recv_sem=recv.at[i],
                device_id=(target, sub),
                device_id_type=MESH,
            )

        @pl.loop(1, n_dom)
        def _(i):
            copy(i).start()

        dst[pl.ds(dom, 1)] = src[pl.ds(dom, 1)]
        return copy

    def finish(copy):
        @pl.loop(1, n_dom)
        def _(i):
            copy(i).wait()

    def to_neighbours(src, dst, send, recv):
        copies = []
        for side, target in enumerate((after_id, before_id)):
            copy = pltpu.make_async_remote_copy(
                src_ref=src.at[side],
                dst_ref=dst.at[side],
                send_sem=send.at[side],
                recv_sem=recv.at[side],
                device_id=target,
                device_id_type=MESH,
            )
            copy.start()
            copies.append(copy)
        return copies

    def slots_of(d, row):
        at = lax.broadcasted_iota(jnp.int32, (128, row.shape[1]), 0)
        return jnp.where((row - d * cap == at) & (at < cap), 1.0, 0.0).astype(bf16)

    codes = [fine_nbr[f : f + 1, :] for f in range(4)]
    frozen_code = 4 * fine + 8 * width
    frozen[...] = jnp.zeros(frozen.shape, f32)
    frozen[0:4, :] = jnp.where(fine_nbr[...] == frozen_code, 1.0, 0.0)
    my_slots = fine_slots[...]

    @pl.loop(0, n_dom)
    def _(d):
        mask_out[d] = dot_t(frozen[...].astype(bf16), slots_of(d, my_slots))[:8]

    for ref, first in ((own_e, 0), (own_h, 3)):
        ref[...] = jnp.zeros(ref.shape, f32)
        for c in range(3):
            ref[c * PADC : c * PADC + 20, :] = fields[first + c]
    halo_out[0, 0] = own_e[:, count - 128 :]
    halo_out[0, 1] = own_e[:, :128]

    pl.semaphore_wait(barrier, n_dom + 1)
    masks = exchange(mask_out, mask_in, mask_send, mask_recv)
    halo_e = to_neighbours(halo_out.at[0], halo_in.at[0], halo_send.at[0], halo_recv.at[0])

    stat[...] = jnp.zeros(stat.shape, f32)
    stat[GEO : GEO + 9, :] = geometry[...]
    for c in range(3):
        stat[NS + 4 * c : NS + 4 * c + 4, :] = normals[c] * face_scale[...]
    stat[CODE : CODE + 4, :] = face_nbr[...].astype(f32)
    pool[: 2 * FR, :count] = split2(own_e[...])
    pool[2 * FR : 4 * FR, :count] = split2(own_h[...])
    pool[4 * FR :, :count] = split2(stat[...])

    rows = send_rows[...]
    send_hot[...] = one_hot(count, rows)
    picked = dot(pool[:, :count], send_hot[...])
    slot_stat = picked[4 * FR : 4 * FR + 32] + picked[4 * FR + 32 :]
    picked = picked[: 4 * FR].astype(bf16)
    message = jnp.concatenate([dot(pack[...], picked)[:120], slot_stat[:8]], axis=0)
    hand_out[0] = message.T.reshape(n_dom, cap, RK)
    handed_fields = exchange(hand_out.at[0], hand_in.at[0], hand_send.at[0], hand_recv.at[0])
    slot_row = lax.broadcasted_iota(jnp.int32, (1, slots), 1)
    extra = split2(slot_stat[16:24])

    @pl.loop(0, n_dom)
    def _(d):
        part = dot_t(extra, slots_of(d, slot_row))
        extra_out[d] = part[:8] + part[8:]

    extras = exchange(extra_out, extra_in, extra_send, extra_recv)

    rows_hi = rows_lo = None
    for a in range(3):
        hi, lo = split(derivatives[a])
        hi = dot(d_rows[a], hi.astype(bf16))
        lo = dot(d_rows[a], lo.astype(bf16))
        rows_hi = hi if a == 0 else rows_hi + hi
        rows_lo = lo if a == 0 else rows_lo + lo
    wide = dot(rows_hi.astype(bf16), d_hi[...]) + dot(rows_lo.astype(bf16), d_lo[...])
    dmat[...] = (wide * d_mask[...]).astype(bf16)
    hi, lo = split(lift_matrix[...])
    hi = dot(l_rows[...], hi.astype(bf16))
    lo = dot(l_rows[...], lo.astype(bf16))
    wide = dot(hi.astype(bf16), l_hi[...]) + dot(lo.astype(bf16), l_lo[...])
    lmat[...] = (wide * l_mask[...]).astype(bf16)

    traces_e = dot(sel[...], picked[: 2 * FR])
    traces_h = dot(sel[...], picked[2 * FR :])
    held_e, held_h = [], []
    for f in range(4):
        code = slot_stat[CODE + f : CODE + f + 1].astype(jnp.int32)
        face = code & 3
        wall = code == 4 * rows + f
        near = dot(pool[: 4 * FR, :count], one_hot(count, code >> 2)).astype(bf16)
        e = pick_face(dot(sel[...], near[: 2 * FR]), face)
        h = pick_face(dot(sel[...], near[2 * FR :]), face)
        at = f * 3 * FN
        held_e.append(jnp.where(wall, -traces_e[at : at + 3 * FN], e))
        held_h.append(jnp.where(wall, traces_h[at : at + 3 * FN], h))
    finish(masks)

    def add_mask(d, mask):
        part = jnp.concatenate([mask_in[d], jnp.zeros((8, 128), f32)], axis=0).astype(bf16)
        return mask + dot(part, slots_of(d, slot_row))

    mask = lax.fori_loop(0, n_dom, add_mask, jnp.zeros((16, slots), f32))
    kept_e, kept_h = [], []
    for f in range(4):
        keep = mask[f : f + 1] > 0.5
        kept_e += flux(jnp.where(keep, held_e[f], 0.0), slot_stat[NS : NS + 12], f)
        kept_h += flux(jnp.where(keep, held_h[f], 0.0), slot_stat[NS : NS + 12], f)
    kept_e = dot(lmat[...], split3(jnp.concatenate(kept_e, axis=0)))
    kept_h = dot(lmat[...], split3(jnp.concatenate(kept_h, axis=0)))
    kept = jnp.concatenate([split2(kept_e), split2(kept_h)], axis=0)
    message = jnp.concatenate([dot(pack[...], kept)[:120], slot_stat[8:16]], axis=0)
    hand_out[1] = message.T.reshape(n_dom, cap, RK)
    handed_kept = exchange(hand_out.at[1], hand_in.at[1], hand_send.at[1], hand_recv.at[1])

    code_row = jnp.concatenate(codes, axis=1) >> 2
    fine_own[...] = one_hot(fine, code_row)
    fine_halo[...] = one_hot(2 * width, code_row - fine)
    export_at = lax.broadcasted_iota(jnp.int32, (2 * width, fine), 1)
    export_hot = jnp.where(export_at == export_rows[...], 1.0, 0.0).astype(bf16)
    slot_hot = one_hot(slots, my_slots)
    fine_out[...] = jnp.zeros(fine_out.shape, f32)

    @pl.loop(0, count // CHUNK)
    def _(i):
        start = pl.multiple_of(i * CHUNK, CHUNK)
        for f in range(4):
            code = face_nbr[f : f + 1, pl.ds(start, CHUNK)]
            coarse_hot[f, :, pl.ds(start, CHUNK)] = one_hot(full, code >> 2)

    def take(message):
        got = dot(split2(message.reshape(slots, RK).T), slot_hot)
        state = dot(unpack[...], got.astype(bf16))
        return state[:FR], state[FR:], got[120:RK] + got[RK + 120 :]

    finish(handed_fields)
    efield, hfield, stat_a = take(hand_in[0])
    finish(extras)

    def add_extra(d, value):
        return value + dot(split2(extra_in[d]), slots_of(d, my_slots))

    stat_c = lax.fori_loop(0, n_dom, add_extra, jnp.zeros((16, fine), f32))
    stat_c = stat_c[:8] + stat_c[8:]
    finish(handed_kept)
    kept_e, kept_h, stat_b = take(hand_in[1])
    fine_stat = jnp.concatenate([stat_a, stat_b, stat_c], axis=0)
    fine_geo, fine_ns = fine_stat[GEO : GEO + 9], fine_stat[NS : NS + 12]

    def fine_rate(field, kept, turn):
        hi, lo = split(field)
        parts = jnp.concatenate([hi, lo], axis=0).astype(bf16)
        export = dot_t(export_hot, hi.astype(bf16)) + dot_t(export_hot, lo.astype(bf16))
        fine_out[turn, 0, :, :FR] = export[:width]
        fine_out[turn, 1, :, :FR] = export[width:]
        copies = to_neighbours(
            fine_out.at[turn], fine_in.at[turn], fine_send.at[turn], fine_recv.at[turn]
        )
        near = dot(parts, fine_own[...])
        own = dot(sel[...], parts)
        spin = curl(dot(dmat[...], split3(field)), fine_geo) + kept
        for copy in copies:
            copy.wait()
        halo = fine_in[turn].reshape(2 * width, 128).T[:FR]
        near = near + dot(split2(halo), fine_halo[...])
        traces = dot(sel[...], near.astype(bf16))
        fluxes = []
        for f in range(4):
            at = f * 3 * FN
            outside = pick_face(traces[:, f * fine : (f + 1) * fine], codes[f] & 3)
            fluxes += flux(outside - own[at : at + 3 * FN], fine_ns, f)
        return spin + dot(lmat[...], split3(jnp.concatenate(fluxes, axis=0)))

    fine_step = coarse_step / SUBSTEPS
    for substep in range(SUBSTEPS):
        hfield = hfield - fine_step * fine_rate(efield, kept_e, 2 * substep)
        efield = efield + fine_step * fine_rate(hfield, kept_h, 2 * substep + 1)

    result = jnp.concatenate([split2(efield), split2(hfield)], axis=0)
    result = split2(dot(pack[...], result))
    result = dot_t(slot_hot, result)
    result = result[:, :RK] + result[:, RK:]
    back_out[...] = result.reshape(n_dom, cap, RK)
    returned = exchange(back_out, back_in, back_send, back_recv)
    is_fine = dot_t(jnp.ones((16, slots), bf16), send_hot[...])[:1] > 0.5
    finish(returned)
    came = back_in[...].reshape(slots, RK).T
    came = dot_t(split2(came), send_hot[...]).astype(bf16)
    came = dot(unpack[...], came)
    merged_e = jnp.where(is_fine, came[:FR], own_e[...])
    merged_h = jnp.where(is_fine, came[FR:], own_h[...])
    own_e[...] = merged_e
    own_h[...] = merged_h
    pool_e, pool_h = pool.at[: 2 * FR], pool.at[2 * FR : 4 * FR]
    pool_e[:, :count] = split2(merged_e)

    halo_lane = lax.broadcasted_iota(jnp.int32, (FR, 128), 1)
    place = lax.broadcasted_iota(jnp.int32, (1, CHUNK), 1)

    def coarse_rate(start, source, pool, reach, mirror):
        window = pl.ds(start, CHUNK)
        field = source[:, window]
        table = stat[:, window]
        spin = curl(dot(dmat[...], split3(field)), table[GEO : GEO + 9])
        own = dot(sel[...], split2(field))
        ns = table[NS : NS + 12]
        fluxes = []
        for f in range(4):
            code = face_nbr[f : f + 1, window]
            near = dot(pool[:, :reach], coarse_hot[f, :reach, window]).astype(bf16)
            outside = pick_face(dot(sel[...], near), code & 3)
            mine = own[f * 3 * FN : (f + 1) * 3 * FN]
            wall = code == 4 * (start + place) + f
            outside = jnp.where(wall, mirror * mine, outside)
            fluxes += flux(outside - mine, ns, f)
        return spin + dot(lmat[...], split3(jnp.concatenate(fluxes, axis=0)))

    def set_halo(pool, turn, copies):
        for copy in copies:
            copy.wait()
        tile = jnp.where(halo_lane < 64, halo_in[turn, 1], halo_in[turn, 0])
        pool[:, count:] = split2(pltpu.roll(tile, 64, 1))

    def update(start, source, pool, target, first, scale, reach, mirror):
        start = pl.multiple_of(start, CHUNK)
        window = pl.ds(start, CHUNK)
        new = target[:, window] + scale * coarse_rate(start, source, pool, reach, mirror)
        target[:, window] = new
        for c in range(3):
            out[first + c, :, window] = new[c * PADC : c * PADC + 20]
        if first == 3:
            pool_h[:, window] = split2(new)

    last = count - CHUNK
    set_halo(pool_e, 0, halo_e)

    @pl.loop(0, 2)
    def _(i):
        update(i * last, own_e, pool_e, own_h, 3, -coarse_step, full, -1.0)

    halo_out[1, 0] = own_h[:, count - 128 :]
    halo_out[1, 1] = own_h[:, :128]
    halo_h = to_neighbours(halo_out.at[1], halo_in.at[1], halo_send.at[1], halo_recv.at[1])

    @pl.loop(1, count // CHUNK - 1)
    def _(i):
        update(i * CHUNK, own_e, pool_e, own_h, 3, -coarse_step, count, -1.0)

    @pl.loop(1, count // CHUNK - 1)
    def _(i):
        update(i * CHUNK, own_h, pool_h, own_e, 0, coarse_step, count, 1.0)

    set_halo(pool_h, 1, halo_h)

    @pl.loop(0, 2)
    def _(i):
        update(i * last, own_h, pool_h, own_e, 0, coarse_step, full, 1.0)


def per_device(
    n_dom,
    n_sub,
    fields,
    geometry,
    normals,
    face_scale,
    derivatives,
    lift_matrix,
    face_nbr,
    send_rows,
    fine_slots,
    export_rows,
    fine_nbr,
):
    count = fields.shape[2]
    fine = fine_slots.shape[0]
    width = export_rows.shape[1]
    group = send_rows.shape[0] // n_dom
    cap = -(-group // 8) * 8
    slots = n_dom * cap
    turns = 2 * SUBSTEPS
    if cap != group:
        send_rows = jnp.pad(
            send_rows.reshape(n_dom, group),
            ((0, 0), (0, cap - group)),
            constant_values=count,
        ).reshape(-1)
        fine_slots = fine_slots // group * cap + fine_slots % group
    export_rows = jnp.concatenate([export_rows[1], export_rows[0]])
    operands = [
        fields,
        geometry,
        normals,
        face_scale,
        derivatives,
        lift_matrix,
        face_nbr,
        send_rows[None],
        fine_slots[None],
        export_rows[:, None],
        fine_nbr,
        *[jnp.asarray(x) for x in tables()],
    ]
    vmem = pl.BlockSpec(memory_space=pltpu.VMEM)
    dma = pltpu.SemaphoreType.DMA
    return pl.pallas_call(
        functools.partial(kernel, n_dom, n_sub, width),
        out_shape=jax.ShapeDtypeStruct(fields.shape, f32),
        in_specs=[vmem] * len(operands),
        out_specs=vmem,
        scratch_shapes=[
            pltpu.VMEM((FR, count), f32),
            pltpu.VMEM((FR, count), f32),
            pltpu.VMEM((4 * FR + 64, count + 128), bf16),
            pltpu.VMEM((32, count), f32),
            pltpu.VMEM((16, fine), f32),
            pltpu.VMEM((count, slots), bf16),
            pltpu.VMEM((4, count + 128, count), bf16),
            pltpu.VMEM((fine, 4 * fine), bf16),
            pltpu.VMEM((2 * width, 4 * fine), bf16),
            pltpu.VMEM((224, 3 * FR), bf16),
            pltpu.VMEM((FR, 3 * TR), bf16),
            pltpu.VMEM((n_dom, 8, 128), f32),
            pltpu.VMEM((n_dom, 8, 128), f32),
            pltpu.VMEM((n_dom, 8, 128), f32),
            pltpu.VMEM((n_dom, 8, 128), f32),
            pltpu.VMEM((2, n_dom, cap, RK), f32),
            pltpu.VMEM((2, n_dom, cap, RK), f32),
            pltpu.VMEM((n_dom, cap, RK), f32),
            pltpu.VMEM((n_dom, cap, RK), f32),
            pltpu.VMEM((turns, 2, width, 128), f32),
            pltpu.VMEM((turns, 2, width, 128), f32),
            pltpu.VMEM((2, 2, FR, 128), f32),
            pltpu.VMEM((2, 2, FR, 128), f32),
            dma((n_dom,)),
            dma((n_dom,)),
            dma((n_dom,)),
            dma((n_dom,)),
            dma((2, n_dom)),
            dma((2, n_dom)),
            dma((n_dom,)),
            dma((n_dom,)),
            dma((turns, 2)),
            dma((turns, 2)),
            dma((2, 2)),
            dma((2, 2)),
        ],
        compiler_params=pltpu.CompilerParams(
            collective_id=0, has_side_effects=True, vmem_limit_bytes=56 * 1024 * 1024
        ),
    )(*operands)


def solution(mesh):
    return jax.shard_map(
        functools.partial(per_device, mesh.shape["dom"], mesh.shape["sub"]),
        mesh=mesh,
        in_specs=(
            P(None, None, ("dom", "sub")),
            P(None, ("dom", "sub")),
            P(None, None, ("dom", "sub")),
            P(None, ("dom", "sub")),
            P(),
            P(),
            P(None, ("dom", "sub")),
            P(("dom", "sub")),
            P(("dom", "sub")),
            P(None, ("dom", "sub")),
            P(None, ("dom", "sub")),
        ),
        out_specs=P(None, None, ("dom", "sub")),
        check_vma=False,
    )
```

```python
import functools

import jax
import jax.numpy as jnp
import numpy as np
from jax import lax
from jax.experimental import pallas as pl
from jax.experimental.pallas import tpu as pltpu
from jax.sharding import PartitionSpec as P

SUBSTEPS = 4
coarse_step = 0.2

PADC = 24
FR = 80
FN = 16
TR = 192
RK = 128
GEO, NS, CODE = 0, 9, 24
CHUNK = 256

bf16 = jnp.bfloat16
f32 = jnp.float32
MESH = pl.DeviceIdType.MESH


def face_table():
    places = [
        (along_r, along_s, along_t)
        for along_t in range(4)
        for along_s in range(4 - along_t)
        for along_r in range(4 - along_t - along_s)
    ]
    bottom_face = [number for number, location in enumerate(places) if location[2] == 0]
    front_face = [number for number, location in enumerate(places) if location[1] == 0]
    slanted = [number for number, location in enumerate(places) if sum(location) == 3]
    beside = [number for number, location in enumerate(places) if location[0] == 0]
    return np.array([bottom_face, front_face, slanted, beside], dtype=np.int32).T


def tables():
    nodes = face_table()
    sel = np.zeros((TR, 2 * FR), np.float32)
    pack = np.zeros((RK, 4 * FR), np.float32)
    unpack = np.zeros((2 * FR, 2 * RK), np.float32)
    for c in range(3):
        for p in range(20):
            for field in range(2):
                packed = (field * 3 + c) * 20 + p
                for s in range(2):
                    pack[packed, field * 2 * FR + s * FR + c * PADC + p] = 1
                    unpack[field * FR + c * PADC + p, s * RK + packed] = 1
        for f in range(4):
            for n in range(10):
                for s in range(2):
                    sel[f * 3 * FN + c * FN + n, s * FR + c * PADC + nodes[n, f]] = 1
    d_rows = np.zeros((3, 224, 20), np.float32)
    d_hi = np.zeros((20, 3 * FR), np.float32)
    d_lo = np.zeros((20, 3 * FR), np.float32)
    d_mask = np.zeros((224, 3 * FR), np.float32)
    l_rows = np.zeros((FR, 20), np.float32)
    l_hi = np.zeros((40, 3 * TR), np.float32)
    l_lo = np.zeros((40, 3 * TR), np.float32)
    l_mask = np.zeros((FR, 3 * TR), np.float32)
    for c in range(3):
        for p in range(20):
            l_rows[c * PADC + p, p] = 1
            for a in range(3):
                d_rows[a, (a * 3 + c) * PADC + p, p] = 1
            d_hi[p, c * PADC + p] = 1
            d_hi[p, FR + c * PADC + p] = 1
            d_lo[p, 2 * FR + c * PADC + p] = 1
        for s in range(3):
            for a in range(3):
                at = (a * 3 + c) * PADC
                d_mask[at : at + 20, s * FR + c * PADC : s * FR + c * PADC + 20] = 1
            for f in range(4):
                col = s * TR + f * 3 * FN + c * FN
                l_mask[c * PADC : c * PADC + 20, col : col + 10] = 0.5
                for n in range(10):
                    (l_lo if s == 2 else l_hi)[f * 10 + n, col + n] = 1
    out = [unpack, d_rows, d_hi, d_lo, l_rows, l_hi, l_lo]
    return [sel, pack] + [x.astype(jnp.bfloat16) for x in out] + [d_mask, l_mask]


def split(x):
    hi = x.astype(bf16).astype(f32)
    return hi, x - hi


def split2(x):
    hi, lo = split(x)
    return jnp.concatenate([hi, lo], axis=0).astype(bf16)


def split3(x):
    hi, lo = split(x)
    return jnp.concatenate([hi, lo, hi], axis=0).astype(bf16)


def dot(a, b):
    return jnp.dot(a, b, preferred_element_type=f32)


def dot_t(a, b):
    return lax.dot_general(a, b, (((1,), (1,)), ((), ())), preferred_element_type=f32)


def one_hot(count, row):
    at = lax.broadcasted_iota(jnp.int32, (count, row.shape[1]), 0)
    return jnp.where(at == row, 1.0, 0.0).astype(bf16)


def curl(grad, geo):
    def partial(m, c):
        total = None
        for a in range(3):
            at = (a * 3 + c) * PADC
            term = geo[3 * m + a : 3 * m + a + 1] * grad[at : at + PADC]
            total = term if total is None else total + term
        return total

    parts = [
        partial(1, 2) - partial(2, 1),
        partial(2, 0) - partial(0, 2),
        partial(0, 1) - partial(1, 0),
    ]
    pad = jnp.zeros((FR - 3 * PADC, grad.shape[1]), f32)
    return jnp.concatenate([*parts, pad], axis=0)


def pick_face(traces, face):
    total = traces[: 3 * FN]
    for g in range(1, 4):
        total = jnp.where(face == g, traces[g * 3 * FN : (g + 1) * 3 * FN], total)
    return total


def flux(jump, ns, f):
    n = [ns[c * 4 + f : c * 4 + f + 1] for c in range(3)]
    j = [jump[c * FN : (c + 1) * FN] for c in range(3)]
    return [
        n[1] * j[2] - n[2] * j[1],
        n[2] * j[0] - n[0] * j[2],
        n[0] * j[1] - n[1] * j[0],
    ]


OPERANDS = 22


def kernel(n_dom, n_sub, width, *refs):
    given, out = refs[:OPERANDS], refs[OPERANDS]
    local, load_sem = refs[OPERANDS + 1 : 2 * OPERANDS + 1], refs[2 * OPERANDS + 1]
    (
        fields,
        geometry,
        normals,
        face_scale,
        derivatives,
        lift_matrix,
        face_nbr,
        send_rows,
        fine_slots,
        export_rows,
        fine_nbr,
        sel_full,
        pack_full,
        unpack,
        d_rows,
        d_hi,
        d_lo,
        l_rows,
        l_hi,
        l_lo,
        d_mask,
        l_mask,
    ) = local
    (
    own_e,
    own_h,
    pool,
    stat,
    frozen,
    sel,
    pack,
    send_hot,
    coarse_hot,
    fine_own,
    fine_halo,
    dmat,
    lmat,
    mask_out,
    mask_in,
    extra_out,
    extra_in,
    hand_out,
    hand_in,
    back_out,
    back_in,
    fine_out,
    fine_in,
    halo_out,
    halo_in,
    mask_send,
    mask_recv,
    extra_send,
    extra_recv,
    hand_send,
    hand_recv,
    back_send,
    back_recv,
    fine_send,
    fine_recv,
    halo_send,
    halo_recv,
    ) = refs[2 * OPERANDS + 2 :]
    count = fields.shape[2]
    fine = fine_slots.shape[1]
    cap = hand_out.shape[2]
    slots = n_dom * cap
    full = count + 128
    dom, sub = lax.axis_index("dom"), lax.axis_index("sub")
    me = dom * n_sub + sub
    total = n_dom * n_sub
    after, before = lax.rem(me + 1, total), lax.rem(me + total - 1, total)
    after_id = (after // n_sub, lax.rem(after, n_sub))
    before_id = (before // n_sub, lax.rem(before, n_sub))

    loads = [
        pltpu.make_async_copy(src, dst, load_sem.at[i])
        for i, (src, dst) in enumerate(zip(given, local))
    ]
    first_loads = [10, 8, 0]
    later_loads = [i for i in range(OPERANDS) if i not in first_loads]
    for i in first_loads + later_loads:
        loads[i].start()

    barrier = pltpu.get_barrier_semaphore()
    for target in (after_id, before_id):
        pl.semaphore_signal(barrier, inc=1, device_id=target, device_id_type=MESH)

    @pl.loop(1, n_dom)
    def _(i):
        pl.semaphore_signal(
            barrier, inc=1, device_id=(lax.rem(dom + i, n_dom), sub), device_id_type=MESH
        )

    def exchange(src, dst, send, recv):
        def copy(i):
            target = lax.rem(dom + i, n_dom)
            return pltpu.make_async_remote_copy(
                src_ref=src.at[target],
                dst_ref=dst.at[dom],
                send_sem=send.at[i],
                recv_sem=recv.at[i],
                device_id=(target, sub),
                device_id_type=MESH,
            )

        @pl.loop(1, n_dom)
        def _(i):
            copy(i).start()

        dst[pl.ds(dom, 1)] = src[pl.ds(dom, 1)]
        return copy

    def finish(copy):
        @pl.loop(1, n_dom)
        def _(i):
            copy(i).wait()

    def to_neighbours(src, dst, send, recv):
        copies = []
        for side, target in enumerate((after_id, before_id)):
            copy = pltpu.make_async_remote_copy(
                src_ref=src.at[side],
                dst_ref=dst.at[side],
                send_sem=send.at[side],
                recv_sem=recv.at[side],
                device_id=target,
                device_id_type=MESH,
            )
            copy.start()
            copies.append(copy)
        return copies

    def slots_of(d, row):
        at = lax.broadcasted_iota(jnp.int32, (128, row.shape[1]), 0)
        return jnp.where((row - d * cap == at) & (at < cap), 1.0, 0.0).astype(bf16)

    for i in first_loads:
        loads[i].wait()

    codes = [fine_nbr[f : f + 1, :] for f in range(4)]
    frozen_code = 4 * fine + 8 * width
    frozen[...] = jnp.zeros(frozen.shape, f32)
    frozen[0:4, :] = jnp.where(fine_nbr[...] == frozen_code, 1.0, 0.0)
    my_slots = fine_slots[...]

    @pl.loop(0, n_dom)
    def _(d):
        mask_out[d] = dot_t(frozen[...].astype(bf16), slots_of(d, my_slots))[:8]

    for ref, first in ((own_e, 0), (own_h, 3)):
        ref[...] = jnp.zeros(ref.shape, f32)
        for c in range(3):
            ref[c * PADC : c * PADC + 20, :] = fields[first + c]
    halo_out[0, 0] = own_e[:, count - 128 :]
    halo_out[0, 1] = own_e[:, :128]

    pl.semaphore_wait(barrier, n_dom + 1)
    masks = exchange(mask_out, mask_in, mask_send, mask_recv)
    halo_e = to_neighbours(halo_out.at[0], halo_in.at[0], halo_send.at[0], halo_recv.at[0])

    for i in later_loads:
        loads[i].wait()

    sel[...] = sel_full[...].astype(bf16)
    pack[...] = pack_full[...].astype(bf16)

    stat[...] = jnp.zeros(stat.shape, f32)
    stat[GEO : GEO + 9, :] = geometry[...]
    for c in range(3):
        stat[NS + 4 * c : NS + 4 * c + 4, :] = normals[c] * face_scale[...]
    stat[CODE : CODE + 4, :] = face_nbr[...].astype(f32)
    pool[: 2 * FR, :count] = split2(own_e[...])
    pool[2 * FR : 4 * FR, :count] = split2(own_h[...])
    pool[4 * FR :, :count] = split2(stat[...])

    rows = send_rows[...]
    send_hot[...] = one_hot(count, rows)
    picked = dot(pool[:, :count], send_hot[...])
    slot_stat = picked[4 * FR : 4 * FR + 32] + picked[4 * FR + 32 :]
    picked = picked[: 4 * FR].astype(bf16)
    message = jnp.concatenate([dot(pack[...], picked)[:120], slot_stat[:8]], axis=0)
    hand_out[0] = message.T.reshape(n_dom, cap, RK)
    handed_fields = exchange(hand_out.at[0], hand_in.at[0], hand_send.at[0], hand_recv.at[0])
    slot_row = lax.broadcasted_iota(jnp.int32, (1, slots), 1)
    extra = split2(slot_stat[16:24])

    @pl.loop(0, n_dom)
    def _(d):
        part = dot_t(extra, slots_of(d, slot_row))
        extra_out[d] = part[:8] + part[8:]

    extras = exchange(extra_out, extra_in, extra_send, extra_recv)

    rows_hi = rows_lo = None
    for a in range(3):
        hi, lo = split(derivatives[a])
        hi = dot(d_rows[a], hi.astype(bf16))
        lo = dot(d_rows[a], lo.astype(bf16))
        rows_hi = hi if a == 0 else rows_hi + hi
        rows_lo = lo if a == 0 else rows_lo + lo
    wide = dot(rows_hi.astype(bf16), d_hi[...]) + dot(rows_lo.astype(bf16), d_lo[...])
    dmat[...] = (wide * d_mask[...]).astype(bf16)
    hi, lo = split(lift_matrix[...])
    hi = dot(l_rows[...], hi.astype(bf16))
    lo = dot(l_rows[...], lo.astype(bf16))
    wide = dot(hi.astype(bf16), l_hi[...]) + dot(lo.astype(bf16), l_lo[...])
    lmat[...] = (wide * l_mask[...]).astype(bf16)

    traces_e = dot(sel[...], picked[: 2 * FR])
    traces_h = dot(sel[...], picked[2 * FR :])
    held_e, held_h = [], []
    for f in range(4):
        code = slot_stat[CODE + f : CODE + f + 1].astype(jnp.int32)
        face = code & 3
        wall = code == 4 * rows + f
        near = dot(pool[: 4 * FR, :count], one_hot(count, code >> 2)).astype(bf16)
        e = pick_face(dot(sel[...], near[: 2 * FR]), face)
        h = pick_face(dot(sel[...], near[2 * FR :]), face)
        at = f * 3 * FN
        held_e.append(jnp.where(wall, -traces_e[at : at + 3 * FN], e))
        held_h.append(jnp.where(wall, traces_h[at : at + 3 * FN], h))
    finish(masks)

    def add_mask(d, mask):
        part = jnp.concatenate([mask_in[d], jnp.zeros((8, 128), f32)], axis=0).astype(bf16)
        return mask + dot(part, slots_of(d, slot_row))

    mask = lax.fori_loop(0, n_dom, add_mask, jnp.zeros((16, slots), f32))
    kept_e, kept_h = [], []
    for f in range(4):
        keep = mask[f : f + 1] > 0.5
        kept_e += flux(jnp.where(keep, held_e[f], 0.0), slot_stat[NS : NS + 12], f)
        kept_h += flux(jnp.where(keep, held_h[f], 0.0), slot_stat[NS : NS + 12], f)
    kept_e = dot(lmat[...], split3(jnp.concatenate(kept_e, axis=0)))
    kept_h = dot(lmat[...], split3(jnp.concatenate(kept_h, axis=0)))
    kept = jnp.concatenate([split2(kept_e), split2(kept_h)], axis=0)
    message = jnp.concatenate([dot(pack[...], kept)[:120], slot_stat[8:16]], axis=0)
    hand_out[1] = message.T.reshape(n_dom, cap, RK)
    handed_kept = exchange(hand_out.at[1], hand_in.at[1], hand_send.at[1], hand_recv.at[1])

    code_row = jnp.concatenate(codes, axis=1) >> 2
    fine_own[...] = one_hot(fine, code_row)
    fine_halo[...] = one_hot(2 * width, code_row - fine)
    eye = one_hot(width, lax.broadcasted_iota(jnp.int32, (1, width), 1))
    export_hot = jnp.concatenate(
        [dot_t(eye, one_hot(fine, export_rows[side : side + 1, :])) for side in (1, 0)], axis=0
    ).astype(bf16)
    slot_hot = one_hot(slots, my_slots)
    fine_out[...] = jnp.zeros(fine_out.shape, f32)

    @pl.loop(0, count // CHUNK)
    def _(i):
        start = pl.multiple_of(i * CHUNK, CHUNK)
        for f in range(4):
            code = face_nbr[f : f + 1, pl.ds(start, CHUNK)]
            coarse_hot[f, :, pl.ds(start, CHUNK)] = one_hot(full, code >> 2)

    def take(message):
        got = dot(split2(message.reshape(slots, RK).T), slot_hot)
        state = dot(unpack[...], got.astype(bf16))
        return state[:FR], state[FR:], got[120:RK] + got[RK + 120 :]

    finish(handed_fields)
    efield, hfield, stat_a = take(hand_in[0])
    finish(extras)

    def add_extra(d, value):
        return value + dot(split2(extra_in[d]), slots_of(d, my_slots))

    stat_c = lax.fori_loop(0, n_dom, add_extra, jnp.zeros((16, fine), f32))
    stat_c = stat_c[:8] + stat_c[8:]
    finish(handed_kept)
    kept_e, kept_h, stat_b = take(hand_in[1])
    fine_stat = jnp.concatenate([stat_a, stat_b, stat_c], axis=0)
    fine_geo, fine_ns = fine_stat[GEO : GEO + 9], fine_stat[NS : NS + 12]

    def fine_rate(field, kept, turn):
        hi, lo = split(field)
        parts = jnp.concatenate([hi, lo], axis=0).astype(bf16)
        export = dot_t(export_hot, hi.astype(bf16)) + dot_t(export_hot, lo.astype(bf16))
        fine_out[turn, 0, :, :FR] = export[:width]
        fine_out[turn, 1, :, :FR] = export[width:]
        copies = to_neighbours(
            fine_out.at[turn], fine_in.at[turn], fine_send.at[turn], fine_recv.at[turn]
        )
        near = dot(parts, fine_own[...])
        own = dot(sel[...], parts)
        spin = curl(dot(dmat[...], split3(field)), fine_geo) + kept
        for copy in copies:
            copy.wait()
        halo = fine_in[turn].reshape(2 * width, 128).T[:FR]
        near = near + dot(split2(halo), fine_halo[...])
        traces = dot(sel[...], near.astype(bf16))
        fluxes = []
        for f in range(4):
            at = f * 3 * FN
            outside = pick_face(traces[:, f * fine : (f + 1) * fine], codes[f] & 3)
            fluxes += flux(outside - own[at : at + 3 * FN], fine_ns, f)
        return spin + dot(lmat[...], split3(jnp.concatenate(fluxes, axis=0)))

    fine_step = coarse_step / SUBSTEPS
    for substep in range(SUBSTEPS):
        hfield = hfield - fine_step * fine_rate(efield, kept_e, 2 * substep)
        efield = efield + fine_step * fine_rate(hfield, kept_h, 2 * substep + 1)

    result = jnp.concatenate([split2(efield), split2(hfield)], axis=0)
    result = split2(dot(pack[...], result))
    result = dot_t(slot_hot, result)
    result = result[:, :RK] + result[:, RK:]
    back_out[...] = result.reshape(n_dom, cap, RK)
    returned = exchange(back_out, back_in, back_send, back_recv)
    is_fine = dot_t(jnp.ones((16, slots), bf16), send_hot[...])[:1] > 0.5
    finish(returned)
    came = back_in[...].reshape(slots, RK).T
    came = dot_t(split2(came), send_hot[...]).astype(bf16)
    came = dot(unpack[...], came)
    merged_e = jnp.where(is_fine, came[:FR], own_e[...])
    merged_h = jnp.where(is_fine, came[FR:], own_h[...])
    own_e[...] = merged_e
    own_h[...] = merged_h
    pool_e, pool_h = pool.at[: 2 * FR], pool.at[2 * FR : 4 * FR]
    pool_e[:, :count] = split2(merged_e)

    halo_lane = lax.broadcasted_iota(jnp.int32, (FR, 128), 1)
    place = lax.broadcasted_iota(jnp.int32, (1, CHUNK), 1)

    def coarse_rate(start, source, pool, reach, mirror):
        window = pl.ds(start, CHUNK)
        field = source[:, window]
        table = stat[:, window]
        spin = curl(dot(dmat[...], split3(field)), table[GEO : GEO + 9])
        own = dot(sel[...], split2(field))
        ns = table[NS : NS + 12]
        fluxes = []
        for f in range(4):
            code = face_nbr[f : f + 1, window]
            near = dot(pool[:, :reach], coarse_hot[f, :reach, window]).astype(bf16)
            outside = pick_face(dot(sel[...], near), code & 3)
            mine = own[f * 3 * FN : (f + 1) * 3 * FN]
            wall = code == 4 * (start + place) + f
            outside = jnp.where(wall, mirror * mine, outside)
            fluxes += flux(outside - mine, ns, f)
        return spin + dot(lmat[...], split3(jnp.concatenate(fluxes, axis=0)))

    def set_halo(pool, turn, copies):
        for copy in copies:
            copy.wait()
        tile = jnp.where(halo_lane < 64, halo_in[turn, 1], halo_in[turn, 0])
        pool[:, count:] = split2(pltpu.roll(tile, 64, 1))

    def update(start, source, pool, target, first, scale, reach, mirror):
        start = pl.multiple_of(start, CHUNK)
        window = pl.ds(start, CHUNK)
        new = target[:, window] + scale * coarse_rate(start, source, pool, reach, mirror)
        target[:, window] = new
        for c in range(3):
            out[first + c, :, window] = new[c * PADC : c * PADC + 20]
        if first == 3:
            pool_h[:, window] = split2(new)

    last = count - CHUNK
    set_halo(pool_e, 0, halo_e)

    @pl.loop(0, 2)
    def _(i):
        update(i * last, own_e, pool_e, own_h, 3, -coarse_step, full, -1.0)

    halo_out[1, 0] = own_h[:, count - 128 :]
    halo_out[1, 1] = own_h[:, :128]
    halo_h = to_neighbours(halo_out.at[1], halo_in.at[1], halo_send.at[1], halo_recv.at[1])

    @pl.loop(1, count // CHUNK - 1)
    def _(i):
        update(i * CHUNK, own_e, pool_e, own_h, 3, -coarse_step, count, -1.0)

    @pl.loop(1, count // CHUNK - 1)
    def _(i):
        update(i * CHUNK, own_h, pool_h, own_e, 0, coarse_step, count, 1.0)

    set_halo(pool_h, 1, halo_h)

    @pl.loop(0, 2)
    def _(i):
        update(i * last, own_h, pool_h, own_e, 0, coarse_step, full, 1.0)


def per_device(
    n_dom,
    n_sub,
    fields,
    geometry,
    normals,
    face_scale,
    derivatives,
    lift_matrix,
    face_nbr,
    send_rows,
    fine_slots,
    export_rows,
    fine_nbr,
):
    count = fields.shape[2]
    fine = fine_slots.shape[0]
    width = export_rows.shape[1]
    group = send_rows.shape[0] // n_dom
    cap = -(-group // 8) * 8
    slots = n_dom * cap
    turns = 2 * SUBSTEPS
    if cap != group:
        send_rows = jnp.pad(
            send_rows.reshape(n_dom, group),
            ((0, 0), (0, cap - group)),
            constant_values=count,
        ).reshape(-1)
        fine_slots = fine_slots // group * cap + fine_slots % group
    operands = [
        fields,
        geometry,
        normals,
        face_scale,
        derivatives,
        lift_matrix,
        face_nbr,
        send_rows[None],
        fine_slots[None],
        export_rows,
        fine_nbr,
        *[jnp.asarray(x) for x in tables()],
    ]
    vmem = pl.BlockSpec(memory_space=pltpu.VMEM)
    dma = pltpu.SemaphoreType.DMA
    return pl.pallas_call(
        functools.partial(kernel, n_dom, n_sub, width),
        out_shape=jax.ShapeDtypeStruct(fields.shape, f32),
        in_specs=[pl.BlockSpec(memory_space=pl.ANY)] * len(operands),
        out_specs=vmem,
        scratch_shapes=[
            *[pltpu.VMEM(x.shape, x.dtype) for x in operands],
            dma((len(operands),)),
            pltpu.VMEM((FR, count), f32),
            pltpu.VMEM((FR, count), f32),
            pltpu.VMEM((4 * FR + 64, count + 128), bf16),
            pltpu.VMEM((32, count), f32),
            pltpu.VMEM((16, fine), f32),
            pltpu.VMEM((TR, 2 * FR), bf16),
            pltpu.VMEM((RK, 4 * FR), bf16),
            pltpu.VMEM((count, slots), bf16),
            pltpu.VMEM((4, count + 128, count), bf16),
            pltpu.VMEM((fine, 4 * fine), bf16),
            pltpu.VMEM((2 * width, 4 * fine), bf16),
            pltpu.VMEM((224, 3 * FR), bf16),
            pltpu.VMEM((FR, 3 * TR), bf16),
            pltpu.VMEM((n_dom, 8, 128), f32),
            pltpu.VMEM((n_dom, 8, 128), f32),
            pltpu.VMEM((n_dom, 8, 128), f32),
            pltpu.VMEM((n_dom, 8, 128), f32),
            pltpu.VMEM((2, n_dom, cap, RK), f32),
            pltpu.VMEM((2, n_dom, cap, RK), f32),
            pltpu.VMEM((n_dom, cap, RK), f32),
            pltpu.VMEM((n_dom, cap, RK), f32),
            pltpu.VMEM((turns, 2, width, 128), f32),
            pltpu.VMEM((turns, 2, width, 128), f32),
            pltpu.VMEM((2, 2, FR, 128), f32),
            pltpu.VMEM((2, 2, FR, 128), f32),
            dma((n_dom,)),
            dma((n_dom,)),
            dma((n_dom,)),
            dma((n_dom,)),
            dma((2, n_dom)),
            dma((2, n_dom)),
            dma((n_dom,)),
            dma((n_dom,)),
            dma((turns, 2)),
            dma((turns, 2)),
            dma((2, 2)),
            dma((2, 2)),
        ],
        compiler_params=pltpu.CompilerParams(
            collective_id=0, has_side_effects=True, vmem_limit_bytes=56 * 1024 * 1024
        ),
    )(*operands)


def solution(mesh):
    return jax.shard_map(
        functools.partial(per_device, mesh.shape["dom"], mesh.shape["sub"]),
        mesh=mesh,
        in_specs=(
            P(None, None, ("dom", "sub")),
            P(None, ("dom", "sub")),
            P(None, None, ("dom", "sub")),
            P(None, ("dom", "sub")),
            P(),
            P(),
            P(None, ("dom", "sub")),
            P(("dom", "sub")),
            P(("dom", "sub")),
            P(None, ("dom", "sub")),
            P(None, ("dom", "sub")),
        ),
        out_specs=P(None, None, ("dom", "sub")),
        check_vma=False,
    )
```

```python
import functools

import jax
import jax.numpy as jnp
import numpy as np
from jax import lax
from jax.experimental import pallas as pl
from jax.experimental.pallas import tpu as pltpu
from jax.sharding import PartitionSpec as P

SUBSTEPS = 4
coarse_step = 0.2

PADC = 24
FR = 80
FN = 16
TR = 192
RK = 128
GEO, NS, CODE = 0, 9, 24
CHUNK = 256

bf16 = jnp.bfloat16
f32 = jnp.float32
MESH = pl.DeviceIdType.MESH


def face_table():
    places = [
        (along_r, along_s, along_t)
        for along_t in range(4)
        for along_s in range(4 - along_t)
        for along_r in range(4 - along_t - along_s)
    ]
    bottom_face = [number for number, location in enumerate(places) if location[2] == 0]
    front_face = [number for number, location in enumerate(places) if location[1] == 0]
    slanted = [number for number, location in enumerate(places) if sum(location) == 3]
    beside = [number for number, location in enumerate(places) if location[0] == 0]
    return np.array([bottom_face, front_face, slanted, beside], dtype=np.int32).T


def tables():
    nodes = face_table()
    sel = np.zeros((TR, 2 * FR), np.float32)
    pack = np.zeros((RK, 4 * FR), np.float32)
    unpack = np.zeros((2 * FR, 2 * RK), np.float32)
    for c in range(3):
        for p in range(20):
            for field in range(2):
                packed = (field * 3 + c) * 20 + p
                for s in range(2):
                    pack[packed, field * 2 * FR + s * FR + c * PADC + p] = 1
                    unpack[field * FR + c * PADC + p, s * RK + packed] = 1
        for f in range(4):
            for n in range(10):
                for s in range(2):
                    sel[f * 3 * FN + c * FN + n, s * FR + c * PADC + nodes[n, f]] = 1
    d_rows = np.zeros((3, 224, 20), np.float32)
    d_hi = np.zeros((20, 3 * FR), np.float32)
    d_lo = np.zeros((20, 3 * FR), np.float32)
    d_mask = np.zeros((224, 3 * FR), np.float32)
    l_rows = np.zeros((FR, 20), np.float32)
    l_hi = np.zeros((40, 3 * TR), np.float32)
    l_lo = np.zeros((40, 3 * TR), np.float32)
    l_mask = np.zeros((FR, 3 * TR), np.float32)
    for c in range(3):
        for p in range(20):
            l_rows[c * PADC + p, p] = 1
            for a in range(3):
                d_rows[a, (a * 3 + c) * PADC + p, p] = 1
            d_hi[p, c * PADC + p] = 1
            d_hi[p, FR + c * PADC + p] = 1
            d_lo[p, 2 * FR + c * PADC + p] = 1
        for s in range(3):
            for a in range(3):
                at = (a * 3 + c) * PADC
                d_mask[at : at + 20, s * FR + c * PADC : s * FR + c * PADC + 20] = 1
            for f in range(4):
                col = s * TR + f * 3 * FN + c * FN
                l_mask[c * PADC : c * PADC + 20, col : col + 10] = 0.5
                for n in range(10):
                    (l_lo if s == 2 else l_hi)[f * 10 + n, col + n] = 1
    out = [unpack, d_rows, d_hi, d_lo, l_rows, l_hi, l_lo]
    return [sel, pack] + [x.astype(jnp.bfloat16) for x in out] + [d_mask, l_mask]


def split(x):
    hi = x.astype(bf16).astype(f32)
    return hi, x - hi


def split2(x):
    hi, lo = split(x)
    return jnp.concatenate([hi, lo], axis=0).astype(bf16)


def split3(x):
    hi, lo = split(x)
    return jnp.concatenate([hi, lo, hi], axis=0).astype(bf16)


def dot(a, b):
    return jnp.dot(a, b, preferred_element_type=f32)


def dot_t(a, b):
    return lax.dot_general(a, b, (((1,), (1,)), ((), ())), preferred_element_type=f32)


def one_hot(count, row):
    at = lax.broadcasted_iota(jnp.int32, (count, row.shape[1]), 0)
    return jnp.where(at == row, 1.0, 0.0).astype(bf16)


def curl(grad, geo):
    def partial(m, c):
        total = None
        for a in range(3):
            at = (a * 3 + c) * PADC
            term = geo[3 * m + a : 3 * m + a + 1] * grad[at : at + PADC]
            total = term if total is None else total + term
        return total

    parts = [
        partial(1, 2) - partial(2, 1),
        partial(2, 0) - partial(0, 2),
        partial(0, 1) - partial(1, 0),
    ]
    pad = jnp.zeros((FR - 3 * PADC, grad.shape[1]), f32)
    return jnp.concatenate([*parts, pad], axis=0)


def pick_face(traces, face):
    total = traces[: 3 * FN]
    for g in range(1, 4):
        total = jnp.where(face == g, traces[g * 3 * FN : (g + 1) * 3 * FN], total)
    return total


def flux(jump, ns, f):
    n = [ns[c * 4 + f : c * 4 + f + 1] for c in range(3)]
    j = [jump[c * FN : (c + 1) * FN] for c in range(3)]
    return [
        n[1] * j[2] - n[2] * j[1],
        n[2] * j[0] - n[0] * j[2],
        n[0] * j[1] - n[1] * j[0],
    ]


OPERANDS = 22


def kernel(n_dom, n_sub, width, *refs):
    given, out = refs[:OPERANDS], refs[OPERANDS]
    local, load_sem = refs[OPERANDS + 1 : 2 * OPERANDS + 1], refs[2 * OPERANDS + 1]
    (
        fields,
        geometry,
        normals,
        face_scale,
        derivatives,
        lift_matrix,
        face_nbr,
        send_rows,
        fine_slots,
        export_rows,
        fine_nbr,
        sel_full,
        pack_full,
        unpack,
        d_rows,
        d_hi,
        d_lo,
        l_rows,
        l_hi,
        l_lo,
        d_mask,
        l_mask,
    ) = local
    (
    own_e,
    own_h,
    pool,
    stat,
    frozen,
    sel,
    pack,
    send_hot,
    coarse_hot,
    fine_own,
    fine_halo,
    tile_own,
    tile_halo,
    dmat,
    lmat,
    mask_out,
    mask_in,
    extra_out,
    extra_in,
    hand_out,
    hand_in,
    back_out,
    back_in,
    code_out,
    code_in,
    first_out,
    first_in,
    fine_out,
    fine_in,
    halo_out,
    halo_in,
    mask_send,
    mask_recv,
    extra_send,
    extra_recv,
    hand_send,
    hand_recv,
    back_send,
    back_recv,
    code_send,
    code_recv,
    first_send,
    first_recv,
    fine_send,
    fine_recv,
    halo_send,
    halo_recv,
    ) = refs[2 * OPERANDS + 2 :]
    count = fields.shape[2]
    fine = fine_slots.shape[1]
    cap = hand_out.shape[2]
    slots = n_dom * cap
    full = count + 128
    dom, sub = lax.axis_index("dom"), lax.axis_index("sub")
    me = dom * n_sub + sub
    total = n_dom * n_sub
    after, before = lax.rem(me + 1, total), lax.rem(me + total - 1, total)
    after_id = (after // n_sub, lax.rem(after, n_sub))
    before_id = (before // n_sub, lax.rem(before, n_sub))
    after2, before2 = lax.rem(me + 2, total), lax.rem(me + total - 2, total)
    after2_id = (after2 // n_sub, lax.rem(after2, n_sub))
    before2_id = (before2 // n_sub, lax.rem(before2, n_sub))

    loads = [
        pltpu.make_async_copy(src, dst, load_sem.at[i])
        for i, (src, dst) in enumerate(zip(given, local))
    ]
    first_loads = [10, 8, 9, 0]
    later_loads = [i for i in range(OPERANDS) if i not in first_loads]
    for i in first_loads + later_loads:
        loads[i].start()

    barrier = pltpu.get_barrier_semaphore()
    for target in (after_id, before_id, after2_id, before2_id):
        pl.semaphore_signal(barrier, inc=1, device_id=target, device_id_type=MESH)

    @pl.loop(1, n_dom)
    def _(i):
        pl.semaphore_signal(
            barrier, inc=1, device_id=(lax.rem(dom + i, n_dom), sub), device_id_type=MESH
        )

    def exchange(src, dst, send, recv):
        def copy(i):
            target = lax.rem(dom + i, n_dom)
            return pltpu.make_async_remote_copy(
                src_ref=src.at[target],
                dst_ref=dst.at[dom],
                send_sem=send.at[i],
                recv_sem=recv.at[i],
                device_id=(target, sub),
                device_id_type=MESH,
            )

        @pl.loop(1, n_dom)
        def _(i):
            copy(i).start()

        dst[pl.ds(dom, 1)] = src[pl.ds(dom, 1)]
        return copy

    def finish(copy):
        @pl.loop(1, n_dom)
        def _(i):
            copy(i).wait()

    def to_neighbours(src, dst, send, recv):
        copies = []
        for side, target in enumerate((after_id, before_id)):
            copy = pltpu.make_async_remote_copy(
                src_ref=src.at[side],
                dst_ref=dst.at[side],
                send_sem=send.at[side],
                recv_sem=recv.at[side],
                device_id=target,
                device_id_type=MESH,
            )
            copy.start()
            copies.append(copy)
        return copies

    def slots_of(d, row):
        at = lax.broadcasted_iota(jnp.int32, (128, row.shape[1]), 0)
        return jnp.where((row - d * cap == at) & (at < cap), 1.0, 0.0).astype(bf16)

    for i in first_loads:
        loads[i].wait()

    codes = [fine_nbr[f : f + 1, :] for f in range(4)]
    frozen_code = 4 * fine + 8 * width
    frozen[...] = jnp.zeros(frozen.shape, f32)
    frozen[0:4, :] = jnp.where(fine_nbr[...] == frozen_code, 1.0, 0.0)
    frozen[4:8, :] = fine_nbr[...].astype(f32)
    my_slots = fine_slots[...]

    eye = one_hot(width, lax.broadcasted_iota(jnp.int32, (1, width), 1))
    export_up = dot_t(eye, one_hot(fine, export_rows[1:2, :])).astype(bf16)
    export_down = dot_t(eye, one_hot(fine, export_rows[0:1, :])).astype(bf16)
    export_hot = jnp.concatenate([export_up, export_down], axis=0)
    code_row = jnp.concatenate(codes, axis=1) >> 2
    fine_own[...] = one_hot(fine, code_row)
    hi, lo = split(frozen[...])
    exported = dot_t(export_hot, hi.astype(bf16)) + dot_t(export_hot, lo.astype(bf16))
    code_out[...] = jnp.zeros(code_out.shape, f32)
    code_out[0, :, :16] = exported[:width]
    code_out[1, :, :16] = exported[width:]

    @pl.loop(0, n_dom)
    def _(d):
        mask_out[d] = dot_t(frozen[...].astype(bf16), slots_of(d, my_slots))[:8]

    for ref, first in ((own_e, 0), (own_h, 3)):
        ref[...] = jnp.zeros(ref.shape, f32)
        for c in range(3):
            ref[c * PADC : c * PADC + 20, :] = fields[first + c]
    halo_out[0, 0] = own_e[:, count - 128 :]
    halo_out[0, 1] = own_e[:, :128]

    pl.semaphore_wait(barrier, n_dom + 3)
    masks = exchange(mask_out, mask_in, mask_send, mask_recv)
    sent_codes = to_neighbours(code_out, code_in, code_send, code_recv)
    halo_e = to_neighbours(halo_out.at[0], halo_in.at[0], halo_send.at[0], halo_recv.at[0])

    for i in later_loads:
        loads[i].wait()

    sel[...] = sel_full[...].astype(bf16)
    pack[...] = pack_full[...].astype(bf16)

    stat[...] = jnp.zeros(stat.shape, f32)
    stat[GEO : GEO + 9, :] = geometry[...]
    for c in range(3):
        stat[NS + 4 * c : NS + 4 * c + 4, :] = normals[c] * face_scale[...]
    stat[CODE : CODE + 4, :] = face_nbr[...].astype(f32)
    pool[: 2 * FR, :count] = split2(own_e[...])
    pool[2 * FR : 4 * FR, :count] = split2(own_h[...])
    pool[4 * FR :, :count] = split2(stat[...])

    rows = send_rows[...]
    send_hot[...] = one_hot(count, rows)
    picked = dot(pool[:, :count], send_hot[...])
    slot_stat = picked[4 * FR : 4 * FR + 32] + picked[4 * FR + 32 :]
    picked = picked[: 4 * FR].astype(bf16)
    message = jnp.concatenate([dot(pack[...], picked)[:120], slot_stat[:8]], axis=0)
    hand_out[0] = message.T.reshape(n_dom, cap, RK)
    handed_fields = exchange(hand_out.at[0], hand_in.at[0], hand_send.at[0], hand_recv.at[0])
    slot_row = lax.broadcasted_iota(jnp.int32, (1, slots), 1)
    extra = split2(slot_stat[16:24])

    @pl.loop(0, n_dom)
    def _(d):
        part = dot_t(extra, slots_of(d, slot_row))
        extra_out[d] = part[:8] + part[8:]

    extras = exchange(extra_out, extra_in, extra_send, extra_recv)

    rows_hi = rows_lo = None
    for a in range(3):
        hi, lo = split(derivatives[a])
        hi = dot(d_rows[a], hi.astype(bf16))
        lo = dot(d_rows[a], lo.astype(bf16))
        rows_hi = hi if a == 0 else rows_hi + hi
        rows_lo = lo if a == 0 else rows_lo + lo
    wide = dot(rows_hi.astype(bf16), d_hi[...]) + dot(rows_lo.astype(bf16), d_lo[...])
    dmat[...] = (wide * d_mask[...]).astype(bf16)
    hi, lo = split(lift_matrix[...])
    hi = dot(l_rows[...], hi.astype(bf16))
    lo = dot(l_rows[...], lo.astype(bf16))
    wide = dot(hi.astype(bf16), l_hi[...]) + dot(lo.astype(bf16), l_lo[...])
    lmat[...] = (wide * l_mask[...]).astype(bf16)

    traces_e = dot(sel[...], picked[: 2 * FR])
    traces_h = dot(sel[...], picked[2 * FR :])
    held_e, held_h = [], []
    for f in range(4):
        code = slot_stat[CODE + f : CODE + f + 1].astype(jnp.int32)
        face = code & 3
        wall = code == 4 * rows + f
        near = dot(pool[: 4 * FR, :count], one_hot(count, code >> 2)).astype(bf16)
        e = pick_face(dot(sel[...], near[: 2 * FR]), face)
        h = pick_face(dot(sel[...], near[2 * FR :]), face)
        at = f * 3 * FN
        held_e.append(jnp.where(wall, -traces_e[at : at + 3 * FN], e))
        held_h.append(jnp.where(wall, traces_h[at : at + 3 * FN], h))
    finish(masks)

    def add_mask(d, mask):
        part = jnp.concatenate([mask_in[d], jnp.zeros((8, 128), f32)], axis=0).astype(bf16)
        return mask + dot(part, slots_of(d, slot_row))

    mask = lax.fori_loop(0, n_dom, add_mask, jnp.zeros((16, slots), f32))
    kept_e, kept_h = [], []
    for f in range(4):
        keep = mask[f : f + 1] > 0.5
        kept_e += flux(jnp.where(keep, held_e[f], 0.0), slot_stat[NS : NS + 12], f)
        kept_h += flux(jnp.where(keep, held_h[f], 0.0), slot_stat[NS : NS + 12], f)
    kept_e = dot(lmat[...], split3(jnp.concatenate(kept_e, axis=0)))
    kept_h = dot(lmat[...], split3(jnp.concatenate(kept_h, axis=0)))
    kept = jnp.concatenate([split2(kept_e), split2(kept_h)], axis=0)
    message = jnp.concatenate([dot(pack[...], kept)[:120], slot_stat[8:16]], axis=0)
    hand_out[1] = message.T.reshape(n_dom, cap, RK)
    handed_kept = exchange(hand_out.at[1], hand_in.at[1], hand_send.at[1], hand_recv.at[1])

    around_up = [dot_t(export_up, fine_own[:, f * fine : (f + 1) * fine]) for f in range(4)]
    around_down = [dot_t(export_down, fine_own[:, f * fine : (f + 1) * fine]) for f in range(4)]
    around = jnp.concatenate(
        [*around_up, export_up.astype(f32), *around_down, export_down.astype(f32)], axis=0
    ).astype(bf16)
    export_at = export_hot.astype(f32).T.astype(bf16)
    pad_eye = one_hot(2 * width, lax.broadcasted_iota(jnp.int32, (1, fine), 1))
    for copy in sent_codes:
        copy.wait()
    came_codes = dot(split2(code_in[...].reshape(2 * width, 128).T), pad_eye)
    came_codes = (came_codes[:128] + came_codes[128:])[4:8].astype(jnp.int32)
    ext = lax.broadcasted_iota(jnp.int32, (1, fine), 1)
    below = ext < width
    real = ext < 2 * width
    low_end = 4 * fine + 4 * width
    reach = 5 * width
    codes_all = []
    for f in range(4):
        code = codes[f]
        low, high = (code - 4 * fine) >> 2, (code - low_end) >> 2
        at = jnp.where(code < low_end, 4 * width + low, reach + 4 * width + high)
        at = jnp.where((code < 4 * fine) | (code >= frozen_code), -1, at)
        code_x = came_codes[f : f + 1]
        low, high = (code_x - 4 * fine) >> 2, (code_x - low_end) >> 2
        is_near = code_x < 4 * fine
        is_low = (code_x >= 4 * fine) & (code_x < low_end)
        is_high = (code_x >= low_end) & (code_x < frozen_code)
        at_x = jnp.where(below, f * width + ext, reach + f * width + ext - width)
        at_x = jnp.where(is_near, at_x, -1)
        at_x = jnp.where(is_low & below, 2 * reach + low, at_x)
        at_x = jnp.where(is_high & (ext >= width), 2 * reach + width + high, at_x)
        at_x = jnp.where(real, at_x, -1)
        mine = jnp.where(is_low & (ext >= width), low, jnp.where(is_high & below, width + high, -1))
        mine = jnp.where(real, mine, -1)
        block = slice(2 * f * fine, (2 * f + 1) * fine)
        block_x = slice((2 * f + 1) * fine, (2 * f + 2) * fine)
        tile_own[:, block] = fine_own[:, f * fine : (f + 1) * fine]
        tile_own[:, block_x] = dot(export_at, one_hot(2 * width, mine)).astype(bf16)
        tile_halo[:, block] = one_hot(12 * width, at)
        tile_halo[:, block_x] = one_hot(12 * width, at_x)
        codes_all.append(jnp.concatenate([code, code_x], axis=1))
    at = jnp.where(below, 4 * width + ext, reach + 4 * width + ext - width)
    ext_hot = one_hot(12 * width, jnp.where(real, at, -1))
    fine_halo[...] = one_hot(fine, code_row - fine)
    fine_out[...] = jnp.zeros(fine_out.shape, f32)
    first_out[...] = jnp.zeros(first_out.shape, f32)
    slot_hot = one_hot(slots, my_slots)

    @pl.loop(0, count // CHUNK)
    def _(i):
        start = pl.multiple_of(i * CHUNK, CHUNK)
        for f in range(4):
            code = face_nbr[f : f + 1, pl.ds(start, CHUNK)]
            coarse_hot[f, :, pl.ds(start, CHUNK)] = one_hot(full, code >> 2)

    def take(message):
        got = dot(split2(message.reshape(slots, RK).T), slot_hot)
        state = dot(unpack[...], got.astype(bf16))
        return state[:FR], state[FR:], got[120:RK] + got[RK + 120 :]

    finish(handed_fields)
    efield, hfield, stat_a = take(hand_in[0])
    finish(extras)

    def add_extra(d, value):
        return value + dot(split2(extra_in[d]), slots_of(d, my_slots))

    stat_c = lax.fori_loop(0, n_dom, add_extra, jnp.zeros((16, fine), f32))
    stat_c = stat_c[:8] + stat_c[8:]
    finish(handed_kept)
    kept_e, kept_h, stat_b = take(hand_in[1])
    fine_stat = jnp.concatenate([stat_a, stat_b, stat_c], axis=0)

    def send_electric(parts, turn):
        tile = dot_t(around, parts[:FR]) + dot_t(around, parts[FR:])
        fine_out[turn, :, :FR] = tile
        copies = []
        plan = (
            (after_id, 0, reach, 0),
            (before_id, reach, reach, reach),
            (after2_id, 4 * width, width, 2 * reach),
            (before2_id, reach + 4 * width, width, 2 * reach + width),
        )
        for side, (target, first, size, at) in enumerate(plan):
            copy = pltpu.make_async_remote_copy(
                src_ref=fine_out.at[turn, first : first + size],
                dst_ref=fine_in.at[turn, at : at + size],
                send_sem=fine_send.at[turn, side],
                recv_sem=fine_recv.at[turn, side],
                device_id=target,
                device_id_type=MESH,
            )
            copy.start()
            copies.append(copy)
        return copies

    def fluxes_of(near, own, face_codes, ns, size):
        traces = dot(sel[...], near.astype(bf16))
        fluxes = []
        for f in range(4):
            at = f * 3 * FN
            outside = pick_face(traces[:, f * size : (f + 1) * size], face_codes[f] & 3)
            fluxes += flux(outside - own[at : at + 3 * FN], ns, f)
        return dot(lmat[...], split3(jnp.concatenate(fluxes, axis=0)))

    fine_step = coarse_step / SUBSTEPS
    fine_geo, fine_ns = fine_stat[GEO : GEO + 9], fine_stat[NS : NS + 12]
    for substep in range(SUBSTEPS):
        parts = split2(efield)
        copies = send_electric(parts, substep)
        if substep == 0:
            start = jnp.concatenate([hfield, kept_e, fine_stat], axis=0)
            hi, lo = split(start)
            tile = dot_t(export_hot, hi.astype(bf16)) + dot_t(export_hot, lo.astype(bf16))
            first_out[0, :, : tile.shape[1]] = tile[:width]
            first_out[1, :, : tile.shape[1]] = tile[width:]
            first_copies = to_neighbours(first_out, first_in, first_send, first_recv)
        near = dot(parts, tile_own[...])
        own = dot(sel[...], parts)
        spin = curl(dot(dmat[...], split3(efield)), fine_geo)
        if substep == 0:
            for copy in first_copies:
                copy.wait()
            came = dot(split2(first_in[...].reshape(2 * width, 256).T), pad_eye)
            came = came[:256] + came[256:]
            hfield = jnp.concatenate([hfield, came[:FR]], axis=1)
            kept_all = jnp.concatenate([kept_e, came[FR : 2 * FR]], axis=1)
            stat_x = came[2 * FR : 2 * FR + 24]
            geo_x = stat_x[GEO : GEO + 9]
            ns_all = jnp.concatenate([fine_stat, stat_x], axis=1)[NS : NS + 12]
        for copy in copies:
            copy.wait()
        halo = split2(fine_in[substep].T[:FR])
        near = near + dot(halo, tile_halo[...])
        parts_x = dot(halo, ext_hot)
        field_x = parts_x[:FR] + parts_x[FR:]
        own = jnp.concatenate([own, dot(sel[...], parts_x.astype(bf16))], axis=1)
        spin_x = curl(dot(dmat[...], split3(field_x)), geo_x)
        spin = jnp.concatenate([spin, spin_x], axis=1) + kept_all
        rate = spin + fluxes_of(near, own, codes_all, ns_all, 2 * fine)
        hfield = hfield - fine_step * rate

        field = hfield[:, :fine]
        parts = split2(field)
        near = dot(parts, fine_own[...]) + dot(split2(hfield[:, fine:]), fine_halo[...])
        own = dot(sel[...], parts)
        spin = curl(dot(dmat[...], split3(field)), fine_geo) + kept_h
        efield = efield + fine_step * (spin + fluxes_of(near, own, codes, fine_ns, fine))
    hfield = hfield[:, :fine]

    result = jnp.concatenate([split2(efield), split2(hfield)], axis=0)
    result = split2(dot(pack[...], result))
    result = dot_t(slot_hot, result)
    result = result[:, :RK] + result[:, RK:]
    back_out[...] = result.reshape(n_dom, cap, RK)
    returned = exchange(back_out, back_in, back_send, back_recv)
    is_fine = dot_t(jnp.ones((16, slots), bf16), send_hot[...])[:1] > 0.5
    finish(returned)
    came = back_in[...].reshape(slots, RK).T
    came = dot_t(split2(came), send_hot[...]).astype(bf16)
    came = dot(unpack[...], came)
    merged_e = jnp.where(is_fine, came[:FR], own_e[...])
    merged_h = jnp.where(is_fine, came[FR:], own_h[...])
    own_e[...] = merged_e
    own_h[...] = merged_h
    pool_e, pool_h = pool.at[: 2 * FR], pool.at[2 * FR : 4 * FR]
    pool_e[:, :count] = split2(merged_e)

    halo_lane = lax.broadcasted_iota(jnp.int32, (FR, 128), 1)
    place = lax.broadcasted_iota(jnp.int32, (1, CHUNK), 1)

    def coarse_rate(start, source, pool, reach, mirror):
        window = pl.ds(start, CHUNK)
        field = source[:, window]
        table = stat[:, window]
        spin = curl(dot(dmat[...], split3(field)), table[GEO : GEO + 9])
        own = dot(sel[...], split2(field))
        ns = table[NS : NS + 12]
        fluxes = []
        for f in range(4):
            code = face_nbr[f : f + 1, window]
            near = dot(pool[:, :reach], coarse_hot[f, :reach, window]).astype(bf16)
            outside = pick_face(dot(sel[...], near), code & 3)
            mine = own[f * 3 * FN : (f + 1) * 3 * FN]
            wall = code == 4 * (start + place) + f
            outside = jnp.where(wall, mirror * mine, outside)
            fluxes += flux(outside - mine, ns, f)
        return spin + dot(lmat[...], split3(jnp.concatenate(fluxes, axis=0)))

    def set_halo(pool, turn, copies):
        for copy in copies:
            copy.wait()
        tile = jnp.where(halo_lane < 64, halo_in[turn, 1], halo_in[turn, 0])
        pool[:, count:] = split2(pltpu.roll(tile, 64, 1))

    def update(start, source, pool, target, first, scale, reach, mirror):
        start = pl.multiple_of(start, CHUNK)
        window = pl.ds(start, CHUNK)
        new = target[:, window] + scale * coarse_rate(start, source, pool, reach, mirror)
        target[:, window] = new
        for c in range(3):
            out[first + c, :, window] = new[c * PADC : c * PADC + 20]
        if first == 3:
            pool_h[:, window] = split2(new)

    last = count - CHUNK
    set_halo(pool_e, 0, halo_e)

    @pl.loop(0, 2)
    def _(i):
        update(i * last, own_e, pool_e, own_h, 3, -coarse_step, full, -1.0)

    halo_out[1, 0] = own_h[:, count - 128 :]
    halo_out[1, 1] = own_h[:, :128]
    halo_h = to_neighbours(halo_out.at[1], halo_in.at[1], halo_send.at[1], halo_recv.at[1])

    @pl.loop(1, count // CHUNK - 1)
    def _(i):
        update(i * CHUNK, own_e, pool_e, own_h, 3, -coarse_step, count, -1.0)

    @pl.loop(1, count // CHUNK - 1)
    def _(i):
        update(i * CHUNK, own_h, pool_h, own_e, 0, coarse_step, count, 1.0)

    set_halo(pool_h, 1, halo_h)

    @pl.loop(0, 2)
    def _(i):
        update(i * last, own_h, pool_h, own_e, 0, coarse_step, full, 1.0)


def per_device(
    n_dom,
    n_sub,
    fields,
    geometry,
    normals,
    face_scale,
    derivatives,
    lift_matrix,
    face_nbr,
    send_rows,
    fine_slots,
    export_rows,
    fine_nbr,
):
    count = fields.shape[2]
    fine = fine_slots.shape[0]
    width = export_rows.shape[1]
    group = send_rows.shape[0] // n_dom
    cap = -(-group // 8) * 8
    slots = n_dom * cap
    if cap != group:
        send_rows = jnp.pad(
            send_rows.reshape(n_dom, group),
            ((0, 0), (0, cap - group)),
            constant_values=count,
        ).reshape(-1)
        fine_slots = fine_slots // group * cap + fine_slots % group
    operands = [
        fields,
        geometry,
        normals,
        face_scale,
        derivatives,
        lift_matrix,
        face_nbr,
        send_rows[None],
        fine_slots[None],
        export_rows,
        fine_nbr,
        *[jnp.asarray(x) for x in tables()],
    ]
    vmem = pl.BlockSpec(memory_space=pltpu.VMEM)
    dma = pltpu.SemaphoreType.DMA
    return pl.pallas_call(
        functools.partial(kernel, n_dom, n_sub, width),
        out_shape=jax.ShapeDtypeStruct(fields.shape, f32),
        in_specs=[pl.BlockSpec(memory_space=pl.ANY)] * len(operands),
        out_specs=vmem,
        scratch_shapes=[
            *[pltpu.VMEM(x.shape, x.dtype) for x in operands],
            dma((len(operands),)),
            pltpu.VMEM((FR, count), f32),
            pltpu.VMEM((FR, count), f32),
            pltpu.VMEM((4 * FR + 64, count + 128), bf16),
            pltpu.VMEM((32, count), f32),
            pltpu.VMEM((16, fine), f32),
            pltpu.VMEM((TR, 2 * FR), bf16),
            pltpu.VMEM((RK, 4 * FR), bf16),
            pltpu.VMEM((count, slots), bf16),
            pltpu.VMEM((4, count + 128, count), bf16),
            pltpu.VMEM((fine, 4 * fine), bf16),
            pltpu.VMEM((fine, 4 * fine), bf16),
            pltpu.VMEM((fine, 8 * fine), bf16),
            pltpu.VMEM((12 * width, 8 * fine), bf16),
            pltpu.VMEM((224, 3 * FR), bf16),
            pltpu.VMEM((FR, 3 * TR), bf16),
            pltpu.VMEM((n_dom, 8, 128), f32),
            pltpu.VMEM((n_dom, 8, 128), f32),
            pltpu.VMEM((n_dom, 8, 128), f32),
            pltpu.VMEM((n_dom, 8, 128), f32),
            pltpu.VMEM((2, n_dom, cap, RK), f32),
            pltpu.VMEM((2, n_dom, cap, RK), f32),
            pltpu.VMEM((n_dom, cap, RK), f32),
            pltpu.VMEM((n_dom, cap, RK), f32),
            pltpu.VMEM((2, width, 128), f32),
            pltpu.VMEM((2, width, 128), f32),
            pltpu.VMEM((2, width, 256), f32),
            pltpu.VMEM((2, width, 256), f32),
            pltpu.VMEM((SUBSTEPS, 10 * width, 128), f32),
            pltpu.VMEM((SUBSTEPS, 12 * width, 128), f32),
            pltpu.VMEM((2, 2, FR, 128), f32),
            pltpu.VMEM((2, 2, FR, 128), f32),
            dma((n_dom,)),
            dma((n_dom,)),
            dma((n_dom,)),
            dma((n_dom,)),
            dma((2, n_dom)),
            dma((2, n_dom)),
            dma((n_dom,)),
            dma((n_dom,)),
            dma((2,)),
            dma((2,)),
            dma((2,)),
            dma((2,)),
            dma((SUBSTEPS, 4)),
            dma((SUBSTEPS, 4)),
            dma((2, 2)),
            dma((2, 2)),
        ],
        compiler_params=pltpu.CompilerParams(
            collective_id=0, has_side_effects=True, vmem_limit_bytes=56 * 1024 * 1024
        ),
    )(*operands)


def solution(mesh):
    return jax.shard_map(
        functools.partial(per_device, mesh.shape["dom"], mesh.shape["sub"]),
        mesh=mesh,
        in_specs=(
            P(None, None, ("dom", "sub")),
            P(None, ("dom", "sub")),
            P(None, None, ("dom", "sub")),
            P(None, ("dom", "sub")),
            P(),
            P(),
            P(None, ("dom", "sub")),
            P(("dom", "sub")),
            P(("dom", "sub")),
            P(None, ("dom", "sub")),
            P(None, ("dom", "sub")),
        ),
        out_specs=P(None, None, ("dom", "sub")),
        check_vma=False,
    )
```

```python
import functools

import jax
import jax.numpy as jnp
import numpy as np
from jax import lax
from jax.experimental import pallas as pl
from jax.experimental.pallas import tpu as pltpu
from jax.sharding import PartitionSpec as P

SUBSTEPS = 4
coarse_step = 0.2

PADC = 24
FR = 80
FN = 16
TR = 192
RK = 128
GEO, NS, CODE = 0, 9, 24
CHUNK = 256

bf16 = jnp.bfloat16
f32 = jnp.float32
MESH = pl.DeviceIdType.MESH


def face_table():
    places = [
        (along_r, along_s, along_t)
        for along_t in range(4)
        for along_s in range(4 - along_t)
        for along_r in range(4 - along_t - along_s)
    ]
    bottom_face = [number for number, location in enumerate(places) if location[2] == 0]
    front_face = [number for number, location in enumerate(places) if location[1] == 0]
    slanted = [number for number, location in enumerate(places) if sum(location) == 3]
    beside = [number for number, location in enumerate(places) if location[0] == 0]
    return np.array([bottom_face, front_face, slanted, beside], dtype=np.int32).T


def tables():
    nodes = face_table()
    sel = np.zeros((TR, 2 * FR), np.float32)
    pack = np.zeros((RK, 4 * FR), np.float32)
    unpack = np.zeros((2 * FR, 2 * RK), np.float32)
    for c in range(3):
        for p in range(20):
            for field in range(2):
                packed = (field * 3 + c) * 20 + p
                for s in range(2):
                    pack[packed, field * 2 * FR + s * FR + c * PADC + p] = 1
                    unpack[field * FR + c * PADC + p, s * RK + packed] = 1
        for f in range(4):
            for n in range(10):
                for s in range(2):
                    sel[f * 3 * FN + c * FN + n, s * FR + c * PADC + nodes[n, f]] = 1
    d_rows = np.zeros((3, 224, 20), np.float32)
    d_hi = np.zeros((20, 3 * FR), np.float32)
    d_lo = np.zeros((20, 3 * FR), np.float32)
    d_mask = np.zeros((224, 3 * FR), np.float32)
    l_rows = np.zeros((FR, 20), np.float32)
    l_hi = np.zeros((40, 3 * TR), np.float32)
    l_lo = np.zeros((40, 3 * TR), np.float32)
    l_mask = np.zeros((FR, 3 * TR), np.float32)
    for c in range(3):
        for p in range(20):
            l_rows[c * PADC + p, p] = 1
            for a in range(3):
                d_rows[a, (a * 3 + c) * PADC + p, p] = 1
            d_hi[p, c * PADC + p] = 1
            d_hi[p, FR + c * PADC + p] = 1
            d_lo[p, 2 * FR + c * PADC + p] = 1
        for s in range(3):
            for a in range(3):
                at = (a * 3 + c) * PADC
                d_mask[at : at + 20, s * FR + c * PADC : s * FR + c * PADC + 20] = 1
            for f in range(4):
                col = s * TR + f * 3 * FN + c * FN
                l_mask[c * PADC : c * PADC + 20, col : col + 10] = 0.5
                for n in range(10):
                    (l_lo if s == 2 else l_hi)[f * 10 + n, col + n] = 1
    out = [unpack, d_rows, d_hi, d_lo, l_rows, l_hi, l_lo]
    return [sel, pack] + [x.astype(jnp.bfloat16) for x in out] + [d_mask, l_mask]


def split(x):
    hi = x.astype(bf16).astype(f32)
    return hi, x - hi


def split2(x):
    hi, lo = split(x)
    return jnp.concatenate([hi, lo], axis=0).astype(bf16)


def split3(x):
    hi, lo = split(x)
    return jnp.concatenate([hi, lo, hi], axis=0).astype(bf16)


def dot(a, b):
    return jnp.dot(a, b, preferred_element_type=f32)


def dot_t(a, b):
    return lax.dot_general(a, b, (((1,), (1,)), ((), ())), preferred_element_type=f32)


def one_hot(count, row):
    at = lax.broadcasted_iota(jnp.int32, (count, row.shape[1]), 0)
    return jnp.where(at == row, 1.0, 0.0).astype(bf16)


def curl(grad, geo):
    def partial(m, c):
        total = None
        for a in range(3):
            at = (a * 3 + c) * PADC
            term = geo[3 * m + a : 3 * m + a + 1] * grad[at : at + PADC]
            total = term if total is None else total + term
        return total

    parts = [
        partial(1, 2) - partial(2, 1),
        partial(2, 0) - partial(0, 2),
        partial(0, 1) - partial(1, 0),
    ]
    pad = jnp.zeros((FR - 3 * PADC, grad.shape[1]), f32)
    return jnp.concatenate([*parts, pad], axis=0)


def pick_face(traces, face):
    total = traces[: 3 * FN]
    for g in range(1, 4):
        total = jnp.where(face == g, traces[g * 3 * FN : (g + 1) * 3 * FN], total)
    return total


def flux(jump, ns, f):
    n = [ns[c * 4 + f : c * 4 + f + 1] for c in range(3)]
    j = [jump[c * FN : (c + 1) * FN] for c in range(3)]
    return [
        n[1] * j[2] - n[2] * j[1],
        n[2] * j[0] - n[0] * j[2],
        n[0] * j[1] - n[1] * j[0],
    ]


OPERANDS = 22


def kernel(n_dom, n_sub, width, *refs):
    given, out = refs[:OPERANDS], refs[OPERANDS]
    local, load_sem = refs[OPERANDS + 1 : 2 * OPERANDS + 1], refs[2 * OPERANDS + 1]
    (
        fields,
        geometry,
        normals,
        face_scale,
        derivatives,
        lift_matrix,
        face_nbr,
        send_rows,
        fine_slots,
        export_rows,
        fine_nbr,
        sel_full,
        pack_full,
        unpack,
        d_rows,
        d_hi,
        d_lo,
        l_rows,
        l_hi,
        l_lo,
        d_mask,
        l_mask,
    ) = local
    (
    own_e,
    own_h,
    pool,
    stat,
    frozen,
    sel,
    pack,
    send_hot,
    coarse_hot,
    fine_own,
    fine_halo,
    tile_own,
    tile_halo,
    dmat,
    lmat,
    mask_out,
    mask_in,
    extra_out,
    extra_in,
    hand_out,
    hand_in,
    back_out,
    back_in,
    code_out,
    code_in,
    first_out,
    first_in,
    fine_out,
    fine_in,
    halo_out,
    halo_in,
    mask_send,
    mask_recv,
    extra_send,
    extra_recv,
    hand_send,
    hand_recv,
    back_send,
    back_recv,
    code_send,
    code_recv,
    first_send,
    first_recv,
    fine_send,
    fine_recv,
    halo_send,
    halo_recv,
    ) = refs[2 * OPERANDS + 2 :]
    count = fields.shape[2]
    fine = fine_slots.shape[1]
    cap = hand_out.shape[2]
    slots = n_dom * cap
    full = count + 128
    dom, sub = lax.axis_index("dom"), lax.axis_index("sub")
    me = dom * n_sub + sub
    total = n_dom * n_sub
    after, before = lax.rem(me + 1, total), lax.rem(me + total - 1, total)
    after_id = (after // n_sub, lax.rem(after, n_sub))
    before_id = (before // n_sub, lax.rem(before, n_sub))
    after2, before2 = lax.rem(me + 2, total), lax.rem(me + total - 2, total)
    after2_id = (after2 // n_sub, lax.rem(after2, n_sub))
    before2_id = (before2 // n_sub, lax.rem(before2, n_sub))

    loads = [
        pltpu.make_async_copy(src, dst, load_sem.at[i])
        for i, (src, dst) in enumerate(zip(given, local))
    ]
    first_loads = [10, 8, 9, 0]
    later_loads = [i for i in range(OPERANDS) if i not in first_loads]
    for i in first_loads + later_loads:
        loads[i].start()

    barrier = pltpu.get_barrier_semaphore()
    for target in (after_id, before_id, after2_id, before2_id):
        pl.semaphore_signal(barrier, inc=1, device_id=target, device_id_type=MESH)

    @pl.loop(1, n_dom)
    def _(i):
        pl.semaphore_signal(
            barrier, inc=1, device_id=(lax.rem(dom + i, n_dom), sub), device_id_type=MESH
        )

    def exchange(src, dst, send, recv):
        def copy(i):
            target = lax.rem(dom + i, n_dom)
            return pltpu.make_async_remote_copy(
                src_ref=src.at[target],
                dst_ref=dst.at[dom],
                send_sem=send.at[i],
                recv_sem=recv.at[i],
                device_id=(target, sub),
                device_id_type=MESH,
            )

        @pl.loop(1, n_dom)
        def _(i):
            copy(i).start()

        dst[pl.ds(dom, 1)] = src[pl.ds(dom, 1)]
        return copy

    def finish(copy):
        @pl.loop(1, n_dom)
        def _(i):
            copy(i).wait()

    def to_neighbours(src, dst, send, recv):
        copies = []
        for side, target in enumerate((after_id, before_id)):
            copy = pltpu.make_async_remote_copy(
                src_ref=src.at[side],
                dst_ref=dst.at[side],
                send_sem=send.at[side],
                recv_sem=recv.at[side],
                device_id=target,
                device_id_type=MESH,
            )
            copy.start()
            copies.append(copy)
        return copies

    def slots_of(d, row):
        at = lax.broadcasted_iota(jnp.int32, (128, row.shape[1]), 0)
        return jnp.where((row - d * cap == at) & (at < cap), 1.0, 0.0).astype(bf16)

    for i in first_loads:
        loads[i].wait()

    codes = [fine_nbr[f : f + 1, :] for f in range(4)]
    frozen_code = 4 * fine + 8 * width
    frozen[...] = jnp.zeros(frozen.shape, f32)
    frozen[0:4, :] = jnp.where(fine_nbr[...] == frozen_code, 1.0, 0.0)
    frozen[4:8, :] = fine_nbr[...].astype(f32)
    my_slots = fine_slots[...]

    eye = one_hot(width, lax.broadcasted_iota(jnp.int32, (1, width), 1))
    export_up = dot_t(eye, one_hot(fine, export_rows[1:2, :])).astype(bf16)
    export_down = dot_t(eye, one_hot(fine, export_rows[0:1, :])).astype(bf16)
    export_hot = jnp.concatenate([export_up, export_down], axis=0)
    code_row = jnp.concatenate(codes, axis=1) >> 2
    fine_own[...] = one_hot(fine, code_row)
    hi, lo = split(frozen[...])
    exported = dot_t(export_hot, hi.astype(bf16)) + dot_t(export_hot, lo.astype(bf16))
    code_out[...] = jnp.zeros(code_out.shape, f32)
    code_out[0, :, :16] = exported[:width]
    code_out[1, :, :16] = exported[width:]

    @pl.loop(0, n_dom)
    def _(d):
        mask_out[d] = dot_t(frozen[...].astype(bf16), slots_of(d, my_slots))[:8]

    for ref, first in ((own_e, 0), (own_h, 3)):
        ref[...] = jnp.zeros(ref.shape, f32)
        for c in range(3):
            ref[c * PADC : c * PADC + 20, :] = fields[first + c]
    halo_out[0, 0] = own_e[:, count - 128 :]
    halo_out[0, 1] = own_e[:, :128]

    pl.semaphore_wait(barrier, n_dom + 3)
    masks = exchange(mask_out, mask_in, mask_send, mask_recv)
    sent_codes = to_neighbours(code_out, code_in, code_send, code_recv)
    halo_e = to_neighbours(halo_out.at[0], halo_in.at[0], halo_send.at[0], halo_recv.at[0])

    for i in later_loads:
        loads[i].wait()

    sel[...] = sel_full[...].astype(bf16)
    pack[...] = pack_full[...].astype(bf16)

    stat[...] = jnp.zeros(stat.shape, f32)
    stat[GEO : GEO + 9, :] = geometry[...]
    for c in range(3):
        stat[NS + 4 * c : NS + 4 * c + 4, :] = normals[c] * face_scale[...]
    stat[CODE : CODE + 4, :] = face_nbr[...].astype(f32)
    pool[: 2 * FR, :count] = split2(own_e[...])
    pool[2 * FR : 4 * FR, :count] = split2(own_h[...])
    pool[4 * FR :, :count] = split2(stat[...])

    rows = send_rows[...]
    send_hot[...] = one_hot(count, rows)
    picked = dot(pool[:, :count], send_hot[...])
    slot_stat = picked[4 * FR : 4 * FR + 32] + picked[4 * FR + 32 :]
    picked = picked[: 4 * FR].astype(bf16)
    message = jnp.concatenate([dot(pack[...], picked)[:120], slot_stat[:8]], axis=0)
    hand_out[0] = message.T.reshape(n_dom, cap, RK)
    handed_fields = exchange(hand_out.at[0], hand_in.at[0], hand_send.at[0], hand_recv.at[0])
    slot_row = lax.broadcasted_iota(jnp.int32, (1, slots), 1)
    extra = split2(slot_stat[16:24])

    @pl.loop(0, n_dom)
    def _(d):
        part = dot_t(extra, slots_of(d, slot_row))
        extra_out[d] = part[:8] + part[8:]

    extras = exchange(extra_out, extra_in, extra_send, extra_recv)

    rows_hi = rows_lo = None
    for a in range(3):
        hi, lo = split(derivatives[a])
        hi = dot(d_rows[a], hi.astype(bf16))
        lo = dot(d_rows[a], lo.astype(bf16))
        rows_hi = hi if a == 0 else rows_hi + hi
        rows_lo = lo if a == 0 else rows_lo + lo
    wide = dot(rows_hi.astype(bf16), d_hi[...]) + dot(rows_lo.astype(bf16), d_lo[...])
    dmat[...] = (wide * d_mask[...]).astype(bf16)
    hi, lo = split(lift_matrix[...])
    hi = dot(l_rows[...], hi.astype(bf16))
    lo = dot(l_rows[...], lo.astype(bf16))
    wide = dot(hi.astype(bf16), l_hi[...]) + dot(lo.astype(bf16), l_lo[...])
    lmat[...] = (wide * l_mask[...]).astype(bf16)

    traces_e = dot(sel[...], picked[: 2 * FR])
    traces_h = dot(sel[...], picked[2 * FR :])
    held_e, held_h = [], []
    for f in range(4):
        code = slot_stat[CODE + f : CODE + f + 1].astype(jnp.int32)
        face = code & 3
        wall = code == 4 * rows + f
        near = dot(pool[: 4 * FR, :count], one_hot(count, code >> 2)).astype(bf16)
        e = pick_face(dot(sel[...], near[: 2 * FR]), face)
        h = pick_face(dot(sel[...], near[2 * FR :]), face)
        at = f * 3 * FN
        held_e.append(jnp.where(wall, -traces_e[at : at + 3 * FN], e))
        held_h.append(jnp.where(wall, traces_h[at : at + 3 * FN], h))
    finish(masks)

    def add_mask(d, mask):
        part = jnp.concatenate([mask_in[d], jnp.zeros((8, 128), f32)], axis=0).astype(bf16)
        return mask + dot(part, slots_of(d, slot_row))

    mask = lax.fori_loop(0, n_dom, add_mask, jnp.zeros((16, slots), f32))
    kept_e, kept_h = [], []
    for f in range(4):
        keep = mask[f : f + 1] > 0.5
        kept_e += flux(jnp.where(keep, held_e[f], 0.0), slot_stat[NS : NS + 12], f)
        kept_h += flux(jnp.where(keep, held_h[f], 0.0), slot_stat[NS : NS + 12], f)
    kept_e = dot(lmat[...], split3(jnp.concatenate(kept_e, axis=0)))
    kept_h = dot(lmat[...], split3(jnp.concatenate(kept_h, axis=0)))
    kept = jnp.concatenate([split2(kept_e), split2(kept_h)], axis=0)
    message = jnp.concatenate([dot(pack[...], kept)[:120], slot_stat[8:16]], axis=0)
    hand_out[1] = message.T.reshape(n_dom, cap, RK)
    handed_kept = exchange(hand_out.at[1], hand_in.at[1], hand_send.at[1], hand_recv.at[1])

    around_up = [dot_t(export_up, fine_own[:, f * fine : (f + 1) * fine]) for f in range(4)]
    around_down = [dot_t(export_down, fine_own[:, f * fine : (f + 1) * fine]) for f in range(4)]
    around = jnp.concatenate(
        [*around_up, export_up.astype(f32), *around_down, export_down.astype(f32)], axis=0
    ).astype(bf16)
    export_at = export_hot.astype(f32).T.astype(bf16)
    pad_eye = one_hot(2 * width, lax.broadcasted_iota(jnp.int32, (1, fine), 1))
    for copy in sent_codes:
        copy.wait()
    came_codes = dot(split2(code_in[...].reshape(2 * width, 128).T), pad_eye)
    came_codes = (came_codes[:128] + came_codes[128:])[4:8].astype(jnp.int32)
    ext = lax.broadcasted_iota(jnp.int32, (1, fine), 1)
    below = ext < width
    real = ext < 2 * width
    low_end = 4 * fine + 4 * width
    reach = 5 * width
    codes_all = []
    for f in range(4):
        code = codes[f]
        low, high = (code - 4 * fine) >> 2, (code - low_end) >> 2
        at = jnp.where(code < low_end, 4 * width + low, reach + 4 * width + high)
        at = jnp.where((code < 4 * fine) | (code >= frozen_code), -1, at)
        code_x = came_codes[f : f + 1]
        low, high = (code_x - 4 * fine) >> 2, (code_x - low_end) >> 2
        is_near = code_x < 4 * fine
        is_low = (code_x >= 4 * fine) & (code_x < low_end)
        is_high = (code_x >= low_end) & (code_x < frozen_code)
        at_x = jnp.where(below, f * width + ext, reach + f * width + ext - width)
        at_x = jnp.where(is_near, at_x, -1)
        at_x = jnp.where(is_low & below, 2 * reach + low, at_x)
        at_x = jnp.where(is_high & (ext >= width), 2 * reach + width + high, at_x)
        at_x = jnp.where(real, at_x, -1)
        mine = jnp.where(is_low & (ext >= width), low, jnp.where(is_high & below, width + high, -1))
        mine = jnp.where(real, mine, -1)
        block = slice(2 * f * fine, (2 * f + 1) * fine)
        block_x = slice((2 * f + 1) * fine, (2 * f + 2) * fine)
        tile_own[:, block] = fine_own[:, f * fine : (f + 1) * fine]
        tile_own[:, block_x] = dot(export_at, one_hot(2 * width, mine)).astype(bf16)
        tile_halo[:, block] = one_hot(12 * width, at)
        tile_halo[:, block_x] = one_hot(12 * width, at_x)
        codes_all.append(jnp.concatenate([code, code_x], axis=1))
    at = jnp.where(below, 4 * width + ext, reach + 4 * width + ext - width)
    ext_hot = one_hot(12 * width, jnp.where(real, at, -1))
    fine_halo[...] = one_hot(fine, code_row - fine)
    fine_out[...] = jnp.zeros(fine_out.shape, f32)
    first_out[...] = jnp.zeros(first_out.shape, f32)
    slot_hot = one_hot(slots, my_slots)

    @pl.loop(0, count // CHUNK)
    def _(i):
        start = pl.multiple_of(i * CHUNK, CHUNK)
        for f in range(4):
            code = face_nbr[f : f + 1, pl.ds(start, CHUNK)]
            coarse_hot[f, :, pl.ds(start, CHUNK)] = one_hot(full, code >> 2)

    def take(message):
        got = dot(split2(message.reshape(slots, RK).T), slot_hot)
        state = dot(unpack[...], got.astype(bf16))
        return state[:FR], state[FR:], got[120:RK] + got[RK + 120 :]

    finish(handed_fields)
    efield, hfield, stat_a = take(hand_in[0])
    finish(extras)

    def add_extra(d, value):
        return value + dot(split2(extra_in[d]), slots_of(d, my_slots))

    stat_c = lax.fori_loop(0, n_dom, add_extra, jnp.zeros((16, fine), f32))
    stat_c = stat_c[:8] + stat_c[8:]
    finish(handed_kept)
    kept_e, kept_h, stat_b = take(hand_in[1])
    fine_stat = jnp.concatenate([stat_a, stat_b, stat_c], axis=0)

    def send_electric(parts, turn):
        tile = dot_t(around, parts[:FR]) + dot_t(around, parts[FR:])
        fine_out[turn, :, :FR] = tile
        copies = []
        plan = (
            (after_id, 0, reach, 0),
            (before_id, reach, reach, reach),
            (after2_id, 4 * width, width, 2 * reach),
            (before2_id, reach + 4 * width, width, 2 * reach + width),
        )
        for side, (target, first, size, at) in enumerate(plan):
            copy = pltpu.make_async_remote_copy(
                src_ref=fine_out.at[turn, first : first + size],
                dst_ref=fine_in.at[turn, at : at + size],
                send_sem=fine_send.at[turn, side],
                recv_sem=fine_recv.at[turn, side],
                device_id=target,
                device_id_type=MESH,
            )
            copy.start()
            copies.append(copy)
        return copies

    def fluxes_of(near, own, face_codes, ns, size):
        traces = dot(sel[...], near.astype(bf16))
        fluxes = []
        for f in range(4):
            at = f * 3 * FN
            outside = pick_face(traces[:, f * size : (f + 1) * size], face_codes[f] & 3)
            fluxes += flux(outside - own[at : at + 3 * FN], ns, f)
        return dot(lmat[...], split3(jnp.concatenate(fluxes, axis=0)))

    fine_step = coarse_step / SUBSTEPS
    fine_geo, fine_ns = fine_stat[GEO : GEO + 9], fine_stat[NS : NS + 12]
    for substep in range(SUBSTEPS):
        parts = split2(efield)
        copies = send_electric(parts, substep)
        if substep == 0:
            start = jnp.concatenate([hfield, kept_e, fine_stat], axis=0)
            hi, lo = split(start)
            tile = dot_t(export_hot, hi.astype(bf16)) + dot_t(export_hot, lo.astype(bf16))
            first_out[0, :, : tile.shape[1]] = tile[:width]
            first_out[1, :, : tile.shape[1]] = tile[width:]
            first_copies = to_neighbours(first_out, first_in, first_send, first_recv)
        near = dot(parts, tile_own[...])
        own = dot(sel[...], parts)
        spin = curl(dot(dmat[...], split3(efield)), fine_geo)
        if substep == 0:
            for copy in first_copies:
                copy.wait()
            came = dot(split2(first_in[...].reshape(2 * width, 256).T), pad_eye)
            came = came[:256] + came[256:]
            hfield = jnp.concatenate([hfield, came[:FR]], axis=1)
            kept_all = jnp.concatenate([kept_e, came[FR : 2 * FR]], axis=1)
            stat_x = came[2 * FR : 2 * FR + 24]
            geo_x = stat_x[GEO : GEO + 9]
            ns_all = jnp.concatenate([fine_stat, stat_x], axis=1)[NS : NS + 12]
        for copy in copies:
            copy.wait()
        halo = split2(fine_in[substep].T[:FR])
        near = near + dot(halo, tile_halo[...])
        parts_x = dot(halo, ext_hot)
        field_x = parts_x[:FR] + parts_x[FR:]
        own = jnp.concatenate([own, dot(sel[...], parts_x.astype(bf16))], axis=1)
        spin_x = curl(dot(dmat[...], split3(field_x)), geo_x)
        spin = jnp.concatenate([spin, spin_x], axis=1) + kept_all
        rate = spin + fluxes_of(near, own, codes_all, ns_all, 2 * fine)
        hfield = hfield - fine_step * rate

        field = hfield[:, :fine]
        parts = split2(field)
        near = dot(parts, fine_own[...]) + dot(split2(hfield[:, fine:]), fine_halo[...])
        own = dot(sel[...], parts)
        spin = curl(dot(dmat[...], split3(field)), fine_geo) + kept_h
        efield = efield + fine_step * (spin + fluxes_of(near, own, codes, fine_ns, fine))
    hfield = hfield[:, :fine]

    result = jnp.concatenate([split2(efield), split2(hfield)], axis=0)
    result = split2(dot(pack[...], result))
    result = dot_t(slot_hot, result)
    result = result[:, :RK] + result[:, RK:]
    back_out[...] = result.reshape(n_dom, cap, RK)
    returned = exchange(back_out, back_in, back_send, back_recv)
    is_fine = dot_t(jnp.ones((16, slots), bf16), send_hot[...])[:1] > 0.5
    finish(returned)
    came = back_in[...].reshape(slots, RK).T
    came = dot_t(split2(came), send_hot[...]).astype(bf16)
    came = dot(unpack[...], came)
    merged_e = jnp.where(is_fine, came[:FR], own_e[...])
    merged_h = jnp.where(is_fine, came[FR:], own_h[...])
    own_e[...] = merged_e
    own_h[...] = merged_h
    pool_e, pool_h = pool.at[: 2 * FR], pool.at[2 * FR : 4 * FR]
    pool_e[:, :count] = split2(merged_e)

    halo_lane = lax.broadcasted_iota(jnp.int32, (FR, 128), 1)
    place = lax.broadcasted_iota(jnp.int32, (1, CHUNK), 1)

    def coarse_rate(start, source, pool, reach, mirror):
        window = pl.ds(start, CHUNK)
        field = source[:, window]
        table = stat[:, window]
        spin = curl(dot(dmat[...], split3(field)), table[GEO : GEO + 9])
        own = dot(sel[...], split2(field))
        ns = table[NS : NS + 12]
        fluxes = []
        for f in range(4):
            code = face_nbr[f : f + 1, window]
            near = dot(pool[:, :reach], coarse_hot[f, :reach, window]).astype(bf16)
            outside = pick_face(dot(sel[...], near), code & 3)
            mine = own[f * 3 * FN : (f + 1) * 3 * FN]
            wall = code == 4 * (start + place) + f
            outside = jnp.where(wall, mirror * mine, outside)
            fluxes += flux(outside - mine, ns, f)
        return spin + dot(lmat[...], split3(jnp.concatenate(fluxes, axis=0)))

    def set_halo(pool, turn, copies):
        for copy in copies:
            copy.wait()
        tile = jnp.where(halo_lane < 64, halo_in[turn, 1], halo_in[turn, 0])
        pool[:, count:] = split2(pltpu.roll(tile, 64, 1))

    def update(start, source, pool, target, first, scale, reach, mirror):
        window = pl.ds(start, CHUNK)
        new = target[:, window] + scale * coarse_rate(start, source, pool, reach, mirror)
        target[:, window] = new
        for c in range(3):
            out[first + c, :, window] = new[c * PADC : c * PADC + 20]
        if first == 3:
            pool_h[:, window] = split2(new)

    last = count - CHUNK
    set_halo(pool_e, 0, halo_e)

    for start in (0, last):
        update(start, own_e, pool_e, own_h, 3, -coarse_step, full, -1.0)

    halo_out[1, 0] = own_h[:, count - 128 :]
    halo_out[1, 1] = own_h[:, :128]
    halo_h = to_neighbours(halo_out.at[1], halo_in.at[1], halo_send.at[1], halo_recv.at[1])

    for start in range(CHUNK, last, CHUNK):
        update(start, own_e, pool_e, own_h, 3, -coarse_step, count, -1.0)
    for start in range(CHUNK, last, CHUNK):
        update(start, own_h, pool_h, own_e, 0, coarse_step, count, 1.0)

    set_halo(pool_h, 1, halo_h)

    for start in (0, last):
        update(start, own_h, pool_h, own_e, 0, coarse_step, full, 1.0)


def per_device(
    n_dom,
    n_sub,
    fields,
    geometry,
    normals,
    face_scale,
    derivatives,
    lift_matrix,
    face_nbr,
    send_rows,
    fine_slots,
    export_rows,
    fine_nbr,
):
    count = fields.shape[2]
    fine = fine_slots.shape[0]
    width = export_rows.shape[1]
    group = send_rows.shape[0] // n_dom
    cap = -(-group // 8) * 8
    slots = n_dom * cap
    if cap != group:
        send_rows = jnp.pad(
            send_rows.reshape(n_dom, group),
            ((0, 0), (0, cap - group)),
            constant_values=count,
        ).reshape(-1)
        fine_slots = fine_slots // group * cap + fine_slots % group
    operands = [
        fields,
        geometry,
        normals,
        face_scale,
        derivatives,
        lift_matrix,
        face_nbr,
        send_rows[None],
        fine_slots[None],
        export_rows,
        fine_nbr,
        *[jnp.asarray(x) for x in tables()],
    ]
    vmem = pl.BlockSpec(memory_space=pltpu.VMEM)
    dma = pltpu.SemaphoreType.DMA
    return pl.pallas_call(
        functools.partial(kernel, n_dom, n_sub, width),
        out_shape=pltpu.VMEM(fields.shape, f32),
        in_specs=[pl.BlockSpec(memory_space=pl.ANY)] * len(operands),
        out_specs=vmem,
        scratch_shapes=[
            *[pltpu.VMEM(x.shape, x.dtype) for x in operands],
            dma((len(operands),)),
            pltpu.VMEM((FR, count), f32),
            pltpu.VMEM((FR, count), f32),
            pltpu.VMEM((4 * FR + 64, count + 128), bf16),
            pltpu.VMEM((32, count), f32),
            pltpu.VMEM((16, fine), f32),
            pltpu.VMEM((TR, 2 * FR), bf16),
            pltpu.VMEM((RK, 4 * FR), bf16),
            pltpu.VMEM((count, slots), bf16),
            pltpu.VMEM((4, count + 128, count), bf16),
            pltpu.VMEM((fine, 4 * fine), bf16),
            pltpu.VMEM((fine, 4 * fine), bf16),
            pltpu.VMEM((fine, 8 * fine), bf16),
            pltpu.VMEM((12 * width, 8 * fine), bf16),
            pltpu.VMEM((224, 3 * FR), bf16),
            pltpu.VMEM((FR, 3 * TR), bf16),
            pltpu.VMEM((n_dom, 8, 128), f32),
            pltpu.VMEM((n_dom, 8, 128), f32),
            pltpu.VMEM((n_dom, 8, 128), f32),
            pltpu.VMEM((n_dom, 8, 128), f32),
            pltpu.VMEM((2, n_dom, cap, RK), f32),
            pltpu.VMEM((2, n_dom, cap, RK), f32),
            pltpu.VMEM((n_dom, cap, RK), f32),
            pltpu.VMEM((n_dom, cap, RK), f32),
            pltpu.VMEM((2, width, 128), f32),
            pltpu.VMEM((2, width, 128), f32),
            pltpu.VMEM((2, width, 256), f32),
            pltpu.VMEM((2, width, 256), f32),
            pltpu.VMEM((SUBSTEPS, 10 * width, 128), f32),
            pltpu.VMEM((SUBSTEPS, 12 * width, 128), f32),
            pltpu.VMEM((2, 2, FR, 128), f32),
            pltpu.VMEM((2, 2, FR, 128), f32),
            dma((n_dom,)),
            dma((n_dom,)),
            dma((n_dom,)),
            dma((n_dom,)),
            dma((2, n_dom)),
            dma((2, n_dom)),
            dma((n_dom,)),
            dma((n_dom,)),
            dma((2,)),
            dma((2,)),
            dma((2,)),
            dma((2,)),
            dma((SUBSTEPS, 4)),
            dma((SUBSTEPS, 4)),
            dma((2, 2)),
            dma((2, 2)),
        ],
        compiler_params=pltpu.CompilerParams(
            collective_id=0, has_side_effects=True, vmem_limit_bytes=56 * 1024 * 1024
        ),
    )(*operands)


def solution(mesh):
    return jax.shard_map(
        functools.partial(per_device, mesh.shape["dom"], mesh.shape["sub"]),
        mesh=mesh,
        in_specs=(
            P(None, None, ("dom", "sub")),
            P(None, ("dom", "sub")),
            P(None, None, ("dom", "sub")),
            P(None, ("dom", "sub")),
            P(),
            P(),
            P(None, ("dom", "sub")),
            P(("dom", "sub")),
            P(("dom", "sub")),
            P(None, ("dom", "sub")),
            P(None, ("dom", "sub")),
        ),
        out_specs=P(None, None, ("dom", "sub")),
        check_vma=False,
    )
```

```python
import functools

import jax
import jax.numpy as jnp
import numpy as np
from jax import lax
from jax.experimental import pallas as pl
from jax.experimental.pallas import tpu as pltpu
from jax.sharding import PartitionSpec as P

SUBSTEPS = 4
coarse_step = 0.2

PADC = 24
FR = 80
FN = 16
TR = 192
RK = 128
GEO, NS, CODE = 0, 9, 24
CHUNK = 256

bf16 = jnp.bfloat16
f32 = jnp.float32
MESH = pl.DeviceIdType.MESH


def face_table():
    places = [
        (along_r, along_s, along_t)
        for along_t in range(4)
        for along_s in range(4 - along_t)
        for along_r in range(4 - along_t - along_s)
    ]
    bottom_face = [number for number, location in enumerate(places) if location[2] == 0]
    front_face = [number for number, location in enumerate(places) if location[1] == 0]
    slanted = [number for number, location in enumerate(places) if sum(location) == 3]
    beside = [number for number, location in enumerate(places) if location[0] == 0]
    return np.array([bottom_face, front_face, slanted, beside], dtype=np.int32).T


def tables():
    nodes = face_table()
    sel = np.zeros((TR, 2 * FR), np.float32)
    pack = np.zeros((RK, 4 * FR), np.float32)
    unpack = np.zeros((2 * FR, 2 * RK), np.float32)
    for c in range(3):
        for p in range(20):
            for field in range(2):
                packed = (field * 3 + c) * 20 + p
                for s in range(2):
                    pack[packed, field * 2 * FR + s * FR + c * PADC + p] = 1
                    unpack[field * FR + c * PADC + p, s * RK + packed] = 1
        for f in range(4):
            for n in range(10):
                for s in range(2):
                    sel[f * 3 * FN + c * FN + n, s * FR + c * PADC + nodes[n, f]] = 1
    d_rows = np.zeros((3, 224, 20), np.float32)
    d_hi = np.zeros((20, 3 * FR), np.float32)
    d_lo = np.zeros((20, 3 * FR), np.float32)
    d_mask = np.zeros((224, 3 * FR), np.float32)
    l_rows = np.zeros((FR, 20), np.float32)
    l_hi = np.zeros((40, 3 * TR), np.float32)
    l_lo = np.zeros((40, 3 * TR), np.float32)
    l_mask = np.zeros((FR, 3 * TR), np.float32)
    for c in range(3):
        for p in range(20):
            l_rows[c * PADC + p, p] = 1
            for a in range(3):
                d_rows[a, (a * 3 + c) * PADC + p, p] = 1
            d_hi[p, c * PADC + p] = 1
            d_hi[p, FR + c * PADC + p] = 1
            d_lo[p, 2 * FR + c * PADC + p] = 1
        for s in range(3):
            for a in range(3):
                at = (a * 3 + c) * PADC
                d_mask[at : at + 20, s * FR + c * PADC : s * FR + c * PADC + 20] = 1
            for f in range(4):
                col = s * TR + f * 3 * FN + c * FN
                l_mask[c * PADC : c * PADC + 20, col : col + 10] = 0.5
                for n in range(10):
                    (l_lo if s == 2 else l_hi)[f * 10 + n, col + n] = 1
    out = [unpack, d_rows, d_hi, d_lo, l_rows, l_hi, l_lo]
    return [sel, pack] + [x.astype(jnp.bfloat16) for x in out] + [d_mask, l_mask]


def split(x):
    hi = x.astype(bf16).astype(f32)
    return hi, x - hi


def split2(x):
    hi, lo = split(x)
    return jnp.concatenate([hi, lo], axis=0).astype(bf16)


def split3(x):
    hi, lo = split(x)
    return jnp.concatenate([hi, lo, hi], axis=0).astype(bf16)


def dot(a, b):
    return jnp.dot(a, b, preferred_element_type=f32)


def dot_t(a, b):
    return lax.dot_general(a, b, (((1,), (1,)), ((), ())), preferred_element_type=f32)


def one_hot(count, row):
    at = lax.broadcasted_iota(jnp.int32, (count, row.shape[1]), 0)
    return jnp.where(at == row, 1.0, 0.0).astype(bf16)


def curl(grad, geo):
    def partial(m, c):
        total = None
        for a in range(3):
            at = (a * 3 + c) * PADC
            term = geo[3 * m + a : 3 * m + a + 1] * grad[at : at + PADC]
            total = term if total is None else total + term
        return total

    parts = [
        partial(1, 2) - partial(2, 1),
        partial(2, 0) - partial(0, 2),
        partial(0, 1) - partial(1, 0),
    ]
    pad = jnp.zeros((FR - 3 * PADC, grad.shape[1]), f32)
    return jnp.concatenate([*parts, pad], axis=0)


def pick_face(traces, face):
    total = traces[: 3 * FN]
    for g in range(1, 4):
        total = jnp.where(face == g, traces[g * 3 * FN : (g + 1) * 3 * FN], total)
    return total


def flux(jump, ns, f):
    n = [ns[c * 4 + f : c * 4 + f + 1] for c in range(3)]
    j = [jump[c * FN : (c + 1) * FN] for c in range(3)]
    return [
        n[1] * j[2] - n[2] * j[1],
        n[2] * j[0] - n[0] * j[2],
        n[0] * j[1] - n[1] * j[0],
    ]


OPERANDS = 22


def kernel(n_dom, n_sub, width, *refs):
    given, out = refs[:OPERANDS], refs[OPERANDS]
    local, load_sem = refs[OPERANDS + 1 : 2 * OPERANDS + 1], refs[2 * OPERANDS + 1]
    (
        fields,
        geometry,
        normals,
        face_scale,
        derivatives,
        lift_matrix,
        face_nbr,
        send_rows,
        fine_slots,
        export_rows,
        fine_nbr,
        sel_full,
        pack_full,
        unpack,
        d_rows,
        d_hi,
        d_lo,
        l_rows,
        l_hi,
        l_lo,
        d_mask,
        l_mask,
    ) = local
    (
    own_e,
    own_h,
    pool,
    stat,
    frozen,
    sel,
    pack,
    send_hot,
    coarse_hot,
    still,
    moved,
    moved_hot,
    fine_own,
    fine_halo,
    tile_own,
    tile_halo,
    dmat,
    lmat,
    mask_out,
    mask_in,
    extra_out,
    extra_in,
    hand_out,
    hand_in,
    back_out,
    back_in,
    code_out,
    code_in,
    first_out,
    first_in,
    kept_out,
    kept_in,
    fine_out,
    fine_in,
    halo_out,
    halo_in,
    mask_send,
    mask_recv,
    extra_send,
    extra_recv,
    hand_send,
    hand_recv,
    back_send,
    back_recv,
    code_send,
    code_recv,
    first_send,
    first_recv,
    kept_send,
    kept_recv,
    fine_send,
    fine_recv,
    halo_send,
    halo_recv,
    ) = refs[2 * OPERANDS + 2 :]
    count = fields.shape[2]
    fine = fine_slots.shape[1]
    cap = hand_out.shape[2]
    slots = n_dom * cap
    full = count + 128
    dom, sub = lax.axis_index("dom"), lax.axis_index("sub")
    me = dom * n_sub + sub
    total = n_dom * n_sub
    after, before = lax.rem(me + 1, total), lax.rem(me + total - 1, total)
    after_id = (after // n_sub, lax.rem(after, n_sub))
    before_id = (before // n_sub, lax.rem(before, n_sub))
    after2, before2 = lax.rem(me + 2, total), lax.rem(me + total - 2, total)
    after2_id = (after2 // n_sub, lax.rem(after2, n_sub))
    before2_id = (before2 // n_sub, lax.rem(before2, n_sub))

    loads = [
        pltpu.make_async_copy(src, dst, load_sem.at[i])
        for i, (src, dst) in enumerate(zip(given, local))
    ]
    first_loads = [10, 8, 9, 0]
    later_loads = [i for i in range(OPERANDS) if i not in first_loads]
    for i in first_loads + later_loads:
        loads[i].start()

    barrier = pltpu.get_barrier_semaphore()
    for target in (after_id, before_id, after2_id, before2_id):
        pl.semaphore_signal(barrier, inc=1, device_id=target, device_id_type=MESH)

    @pl.loop(1, n_dom)
    def _(i):
        pl.semaphore_signal(
            barrier, inc=1, device_id=(lax.rem(dom + i, n_dom), sub), device_id_type=MESH
        )

    def exchange(src, dst, send, recv):
        def copy(i):
            target = lax.rem(dom + i, n_dom)
            return pltpu.make_async_remote_copy(
                src_ref=src.at[target],
                dst_ref=dst.at[dom],
                send_sem=send.at[i],
                recv_sem=recv.at[i],
                device_id=(target, sub),
                device_id_type=MESH,
            )

        @pl.loop(1, n_dom)
        def _(i):
            copy(i).start()

        dst[pl.ds(dom, 1)] = src[pl.ds(dom, 1)]
        return copy

    def finish(copy):
        @pl.loop(1, n_dom)
        def _(i):
            copy(i).wait()

    def to_neighbours(src, dst, send, recv):
        copies = []
        for side, target in enumerate((after_id, before_id)):
            copy = pltpu.make_async_remote_copy(
                src_ref=src.at[side],
                dst_ref=dst.at[side],
                send_sem=send.at[side],
                recv_sem=recv.at[side],
                device_id=target,
                device_id_type=MESH,
            )
            copy.start()
            copies.append(copy)
        return copies

    def slots_of(d, row):
        at = lax.broadcasted_iota(jnp.int32, (128, row.shape[1]), 0)
        return jnp.where((row - d * cap == at) & (at < cap), 1.0, 0.0).astype(bf16)

    for i in first_loads:
        loads[i].wait()

    codes = [fine_nbr[f : f + 1, :] for f in range(4)]
    frozen_code = 4 * fine + 8 * width
    frozen[...] = jnp.zeros(frozen.shape, f32)
    frozen[0:4, :] = jnp.where(fine_nbr[...] == frozen_code, 1.0, 0.0)
    frozen[4:8, :] = fine_nbr[...].astype(f32)
    my_slots = fine_slots[...]

    eye = one_hot(width, lax.broadcasted_iota(jnp.int32, (1, width), 1))
    export_up = dot_t(eye, one_hot(fine, export_rows[1:2, :])).astype(bf16)
    export_down = dot_t(eye, one_hot(fine, export_rows[0:1, :])).astype(bf16)
    export_hot = jnp.concatenate([export_up, export_down], axis=0)
    code_row = jnp.concatenate(codes, axis=1) >> 2
    fine_own[...] = one_hot(fine, code_row)
    hi, lo = split(frozen[...])
    exported = dot_t(export_hot, hi.astype(bf16)) + dot_t(export_hot, lo.astype(bf16))
    code_out[...] = jnp.zeros(code_out.shape, f32)
    code_out[0, :, :16] = exported[:width]
    code_out[1, :, :16] = exported[width:]

    @pl.loop(0, n_dom)
    def _(d):
        mask_out[d] = dot_t(frozen[...].astype(bf16), slots_of(d, my_slots))[:8]

    for ref, first in ((own_e, 0), (own_h, 3)):
        ref[...] = jnp.zeros(ref.shape, f32)
        for c in range(3):
            ref[c * PADC : c * PADC + 20, :] = fields[first + c]
    halo_out[0, 0] = own_e[:, count - 128 :]
    halo_out[0, 1] = own_e[:, :128]

    pl.semaphore_wait(barrier, n_dom + 3)
    masks = exchange(mask_out, mask_in, mask_send, mask_recv)
    sent_codes = to_neighbours(code_out, code_in, code_send, code_recv)
    halo_e = to_neighbours(halo_out.at[0], halo_in.at[0], halo_send.at[0], halo_recv.at[0])

    for i in later_loads:
        loads[i].wait()

    sel[...] = sel_full[...].astype(bf16)
    pack[...] = pack_full[...].astype(bf16)

    stat[...] = jnp.zeros(stat.shape, f32)
    stat[GEO : GEO + 9, :] = geometry[...]
    for c in range(3):
        stat[NS + 4 * c : NS + 4 * c + 4, :] = normals[c] * face_scale[...]
    stat[CODE : CODE + 4, :] = face_nbr[...].astype(f32)
    pool[: 2 * FR, :count] = split2(own_e[...])
    pool[2 * FR : 4 * FR, :count] = split2(own_h[...])
    pool[4 * FR :, :count] = split2(stat[...])

    rows = send_rows[...]
    send_hot[...] = one_hot(count, rows)
    picked = dot(pool[:, :count], send_hot[...])
    slot_stat = picked[4 * FR : 4 * FR + 32] + picked[4 * FR + 32 :]
    picked = picked[: 4 * FR].astype(bf16)
    message = jnp.concatenate([dot(pack[...], picked)[:120], slot_stat[:8]], axis=0)
    hand_out[0] = message.T.reshape(n_dom, cap, RK)
    handed_fields = exchange(hand_out.at[0], hand_in.at[0], hand_send.at[0], hand_recv.at[0])
    slot_row = lax.broadcasted_iota(jnp.int32, (1, slots), 1)
    extra = split2(slot_stat[8:24])

    @pl.loop(0, n_dom)
    def _(d):
        part = dot_t(extra, slots_of(d, slot_row))
        extra_out[d] = part[:16] + part[16:]

    extras = exchange(extra_out, extra_in, extra_send, extra_recv)

    rows_hi = rows_lo = None
    for a in range(3):
        hi, lo = split(derivatives[a])
        hi = dot(d_rows[a], hi.astype(bf16))
        lo = dot(d_rows[a], lo.astype(bf16))
        rows_hi = hi if a == 0 else rows_hi + hi
        rows_lo = lo if a == 0 else rows_lo + lo
    wide = dot(rows_hi.astype(bf16), d_hi[...]) + dot(rows_lo.astype(bf16), d_lo[...])
    dmat[...] = (wide * d_mask[...]).astype(bf16)
    hi, lo = split(lift_matrix[...])
    hi = dot(l_rows[...], hi.astype(bf16))
    lo = dot(l_rows[...], lo.astype(bf16))
    wide = dot(hi.astype(bf16), l_hi[...]) + dot(lo.astype(bf16), l_lo[...])
    lmat[...] = (wide * l_mask[...]).astype(bf16)

    traces_e = dot(sel[...], picked[: 2 * FR])
    traces_h = dot(sel[...], picked[2 * FR :])
    held_e, held_h = [], []
    for f in range(4):
        code = slot_stat[CODE + f : CODE + f + 1].astype(jnp.int32)
        face = code & 3
        wall = code == 4 * rows + f
        near = dot(pool[: 4 * FR, :count], one_hot(count, code >> 2)).astype(bf16)
        e = pick_face(dot(sel[...], near[: 2 * FR]), face)
        h = pick_face(dot(sel[...], near[2 * FR :]), face)
        at = f * 3 * FN
        held_e.append(jnp.where(wall, -traces_e[at : at + 3 * FN], e))
        held_h.append(jnp.where(wall, traces_h[at : at + 3 * FN], h))
    finish(masks)

    def add_mask(d, mask):
        part = jnp.concatenate([mask_in[d], jnp.zeros((8, 128), f32)], axis=0).astype(bf16)
        return mask + dot(part, slots_of(d, slot_row))

    mask = lax.fori_loop(0, n_dom, add_mask, jnp.zeros((16, slots), f32))
    kept_e, kept_h = [], []
    for f in range(4):
        keep = mask[f : f + 1] > 0.5
        kept_e += flux(jnp.where(keep, held_e[f], 0.0), slot_stat[NS : NS + 12], f)
        kept_h += flux(jnp.where(keep, held_h[f], 0.0), slot_stat[NS : NS + 12], f)
    kept_e = dot(lmat[...], split3(jnp.concatenate(kept_e, axis=0)))
    kept_h = dot(lmat[...], split3(jnp.concatenate(kept_h, axis=0)))
    kept = jnp.concatenate([split2(kept_e), split2(kept_h)], axis=0)
    hand_out[1] = dot(pack[...], kept).T.reshape(n_dom, cap, RK)
    handed_kept = exchange(hand_out.at[1], hand_in.at[1], hand_send.at[1], hand_recv.at[1])

    around_up = [dot_t(export_up, fine_own[:, f * fine : (f + 1) * fine]) for f in range(4)]
    around_down = [dot_t(export_down, fine_own[:, f * fine : (f + 1) * fine]) for f in range(4)]
    around = jnp.concatenate(
        [*around_up, export_up.astype(f32), *around_down, export_down.astype(f32)], axis=0
    ).astype(bf16)
    slot_hot = one_hot(slots, my_slots)
    reach = 5 * width
    fine_out[...] = jnp.zeros(fine_out.shape, f32)
    first_out[...] = jnp.zeros(first_out.shape, f32)
    slot_hot = one_hot(slots, my_slots)
    kept_out[...] = jnp.zeros(kept_out.shape, f32)

    def take(message):
        got = dot(split2(message.reshape(slots, RK).T), slot_hot)
        state = dot(unpack[...], got.astype(bf16))
        return state[:FR], state[FR:], got[120:RK] + got[RK + 120 :]

    finish(handed_fields)
    efield, hfield, stat_a = take(hand_in[0])
    finish(extras)

    def add_extra(d, value):
        return value + dot(split2(extra_in[d]), slots_of(d, my_slots))

    stat_c = lax.fori_loop(0, n_dom, add_extra, jnp.zeros((32, fine), f32))
    stat_c = stat_c[:16] + stat_c[16:]
    fine_stat = jnp.concatenate([stat_a, stat_c], axis=0)

    def send_electric(parts, turn):
        tile = dot_t(around, parts[:FR]) + dot_t(around, parts[FR:])
        fine_out[turn, :, :FR] = tile
        copies = []
        plan = (
            (after_id, 0, reach, 0),
            (before_id, reach, reach, reach),
            (after2_id, 4 * width, width, 2 * reach),
            (before2_id, reach + 4 * width, width, 2 * reach + width),
        )
        for side, (target, first, size, at) in enumerate(plan):
            copy = pltpu.make_async_remote_copy(
                src_ref=fine_out.at[turn, first : first + size],
                dst_ref=fine_in.at[turn, at : at + size],
                send_sem=fine_send.at[turn, side],
                recv_sem=fine_recv.at[turn, side],
                device_id=target,
                device_id_type=MESH,
            )
            copy.start()
            copies.append(copy)
        return copies

    def fluxes_of(near, own, face_codes, ns, size):
        traces = dot(sel[...], near.astype(bf16))
        fluxes = []
        for f in range(4):
            at = f * 3 * FN
            outside = pick_face(traces[:, f * size : (f + 1) * size], face_codes[f] & 3)
            fluxes += flux(outside - own[at : at + 3 * FN], ns, f)
        return dot(lmat[...], split3(jnp.concatenate(fluxes, axis=0)))

    copies = send_electric(split2(efield), 0)
    hi, lo = split(jnp.concatenate([hfield, fine_stat], axis=0))
    tile = dot_t(export_hot, hi.astype(bf16)) + dot_t(export_hot, lo.astype(bf16))
    first_out[0, :, : FR + 24] = tile[:width]
    first_out[1, :, : FR + 24] = tile[width:]
    first_copies = to_neighbours(first_out, first_in, first_send, first_recv)

    export_at = export_hot.astype(f32).T.astype(bf16)
    pad_eye = one_hot(2 * width, lax.broadcasted_iota(jnp.int32, (1, fine), 1))
    for copy in sent_codes:
        copy.wait()
    came_codes = dot(split2(code_in[...].reshape(2 * width, 128).T), pad_eye)
    came_codes = (came_codes[:128] + came_codes[128:])[4:8].astype(jnp.int32)
    ext = lax.broadcasted_iota(jnp.int32, (1, fine), 1)
    below = ext < width
    real = ext < 2 * width
    low_end = 4 * fine + 4 * width
    reach = 5 * width
    codes_all = []
    for f in range(4):
        code = codes[f]
        low, high = (code - 4 * fine) >> 2, (code - low_end) >> 2
        at = jnp.where(code < low_end, 4 * width + low, reach + 4 * width + high)
        at = jnp.where((code < 4 * fine) | (code >= frozen_code), -1, at)
        code_x = came_codes[f : f + 1]
        low, high = (code_x - 4 * fine) >> 2, (code_x - low_end) >> 2
        is_near = code_x < 4 * fine
        is_low = (code_x >= 4 * fine) & (code_x < low_end)
        is_high = (code_x >= low_end) & (code_x < frozen_code)
        at_x = jnp.where(below, f * width + ext, reach + f * width + ext - width)
        at_x = jnp.where(is_near, at_x, -1)
        at_x = jnp.where(is_low & below, 2 * reach + low, at_x)
        at_x = jnp.where(is_high & (ext >= width), 2 * reach + width + high, at_x)
        at_x = jnp.where(real, at_x, -1)
        mine = jnp.where(is_low & (ext >= width), low, jnp.where(is_high & below, width + high, -1))
        mine = jnp.where(real, mine, -1)
        block = slice(2 * f * fine, (2 * f + 1) * fine)
        block_x = slice((2 * f + 1) * fine, (2 * f + 2) * fine)
        tile_own[:, block] = fine_own[:, f * fine : (f + 1) * fine]
        tile_own[:, block_x] = dot(export_at, one_hot(2 * width, mine)).astype(bf16)
        tile_halo[:, block] = one_hot(12 * width, at)
        tile_halo[:, block_x] = one_hot(12 * width, at_x)
        codes_all.append(jnp.concatenate([code, code_x], axis=1))
    at = jnp.where(below, 4 * width + ext, reach + 4 * width + ext - width)
    ext_hot = one_hot(12 * width, jnp.where(real, at, -1))
    fine_halo[...] = one_hot(fine, code_row - fine)

    @pl.loop(0, count // CHUNK)
    def _(i):
        start = pl.multiple_of(i * CHUNK, CHUNK)
        for f in range(4):
            code = face_nbr[f : f + 1, pl.ds(start, CHUNK)]
            coarse_hot[f, :, pl.ds(start, CHUNK)] = one_hot(full, code >> 2)


    fine_step = coarse_step / SUBSTEPS
    fine_geo, fine_ns = fine_stat[GEO : GEO + 9], fine_stat[NS : NS + 12]
    for substep in range(SUBSTEPS):
        parts = split2(efield)
        if substep > 0:
            copies = send_electric(parts, substep)
        near = dot(parts, tile_own[...])
        own = dot(sel[...], parts)
        spin = curl(dot(dmat[...], split3(efield)), fine_geo)
        if substep == 0:
            for copy in first_copies:
                copy.wait()
            came = dot(split2(first_in[...].reshape(2 * width, 128).T), pad_eye)
            came = came[:128] + came[128:]
            hfield = jnp.concatenate([hfield, came[:FR]], axis=1)
            stat_x = came[FR : FR + 24]
            geo_x = stat_x[GEO : GEO + 9]
            ns_all = jnp.concatenate([fine_stat, stat_x], axis=1)[NS : NS + 12]
        for copy in copies:
            copy.wait()
        halo = split2(fine_in[substep].T[:FR])
        near = near + dot(halo, tile_halo[...])
        parts_x = dot(halo, ext_hot)
        field_x = parts_x[:FR] + parts_x[FR:]
        own = jnp.concatenate([own, dot(sel[...], parts_x.astype(bf16))], axis=1)
        spin_x = curl(dot(dmat[...], split3(field_x)), geo_x)
        rate = jnp.concatenate([spin, spin_x], axis=1)
        rate = rate + fluxes_of(near, own, codes_all, ns_all, 2 * fine)
        if substep == 0:
            finish(handed_kept)
            kept_e, kept_h, _ = take(hand_in[1])
            hi, lo = split(kept_e)
            tile = dot_t(export_hot, hi.astype(bf16)) + dot_t(export_hot, lo.astype(bf16))
            kept_out[0, :, :FR] = tile[:width]
            kept_out[1, :, :FR] = tile[width:]
            for copy in to_neighbours(kept_out, kept_in, kept_send, kept_recv):
                copy.wait()
            came = dot(split2(kept_in[...].reshape(2 * width, 128).T), pad_eye)
            kept_all = jnp.concatenate([kept_e, came[:FR] + came[128 : 128 + FR]], axis=1)
        hfield = hfield - fine_step * (rate + kept_all)

        field = hfield[:, :fine]
        parts = split2(field)
        near = dot(parts, fine_own[...]) + dot(split2(hfield[:, fine:]), fine_halo[...])
        own = dot(sel[...], parts)
        spin = curl(dot(dmat[...], split3(field)), fine_geo) + kept_h
        efield = efield + fine_step * (spin + fluxes_of(near, own, codes, fine_ns, fine))
    hfield = hfield[:, :fine]

    result = jnp.concatenate([split2(efield), split2(hfield)], axis=0)
    result = split2(dot(pack[...], result))
    result = dot_t(slot_hot, result)
    result = result[:, :RK] + result[:, RK:]
    back_out[...] = result.reshape(n_dom, cap, RK)
    returned = exchange(back_out, back_in, back_send, back_recv)
    is_fine = dot_t(jnp.ones((16, slots), bf16), send_hot[...])[:1] > 0.5
    pool_e, pool_h = pool.at[: 2 * FR], pool.at[2 * FR : 4 * FR]
    halo_lane = lax.broadcasted_iota(jnp.int32, (FR, 128), 1)

    def set_halo(pool, turn, copies):
        for copy in copies:
            copy.wait()
        tile = jnp.where(halo_lane < 64, halo_in[turn, 1], halo_in[turn, 0])
        pool[:, count:] = split2(pltpu.roll(tile, 64, 1))

    set_halo(pool_e, 0, halo_e)
    pool_e[:, :count] = split2(jnp.where(is_fine, 0.0, own_e[...]))
    slot_at = jnp.broadcast_to(rows.astype(f32), (8, slots)).T[:, :1].astype(jnp.int32)
    slot_at = jnp.where(slot_at < count, slot_at, -1)

    @pl.loop(0, count // CHUNK)
    def _(i):
        window = pl.ds(pl.multiple_of(i * CHUNK, CHUNK), CHUNK)
        for f in range(4):
            near = dot(pool_e[...], coarse_hot[f, :, window])
            still[f, :, window] = near.astype(bf16)
            code = face_nbr[f : f + 1, window] >> 2
            moved_hot[f, :, window] = jnp.where(slot_at == code, 1.0, 0.0).astype(bf16)

    finish(returned)
    came = back_in[...].reshape(slots, RK).T
    came = split2(came)
    moved[...] = split2(dot(unpack[:FR], came))
    came = dot_t(came, send_hot[...]).astype(bf16)
    came = dot(unpack[...], came)
    merged_e = jnp.where(is_fine, came[:FR], own_e[...])
    merged_h = jnp.where(is_fine, came[FR:], own_h[...])
    own_e[...] = merged_e
    own_h[...] = merged_h

    place = lax.broadcasted_iota(jnp.int32, (1, CHUNK), 1)

    def coarse_rate(start, source, gather, mirror):
        window = pl.ds(start, CHUNK)
        field = source[:, window]
        table = stat[:, window]
        spin = curl(dot(dmat[...], split3(field)), table[GEO : GEO + 9])
        own = dot(sel[...], split2(field))
        ns = table[NS : NS + 12]
        fluxes = []
        for f in range(4):
            code = face_nbr[f : f + 1, window]
            near = gather(f, window).astype(bf16)
            outside = pick_face(dot(sel[...], near), code & 3)
            mine = own[f * 3 * FN : (f + 1) * 3 * FN]
            wall = code == 4 * (start + place) + f
            outside = jnp.where(wall, mirror * mine, outside)
            fluxes += flux(outside - mine, ns, f)
        return spin + dot(lmat[...], split3(jnp.concatenate(fluxes, axis=0)))

    def electric_near(f, window):
        return dot(moved[...], moved_hot[f, :, window]) + still[f, :, window].astype(f32)

    def magnetic_near(reach):
        return lambda f, window: dot(pool_h[:, :reach], coarse_hot[f, :reach, window])

    def update(start, source, gather, target, first, scale, mirror):
        window = pl.ds(start, CHUNK)
        new = target[:, window] + scale * coarse_rate(start, source, gather, mirror)
        target[:, window] = new
        for c in range(3):
            out[first + c, :, window] = new[c * PADC : c * PADC + 20]
        if first == 3:
            pool_h[:, window] = split2(new)

    last = count - CHUNK

    for start in (0, last):
        update(start, own_e, electric_near, own_h, 3, -coarse_step, -1.0)

    halo_out[1, 0] = own_h[:, count - 128 :]
    halo_out[1, 1] = own_h[:, :128]
    halo_h = to_neighbours(halo_out.at[1], halo_in.at[1], halo_send.at[1], halo_recv.at[1])

    for start in range(CHUNK, last, CHUNK):
        update(start, own_e, electric_near, own_h, 3, -coarse_step, -1.0)
    for start in range(CHUNK, last, CHUNK):
        update(start, own_h, magnetic_near(count), own_e, 0, coarse_step, 1.0)

    set_halo(pool_h, 1, halo_h)

    for start in (0, last):
        update(start, own_h, magnetic_near(full), own_e, 0, coarse_step, 1.0)


def per_device(
    n_dom,
    n_sub,
    fields,
    geometry,
    normals,
    face_scale,
    derivatives,
    lift_matrix,
    face_nbr,
    send_rows,
    fine_slots,
    export_rows,
    fine_nbr,
):
    count = fields.shape[2]
    fine = fine_slots.shape[0]
    width = export_rows.shape[1]
    group = send_rows.shape[0] // n_dom
    cap = -(-group // 8) * 8
    slots = n_dom * cap
    if cap != group:
        send_rows = jnp.pad(
            send_rows.reshape(n_dom, group),
            ((0, 0), (0, cap - group)),
            constant_values=count,
        ).reshape(-1)
        fine_slots = fine_slots // group * cap + fine_slots % group
    operands = [
        fields,
        geometry,
        normals,
        face_scale,
        derivatives,
        lift_matrix,
        face_nbr,
        send_rows[None],
        fine_slots[None],
        export_rows,
        fine_nbr,
        *[jnp.asarray(x) for x in tables()],
    ]
    vmem = pl.BlockSpec(memory_space=pltpu.VMEM)
    dma = pltpu.SemaphoreType.DMA
    return pl.pallas_call(
        functools.partial(kernel, n_dom, n_sub, width),
        out_shape=pltpu.VMEM(fields.shape, f32),
        in_specs=[pl.BlockSpec(memory_space=pl.ANY)] * len(operands),
        out_specs=vmem,
        scratch_shapes=[
            *[pltpu.VMEM(x.shape, x.dtype) for x in operands],
            dma((len(operands),)),
            pltpu.VMEM((FR, count), f32),
            pltpu.VMEM((FR, count), f32),
            pltpu.VMEM((4 * FR + 64, count + 128), bf16),
            pltpu.VMEM((32, count), f32),
            pltpu.VMEM((16, fine), f32),
            pltpu.VMEM((TR, 2 * FR), bf16),
            pltpu.VMEM((RK, 4 * FR), bf16),
            pltpu.VMEM((count, slots), bf16),
            pltpu.VMEM((4, count + 128, count), bf16),
            pltpu.VMEM((4, 2 * FR, count), bf16),
            pltpu.VMEM((2 * FR, slots), bf16),
            pltpu.VMEM((4, slots, count), bf16),
            pltpu.VMEM((fine, 4 * fine), bf16),
            pltpu.VMEM((fine, 4 * fine), bf16),
            pltpu.VMEM((fine, 8 * fine), bf16),
            pltpu.VMEM((12 * width, 8 * fine), bf16),
            pltpu.VMEM((224, 3 * FR), bf16),
            pltpu.VMEM((FR, 3 * TR), bf16),
            pltpu.VMEM((n_dom, 8, 128), f32),
            pltpu.VMEM((n_dom, 8, 128), f32),
            pltpu.VMEM((n_dom, 16, 128), f32),
            pltpu.VMEM((n_dom, 16, 128), f32),
            pltpu.VMEM((2, n_dom, cap, RK), f32),
            pltpu.VMEM((2, n_dom, cap, RK), f32),
            pltpu.VMEM((n_dom, cap, RK), f32),
            pltpu.VMEM((n_dom, cap, RK), f32),
            pltpu.VMEM((2, width, 128), f32),
            pltpu.VMEM((2, width, 128), f32),
            pltpu.VMEM((2, width, 128), f32),
            pltpu.VMEM((2, width, 128), f32),
            pltpu.VMEM((2, width, 128), f32),
            pltpu.VMEM((2, width, 128), f32),
            pltpu.VMEM((SUBSTEPS, 10 * width, 128), f32),
            pltpu.VMEM((SUBSTEPS, 12 * width, 128), f32),
            pltpu.VMEM((2, 2, FR, 128), f32),
            pltpu.VMEM((2, 2, FR, 128), f32),
            dma((n_dom,)),
            dma((n_dom,)),
            dma((n_dom,)),
            dma((n_dom,)),
            dma((2, n_dom)),
            dma((2, n_dom)),
            dma((n_dom,)),
            dma((n_dom,)),
            dma((2,)),
            dma((2,)),
            dma((2,)),
            dma((2,)),
            dma((2,)),
            dma((2,)),
            dma((SUBSTEPS, 4)),
            dma((SUBSTEPS, 4)),
            dma((2, 2)),
            dma((2, 2)),
        ],
        compiler_params=pltpu.CompilerParams(
            collective_id=0, has_side_effects=True, vmem_limit_bytes=56 * 1024 * 1024
        ),
    )(*operands)


def solution(mesh):
    return jax.shard_map(
        functools.partial(per_device, mesh.shape["dom"], mesh.shape["sub"]),
        mesh=mesh,
        in_specs=(
            P(None, None, ("dom", "sub")),
            P(None, ("dom", "sub")),
            P(None, None, ("dom", "sub")),
            P(None, ("dom", "sub")),
            P(),
            P(),
            P(None, ("dom", "sub")),
            P(("dom", "sub")),
            P(("dom", "sub")),
            P(None, ("dom", "sub")),
            P(None, ("dom", "sub")),
        ),
        out_specs=P(None, None, ("dom", "sub")),
        check_vma=False,
    )
```

```python
import functools

import jax
import jax.numpy as jnp
import numpy as np
from jax import lax
from jax.experimental import pallas as pl
from jax.experimental.pallas import tpu as pltpu
from jax.sharding import PartitionSpec as P

SUBSTEPS = 4
coarse_step = 0.2

PADC = 24
FR = 80
FN = 16
TR = 192
RK = 128
GEO, NS, CODE = 0, 9, 24
CHUNK = 256

bf16 = jnp.bfloat16
f32 = jnp.float32
MESH = pl.DeviceIdType.MESH


def face_table():
    places = [
        (along_r, along_s, along_t)
        for along_t in range(4)
        for along_s in range(4 - along_t)
        for along_r in range(4 - along_t - along_s)
    ]
    bottom_face = [number for number, location in enumerate(places) if location[2] == 0]
    front_face = [number for number, location in enumerate(places) if location[1] == 0]
    slanted = [number for number, location in enumerate(places) if sum(location) == 3]
    beside = [number for number, location in enumerate(places) if location[0] == 0]
    return np.array([bottom_face, front_face, slanted, beside], dtype=np.int32).T


def tables():
    nodes = face_table()
    sel = np.zeros((TR, 2 * FR), np.float32)
    narrow = np.zeros((128, 2 * FR), np.float32)
    for s in range(2):
        for c in range(3):
            for p in range(20):
                narrow[s * 64 + c * 20 + p, s * FR + c * PADC + p] = 1
    pack = np.zeros((RK, 4 * FR), np.float32)
    unpack = np.zeros((2 * FR, 2 * RK), np.float32)
    for c in range(3):
        for p in range(20):
            for field in range(2):
                packed = (field * 3 + c) * 20 + p
                for s in range(2):
                    pack[packed, field * 2 * FR + s * FR + c * PADC + p] = 1
                    unpack[field * FR + c * PADC + p, s * RK + packed] = 1
        for f in range(4):
            for n in range(10):
                for s in range(2):
                    sel[f * 3 * FN + c * FN + n, s * FR + c * PADC + nodes[n, f]] = 1
    d_rows = np.zeros((3, 224, 20), np.float32)
    d_hi = np.zeros((20, 3 * FR), np.float32)
    d_lo = np.zeros((20, 3 * FR), np.float32)
    d_mask = np.zeros((224, 3 * FR), np.float32)
    l_rows = np.zeros((FR, 20), np.float32)
    l_hi = np.zeros((40, 3 * TR), np.float32)
    l_lo = np.zeros((40, 3 * TR), np.float32)
    l_mask = np.zeros((FR, 3 * TR), np.float32)
    for c in range(3):
        for p in range(20):
            l_rows[c * PADC + p, p] = 1
            for a in range(3):
                d_rows[a, (a * 3 + c) * PADC + p, p] = 1
            d_hi[p, c * PADC + p] = 1
            d_hi[p, FR + c * PADC + p] = 1
            d_lo[p, 2 * FR + c * PADC + p] = 1
        for s in range(3):
            for a in range(3):
                at = (a * 3 + c) * PADC
                d_mask[at : at + 20, s * FR + c * PADC : s * FR + c * PADC + 20] = 1
            for f in range(4):
                col = s * TR + f * 3 * FN + c * FN
                l_mask[c * PADC : c * PADC + 20, col : col + 10] = 0.5
                for n in range(10):
                    (l_lo if s == 2 else l_hi)[f * 10 + n, col + n] = 1
    out = [unpack, d_rows, d_hi, d_lo, l_rows, l_hi, l_lo]
    return [sel, pack, narrow] + [x.astype(jnp.bfloat16) for x in out] + [d_mask, l_mask]


def split(x):
    hi = x.astype(bf16).astype(f32)
    return hi, x - hi


def split2(x):
    hi, lo = split(x)
    return jnp.concatenate([hi, lo], axis=0).astype(bf16)


def split3(x):
    hi, lo = split(x)
    return jnp.concatenate([hi, lo, hi], axis=0).astype(bf16)


def dot(a, b):
    return jnp.dot(a, b, preferred_element_type=f32)


def dot_t(a, b):
    return lax.dot_general(a, b, (((1,), (1,)), ((), ())), preferred_element_type=f32)


def one_hot(count, row):
    at = lax.broadcasted_iota(jnp.int32, (count, row.shape[1]), 0)
    return jnp.where(at == row, 1.0, 0.0).astype(bf16)


def curl(grad, geo):
    def partial(m, c):
        total = None
        for a in range(3):
            at = (a * 3 + c) * PADC
            term = geo[3 * m + a : 3 * m + a + 1] * grad[at : at + PADC]
            total = term if total is None else total + term
        return total

    parts = [
        partial(1, 2) - partial(2, 1),
        partial(2, 0) - partial(0, 2),
        partial(0, 1) - partial(1, 0),
    ]
    pad = jnp.zeros((FR - 3 * PADC, grad.shape[1]), f32)
    return jnp.concatenate([*parts, pad], axis=0)


def pick_face(traces, face):
    total = traces[: 3 * FN]
    for g in range(1, 4):
        total = jnp.where(face == g, traces[g * 3 * FN : (g + 1) * 3 * FN], total)
    return total


def flux(jump, ns, f):
    n = [ns[c * 4 + f : c * 4 + f + 1] for c in range(3)]
    j = [jump[c * FN : (c + 1) * FN] for c in range(3)]
    return [
        n[1] * j[2] - n[2] * j[1],
        n[2] * j[0] - n[0] * j[2],
        n[0] * j[1] - n[1] * j[0],
    ]


OPERANDS = 23


def kernel(n_dom, n_sub, width, *refs):
    given, out = refs[:OPERANDS], refs[OPERANDS]
    local, load_sem = refs[OPERANDS + 1 : 2 * OPERANDS + 1], refs[2 * OPERANDS + 1]
    (
        fields,
        geometry,
        normals,
        face_scale,
        derivatives,
        lift_matrix,
        face_nbr,
        send_rows,
        fine_slots,
        export_rows,
        fine_nbr,
        sel_full,
        pack_full,
        narrow_full,
        unpack,
        d_rows,
        d_hi,
        d_lo,
        l_rows,
        l_hi,
        l_lo,
        d_mask,
        l_mask,
    ) = local
    (
    own_e,
    own_h,
    pool,
    stat,
    frozen,
    sel,
    pack,
    narrow,
    sel_narrow,
    send_hot,
    coarse_hot,
    fine_own,
    fine_halo,
    tile_own,
    tile_halo,
    dmat,
    lmat,
    mask_out,
    mask_in,
    extra_out,
    extra_in,
    hand_out,
    hand_in,
    back_out,
    back_in,
    code_out,
    code_in,
    first_out,
    first_in,
    fine_out,
    fine_in,
    halo_out,
    halo_in,
    mask_send,
    mask_recv,
    extra_send,
    extra_recv,
    hand_send,
    hand_recv,
    back_send,
    back_recv,
    code_send,
    code_recv,
    first_send,
    first_recv,
    fine_send,
    fine_recv,
    halo_send,
    halo_recv,
    ) = refs[2 * OPERANDS + 2 :]
    count = fields.shape[2]
    fine = fine_slots.shape[1]
    cap = hand_out.shape[2]
    slots = n_dom * cap
    full = count + 128
    dom, sub = lax.axis_index("dom"), lax.axis_index("sub")
    me = dom * n_sub + sub
    total = n_dom * n_sub
    after, before = lax.rem(me + 1, total), lax.rem(me + total - 1, total)
    after_id = (after // n_sub, lax.rem(after, n_sub))
    before_id = (before // n_sub, lax.rem(before, n_sub))
    after2, before2 = lax.rem(me + 2, total), lax.rem(me + total - 2, total)
    after2_id = (after2 // n_sub, lax.rem(after2, n_sub))
    before2_id = (before2 // n_sub, lax.rem(before2, n_sub))

    loads = [
        pltpu.make_async_copy(src, dst, load_sem.at[i])
        for i, (src, dst) in enumerate(zip(given, local))
    ]
    first_loads = [10, 8, 9, 0]
    later_loads = [i for i in range(OPERANDS) if i not in first_loads]
    for i in first_loads + later_loads:
        loads[i].start()

    barrier = pltpu.get_barrier_semaphore()
    for target in (after_id, before_id, after2_id, before2_id):
        pl.semaphore_signal(barrier, inc=1, device_id=target, device_id_type=MESH)

    @pl.loop(1, n_dom)
    def _(i):
        pl.semaphore_signal(
            barrier, inc=1, device_id=(lax.rem(dom + i, n_dom), sub), device_id_type=MESH
        )

    def exchange(src, dst, send, recv):
        def copy(i):
            target = lax.rem(dom + i, n_dom)
            return pltpu.make_async_remote_copy(
                src_ref=src.at[target],
                dst_ref=dst.at[dom],
                send_sem=send.at[i],
                recv_sem=recv.at[i],
                device_id=(target, sub),
                device_id_type=MESH,
            )

        @pl.loop(1, n_dom)
        def _(i):
            copy(i).start()

        dst[pl.ds(dom, 1)] = src[pl.ds(dom, 1)]
        return copy

    def finish(copy):
        @pl.loop(1, n_dom)
        def _(i):
            copy(i).wait()

    def to_neighbours(src, dst, send, recv):
        copies = []
        for side, target in enumerate((after_id, before_id)):
            copy = pltpu.make_async_remote_copy(
                src_ref=src.at[side],
                dst_ref=dst.at[side],
                send_sem=send.at[side],
                recv_sem=recv.at[side],
                device_id=target,
                device_id_type=MESH,
            )
            copy.start()
            copies.append(copy)
        return copies

    def slots_of(d, row):
        at = lax.broadcasted_iota(jnp.int32, (128, row.shape[1]), 0)
        return jnp.where((row - d * cap == at) & (at < cap), 1.0, 0.0).astype(bf16)

    for i in first_loads:
        loads[i].wait()

    codes = [fine_nbr[f : f + 1, :] for f in range(4)]
    frozen_code = 4 * fine + 8 * width
    frozen[...] = jnp.zeros(frozen.shape, f32)
    frozen[0:4, :] = jnp.where(fine_nbr[...] == frozen_code, 1.0, 0.0)
    frozen[4:8, :] = fine_nbr[...].astype(f32)
    my_slots = fine_slots[...]

    eye = one_hot(width, lax.broadcasted_iota(jnp.int32, (1, width), 1))
    export_up = dot_t(eye, one_hot(fine, export_rows[1:2, :])).astype(bf16)
    export_down = dot_t(eye, one_hot(fine, export_rows[0:1, :])).astype(bf16)
    export_hot = jnp.concatenate([export_up, export_down], axis=0)
    code_row = jnp.concatenate(codes, axis=1) >> 2
    fine_own[...] = one_hot(fine, code_row)
    hi, lo = split(frozen[...])
    exported = dot_t(export_hot, hi.astype(bf16)) + dot_t(export_hot, lo.astype(bf16))
    code_out[...] = jnp.zeros(code_out.shape, f32)
    code_out[0, :, :16] = exported[:width]
    code_out[1, :, :16] = exported[width:]

    @pl.loop(0, n_dom)
    def _(d):
        mask_out[d] = dot_t(frozen[...].astype(bf16), slots_of(d, my_slots))[:8]

    for ref, first in ((own_e, 0), (own_h, 3)):
        ref[...] = jnp.zeros(ref.shape, f32)
        for c in range(3):
            ref[c * PADC : c * PADC + 20, :] = fields[first + c]
    halo_out[0, 0] = own_e[:, count - 128 :]
    halo_out[0, 1] = own_e[:, :128]

    pl.semaphore_wait(barrier, n_dom + 3)
    masks = exchange(mask_out, mask_in, mask_send, mask_recv)
    sent_codes = to_neighbours(code_out, code_in, code_send, code_recv)
    halo_e = to_neighbours(halo_out.at[0], halo_in.at[0], halo_send.at[0], halo_recv.at[0])

    for i in later_loads:
        loads[i].wait()

    sel[...] = sel_full[...].astype(bf16)
    pack[...] = pack_full[...].astype(bf16)
    narrow[...] = narrow_full[...].astype(bf16)
    sel_narrow[...] = dot_t(sel[...], narrow[...]).astype(bf16)

    stat[...] = jnp.zeros(stat.shape, f32)
    stat[GEO : GEO + 9, :] = geometry[...]
    for c in range(3):
        stat[NS + 4 * c : NS + 4 * c + 4, :] = normals[c] * face_scale[...]
    stat[CODE : CODE + 4, :] = face_nbr[...].astype(f32)
    pool[: 2 * FR, :count] = split2(own_e[...])
    pool[2 * FR : 4 * FR, :count] = split2(own_h[...])
    pool[4 * FR :, :count] = split2(stat[...])

    rows = send_rows[...]
    send_hot[...] = one_hot(count, rows)
    picked = dot(pool[:, :count], send_hot[...])
    slot_stat = picked[4 * FR : 4 * FR + 32] + picked[4 * FR + 32 :]
    picked = picked[: 4 * FR].astype(bf16)
    message = jnp.concatenate([dot(pack[...], picked)[:120], slot_stat[:8]], axis=0)
    hand_out[0] = message.T.reshape(n_dom, cap, RK)
    handed_fields = exchange(hand_out.at[0], hand_in.at[0], hand_send.at[0], hand_recv.at[0])
    slot_row = lax.broadcasted_iota(jnp.int32, (1, slots), 1)
    extra = split2(slot_stat[16:24])

    @pl.loop(0, n_dom)
    def _(d):
        part = dot_t(extra, slots_of(d, slot_row))
        extra_out[d] = part[:8] + part[8:]

    extras = exchange(extra_out, extra_in, extra_send, extra_recv)

    rows_hi = rows_lo = None
    for a in range(3):
        hi, lo = split(derivatives[a])
        hi = dot(d_rows[a], hi.astype(bf16))
        lo = dot(d_rows[a], lo.astype(bf16))
        rows_hi = hi if a == 0 else rows_hi + hi
        rows_lo = lo if a == 0 else rows_lo + lo
    wide = dot(rows_hi.astype(bf16), d_hi[...]) + dot(rows_lo.astype(bf16), d_lo[...])
    dmat[...] = (wide * d_mask[...]).astype(bf16)
    hi, lo = split(lift_matrix[...])
    hi = dot(l_rows[...], hi.astype(bf16))
    lo = dot(l_rows[...], lo.astype(bf16))
    wide = dot(hi.astype(bf16), l_hi[...]) + dot(lo.astype(bf16), l_lo[...])
    lmat[...] = (wide * l_mask[...]).astype(bf16)

    traces_e = dot(sel[...], picked[: 2 * FR])
    traces_h = dot(sel[...], picked[2 * FR :])
    held_e, held_h = [], []
    for f in range(4):
        code = slot_stat[CODE + f : CODE + f + 1].astype(jnp.int32)
        face = code & 3
        wall = code == 4 * rows + f
        near = dot(pool[: 4 * FR, :count], one_hot(count, code >> 2)).astype(bf16)
        e = pick_face(dot(sel[...], near[: 2 * FR]), face)
        h = pick_face(dot(sel[...], near[2 * FR :]), face)
        at = f * 3 * FN
        held_e.append(jnp.where(wall, -traces_e[at : at + 3 * FN], e))
        held_h.append(jnp.where(wall, traces_h[at : at + 3 * FN], h))
    finish(masks)

    def add_mask(d, mask):
        part = jnp.concatenate([mask_in[d], jnp.zeros((8, 128), f32)], axis=0).astype(bf16)
        return mask + dot(part, slots_of(d, slot_row))

    mask = lax.fori_loop(0, n_dom, add_mask, jnp.zeros((16, slots), f32))
    kept_e, kept_h = [], []
    for f in range(4):
        keep = mask[f : f + 1] > 0.5
        kept_e += flux(jnp.where(keep, held_e[f], 0.0), slot_stat[NS : NS + 12], f)
        kept_h += flux(jnp.where(keep, held_h[f], 0.0), slot_stat[NS : NS + 12], f)
    kept_e = dot(lmat[...], split3(jnp.concatenate(kept_e, axis=0)))
    kept_h = dot(lmat[...], split3(jnp.concatenate(kept_h, axis=0)))
    kept = jnp.concatenate([split2(kept_e), split2(kept_h)], axis=0)
    message = jnp.concatenate([dot(pack[...], kept)[:120], slot_stat[8:16]], axis=0)
    hand_out[1] = message.T.reshape(n_dom, cap, RK)
    handed_kept = exchange(hand_out.at[1], hand_in.at[1], hand_send.at[1], hand_recv.at[1])

    around_up = [dot_t(export_up, fine_own[:, f * fine : (f + 1) * fine]) for f in range(4)]
    around_down = [dot_t(export_down, fine_own[:, f * fine : (f + 1) * fine]) for f in range(4)]
    around = jnp.concatenate(
        [*around_up, export_up.astype(f32), *around_down, export_down.astype(f32)], axis=0
    ).astype(bf16)
    export_at = export_hot.astype(f32).T.astype(bf16)
    pad_eye = one_hot(2 * width, lax.broadcasted_iota(jnp.int32, (1, fine), 1))
    for copy in sent_codes:
        copy.wait()
    came_codes = dot(split2(code_in[...].reshape(2 * width, 128).T), pad_eye)
    came_codes = (came_codes[:128] + came_codes[128:])[4:8].astype(jnp.int32)
    ext = lax.broadcasted_iota(jnp.int32, (1, fine), 1)
    below = ext < width
    real = ext < 2 * width
    low_end = 4 * fine + 4 * width
    reach = 5 * width
    codes_all = []
    for f in range(4):
        code = codes[f]
        low, high = (code - 4 * fine) >> 2, (code - low_end) >> 2
        at = jnp.where(code < low_end, 4 * width + low, reach + 4 * width + high)
        at = jnp.where((code < 4 * fine) | (code >= frozen_code), -1, at)
        code_x = came_codes[f : f + 1]
        low, high = (code_x - 4 * fine) >> 2, (code_x - low_end) >> 2
        is_near = code_x < 4 * fine
        is_low = (code_x >= 4 * fine) & (code_x < low_end)
        is_high = (code_x >= low_end) & (code_x < frozen_code)
        at_x = jnp.where(below, f * width + ext, reach + f * width + ext - width)
        at_x = jnp.where(is_near, at_x, -1)
        at_x = jnp.where(is_low & below, 2 * reach + low, at_x)
        at_x = jnp.where(is_high & (ext >= width), 2 * reach + width + high, at_x)
        at_x = jnp.where(real, at_x, -1)
        mine = jnp.where(is_low & (ext >= width), low, jnp.where(is_high & below, width + high, -1))
        mine = jnp.where(real, mine, -1)
        block = slice(2 * f * fine, (2 * f + 1) * fine)
        block_x = slice((2 * f + 1) * fine, (2 * f + 2) * fine)
        tile_own[:, block] = fine_own[:, f * fine : (f + 1) * fine]
        tile_own[:, block_x] = dot(export_at, one_hot(2 * width, mine)).astype(bf16)
        tile_halo[:, block] = one_hot(12 * width, at)
        tile_halo[:, block_x] = one_hot(12 * width, at_x)
        codes_all.append(jnp.concatenate([code, code_x], axis=1))
    at = jnp.where(below, 4 * width + ext, reach + 4 * width + ext - width)
    ext_hot = one_hot(12 * width, jnp.where(real, at, -1))
    fine_halo[...] = one_hot(fine, code_row - fine)
    fine_out[...] = jnp.zeros(fine_out.shape, f32)
    first_out[...] = jnp.zeros(first_out.shape, f32)
    slot_hot = one_hot(slots, my_slots)

    @pl.loop(0, count // CHUNK)
    def _(i):
        start = pl.multiple_of(i * CHUNK, CHUNK)
        for f in range(4):
            code = face_nbr[f : f + 1, pl.ds(start, CHUNK)]
            coarse_hot[f, :, pl.ds(start, CHUNK)] = one_hot(full, code >> 2)

    def take(message):
        got = dot(split2(message.reshape(slots, RK).T), slot_hot)
        state = dot(unpack[...], got.astype(bf16))
        return state[:FR], state[FR:], got[120:RK] + got[RK + 120 :]

    finish(handed_fields)
    efield, hfield, stat_a = take(hand_in[0])
    finish(extras)

    def add_extra(d, value):
        return value + dot(split2(extra_in[d]), slots_of(d, my_slots))

    stat_c = lax.fori_loop(0, n_dom, add_extra, jnp.zeros((16, fine), f32))
    stat_c = stat_c[:8] + stat_c[8:]
    finish(handed_kept)
    kept_e, kept_h, stat_b = take(hand_in[1])
    fine_stat = jnp.concatenate([stat_a, stat_b, stat_c], axis=0)

    def send_electric(parts, turn):
        tile = dot_t(around, parts[:FR]) + dot_t(around, parts[FR:])
        fine_out[turn, :, :FR] = tile
        copies = []
        plan = (
            (after_id, 0, reach, 0),
            (before_id, reach, reach, reach),
            (after2_id, 4 * width, width, 2 * reach),
            (before2_id, reach + 4 * width, width, 2 * reach + width),
        )
        for side, (target, first, size, at) in enumerate(plan):
            copy = pltpu.make_async_remote_copy(
                src_ref=fine_out.at[turn, first : first + size],
                dst_ref=fine_in.at[turn, at : at + size],
                send_sem=fine_send.at[turn, side],
                recv_sem=fine_recv.at[turn, side],
                device_id=target,
                device_id_type=MESH,
            )
            copy.start()
            copies.append(copy)
        return copies

    def fluxes_of(near, own, face_codes, ns, size):
        traces = dot(sel[...], near.astype(bf16))
        fluxes = []
        for f in range(4):
            at = f * 3 * FN
            outside = pick_face(traces[:, f * size : (f + 1) * size], face_codes[f] & 3)
            fluxes += flux(outside - own[at : at + 3 * FN], ns, f)
        return dot(lmat[...], split3(jnp.concatenate(fluxes, axis=0)))

    fine_step = coarse_step / SUBSTEPS
    fine_geo, fine_ns = fine_stat[GEO : GEO + 9], fine_stat[NS : NS + 12]
    for substep in range(SUBSTEPS):
        parts = split2(efield)
        copies = send_electric(parts, substep)
        if substep == 0:
            start = jnp.concatenate([hfield, kept_e, fine_stat], axis=0)
            hi, lo = split(start)
            tile = dot_t(export_hot, hi.astype(bf16)) + dot_t(export_hot, lo.astype(bf16))
            first_out[0, :, : tile.shape[1]] = tile[:width]
            first_out[1, :, : tile.shape[1]] = tile[width:]
            first_copies = to_neighbours(first_out, first_in, first_send, first_recv)
        near = dot(parts, tile_own[...])
        own = dot(sel[...], parts)
        spin = curl(dot(dmat[...], split3(efield)), fine_geo)
        if substep == 0:
            for copy in first_copies:
                copy.wait()
            came = dot(split2(first_in[...].reshape(2 * width, 256).T), pad_eye)
            came = came[:256] + came[256:]
            hfield = jnp.concatenate([hfield, came[:FR]], axis=1)
            kept_all = jnp.concatenate([kept_e, came[FR : 2 * FR]], axis=1)
            stat_x = came[2 * FR : 2 * FR + 24]
            geo_x = stat_x[GEO : GEO + 9]
            ns_all = jnp.concatenate([fine_stat, stat_x], axis=1)[NS : NS + 12]
        for copy in copies:
            copy.wait()
        halo = split2(fine_in[substep].T[:FR])
        near = near + dot(halo, tile_halo[...])
        parts_x = dot(halo, ext_hot)
        field_x = parts_x[:FR] + parts_x[FR:]
        own = jnp.concatenate([own, dot(sel[...], parts_x.astype(bf16))], axis=1)
        spin_x = curl(dot(dmat[...], split3(field_x)), geo_x)
        spin = jnp.concatenate([spin, spin_x], axis=1) + kept_all
        rate = spin + fluxes_of(near, own, codes_all, ns_all, 2 * fine)
        hfield = hfield - fine_step * rate

        field = hfield[:, :fine]
        parts = split2(field)
        near = dot(parts, fine_own[...]) + dot(split2(hfield[:, fine:]), fine_halo[...])
        own = dot(sel[...], parts)
        spin = curl(dot(dmat[...], split3(field)), fine_geo) + kept_h
        efield = efield + fine_step * (spin + fluxes_of(near, own, codes, fine_ns, fine))
    hfield = hfield[:, :fine]

    result = jnp.concatenate([split2(efield), split2(hfield)], axis=0)
    result = split2(dot(pack[...], result))
    result = dot_t(slot_hot, result)
    result = result[:, :RK] + result[:, RK:]
    back_out[...] = result.reshape(n_dom, cap, RK)
    returned = exchange(back_out, back_in, back_send, back_recv)
    is_fine = dot_t(jnp.ones((16, slots), bf16), send_hot[...])[:1] > 0.5
    finish(returned)
    came = back_in[...].reshape(slots, RK).T
    came = dot_t(split2(came), send_hot[...]).astype(bf16)
    came = dot(unpack[...], came)
    merged_e = jnp.where(is_fine, came[:FR], own_e[...])
    merged_h = jnp.where(is_fine, came[FR:], own_h[...])
    own_e[...] = merged_e
    own_h[...] = merged_h
    pool_e, pool_h = pool.at[:128], pool.at[128:256]

    def narrowed(x):
        return dot(narrow[...], split2(x)).astype(bf16)

    pool_e[:, :count] = narrowed(merged_e)

    halo_lane = lax.broadcasted_iota(jnp.int32, (FR, 128), 1)
    place = lax.broadcasted_iota(jnp.int32, (1, CHUNK), 1)

    def coarse_rate(start, source, pool, reach, mirror):
        window = pl.ds(start, CHUNK)
        field = source[:, window]
        table = stat[:, window]
        spin = curl(dot(dmat[...], split3(field)), table[GEO : GEO + 9])
        own = dot(sel[...], split2(field))
        ns = table[NS : NS + 12]
        fluxes = []
        for f in range(4):
            code = face_nbr[f : f + 1, window]
            near = dot(pool[:, :reach], coarse_hot[f, :reach, window]).astype(bf16)
            outside = pick_face(dot(sel_narrow[...], near), code & 3)
            mine = own[f * 3 * FN : (f + 1) * 3 * FN]
            wall = code == 4 * (start + place) + f
            outside = jnp.where(wall, mirror * mine, outside)
            fluxes += flux(outside - mine, ns, f)
        return spin + dot(lmat[...], split3(jnp.concatenate(fluxes, axis=0)))

    def set_halo(pool, turn, copies):
        for copy in copies:
            copy.wait()
        tile = jnp.where(halo_lane < 64, halo_in[turn, 1], halo_in[turn, 0])
        pool[:, count:] = narrowed(pltpu.roll(tile, 64, 1))

    def update(start, source, pool, target, first, scale, reach, mirror):
        window = pl.ds(start, CHUNK)
        new = target[:, window] + scale * coarse_rate(start, source, pool, reach, mirror)
        target[:, window] = new
        for c in range(3):
            out[first + c, :, window] = new[c * PADC : c * PADC + 20]
        if first == 3:
            pool_h[:, window] = narrowed(new)

    last = count - CHUNK
    set_halo(pool_e, 0, halo_e)

    for start in (0, last):
        update(start, own_e, pool_e, own_h, 3, -coarse_step, full, -1.0)

    halo_out[1, 0] = own_h[:, count - 128 :]
    halo_out[1, 1] = own_h[:, :128]
    halo_h = to_neighbours(halo_out.at[1], halo_in.at[1], halo_send.at[1], halo_recv.at[1])

    for start in range(CHUNK, last, CHUNK):
        update(start, own_e, pool_e, own_h, 3, -coarse_step, count, -1.0)
    for start in range(CHUNK, last, CHUNK):
        update(start, own_h, pool_h, own_e, 0, coarse_step, count, 1.0)

    set_halo(pool_h, 1, halo_h)

    for start in (0, last):
        update(start, own_h, pool_h, own_e, 0, coarse_step, full, 1.0)


def per_device(
    n_dom,
    n_sub,
    fields,
    geometry,
    normals,
    face_scale,
    derivatives,
    lift_matrix,
    face_nbr,
    send_rows,
    fine_slots,
    export_rows,
    fine_nbr,
):
    count = fields.shape[2]
    fine = fine_slots.shape[0]
    width = export_rows.shape[1]
    group = send_rows.shape[0] // n_dom
    cap = -(-group // 8) * 8
    slots = n_dom * cap
    if cap != group:
        send_rows = jnp.pad(
            send_rows.reshape(n_dom, group),
            ((0, 0), (0, cap - group)),
            constant_values=count,
        ).reshape(-1)
        fine_slots = fine_slots // group * cap + fine_slots % group
    operands = [
        fields,
        geometry,
        normals,
        face_scale,
        derivatives,
        lift_matrix,
        face_nbr,
        send_rows[None],
        fine_slots[None],
        export_rows,
        fine_nbr,
        *[jnp.asarray(x) for x in tables()],
    ]
    vmem = pl.BlockSpec(memory_space=pltpu.VMEM)
    dma = pltpu.SemaphoreType.DMA
    return pl.pallas_call(
        functools.partial(kernel, n_dom, n_sub, width),
        out_shape=pltpu.VMEM(fields.shape, f32),
        in_specs=[pl.BlockSpec(memory_space=pl.ANY)] * len(operands),
        out_specs=vmem,
        scratch_shapes=[
            *[pltpu.VMEM(x.shape, x.dtype) for x in operands],
            dma((len(operands),)),
            pltpu.VMEM((FR, count), f32),
            pltpu.VMEM((FR, count), f32),
            pltpu.VMEM((4 * FR + 64, count + 128), bf16),
            pltpu.VMEM((32, count), f32),
            pltpu.VMEM((16, fine), f32),
            pltpu.VMEM((TR, 2 * FR), bf16),
            pltpu.VMEM((RK, 4 * FR), bf16),
            pltpu.VMEM((128, 2 * FR), bf16),
            pltpu.VMEM((TR, 128), bf16),
            pltpu.VMEM((count, slots), bf16),
            pltpu.VMEM((4, count + 128, count), bf16),
            pltpu.VMEM((fine, 4 * fine), bf16),
            pltpu.VMEM((fine, 4 * fine), bf16),
            pltpu.VMEM((fine, 8 * fine), bf16),
            pltpu.VMEM((12 * width, 8 * fine), bf16),
            pltpu.VMEM((224, 3 * FR), bf16),
            pltpu.VMEM((FR, 3 * TR), bf16),
            pltpu.VMEM((n_dom, 8, 128), f32),
            pltpu.VMEM((n_dom, 8, 128), f32),
            pltpu.VMEM((n_dom, 8, 128), f32),
            pltpu.VMEM((n_dom, 8, 128), f32),
            pltpu.VMEM((2, n_dom, cap, RK), f32),
            pltpu.VMEM((2, n_dom, cap, RK), f32),
            pltpu.VMEM((n_dom, cap, RK), f32),
            pltpu.VMEM((n_dom, cap, RK), f32),
            pltpu.VMEM((2, width, 128), f32),
            pltpu.VMEM((2, width, 128), f32),
            pltpu.VMEM((2, width, 256), f32),
            pltpu.VMEM((2, width, 256), f32),
            pltpu.VMEM((SUBSTEPS, 10 * width, 128), f32),
            pltpu.VMEM((SUBSTEPS, 12 * width, 128), f32),
            pltpu.VMEM((2, 2, FR, 128), f32),
            pltpu.VMEM((2, 2, FR, 128), f32),
            dma((n_dom,)),
            dma((n_dom,)),
            dma((n_dom,)),
            dma((n_dom,)),
            dma((2, n_dom)),
            dma((2, n_dom)),
            dma((n_dom,)),
            dma((n_dom,)),
            dma((2,)),
            dma((2,)),
            dma((2,)),
            dma((2,)),
            dma((SUBSTEPS, 4)),
            dma((SUBSTEPS, 4)),
            dma((2, 2)),
            dma((2, 2)),
        ],
        compiler_params=pltpu.CompilerParams(
            collective_id=0, has_side_effects=True, vmem_limit_bytes=56 * 1024 * 1024
        ),
    )(*operands)


def solution(mesh):
    return jax.shard_map(
        functools.partial(per_device, mesh.shape["dom"], mesh.shape["sub"]),
        mesh=mesh,
        in_specs=(
            P(None, None, ("dom", "sub")),
            P(None, ("dom", "sub")),
            P(None, None, ("dom", "sub")),
            P(None, ("dom", "sub")),
            P(),
            P(),
            P(None, ("dom", "sub")),
            P(("dom", "sub")),
            P(("dom", "sub")),
            P(None, ("dom", "sub")),
            P(None, ("dom", "sub")),
        ),
        out_specs=P(None, None, ("dom", "sub")),
        check_vma=False,
    )
```
